32 devices in a mesh: batch: 4 (over x, core), seq: 8 (over z, y).
Axes of the slice: x: 2, y: 2, z: 4, core: 2. Of those that a mesh axis runs over, the one named last changes fastest.
Arguments:
- tokens: bfloat16 [32, 2048, 768], P('batch', 'seq'), may hold values from -6 to 6
- segment_ids: int32 [32, 2048], P('batch', 'seq'), may hold values from -1 to 7, as said below
- query_weight: bfloat16 [768, 768], replicated, may hold values from -0.21875 to 0.21875
- query_bias: float32 [768], replicated, may hold values from -1.75 to 1.75
- keyval_weight: bfloat16 [768, 128], replicated, may hold values from -0.21875 to 0.21875
- keyval_bias: float32 [128], replicated, may hold values from -1.75 to 1.75
- out_weight: bfloat16 [768, 768], replicated, may hold values from -1.25 to 1.25
- out_bias: float32 [768], replicated, may hold values from -1.75 to 1.75
- up_weight: bfloat16 [768, 3072], replicated, may hold values from -0.21875 to 0.21875
- up_bias: float32 [3072], replicated, may hold values from -1.75 to 1.75
- down_weight: bfloat16 [3072, 768], replicated, may hold values from -0.109375 to 0.109375
- down_bias: float32 [768], replicated, may hold values from -1.75 to 1.75
- attention_gain: float32 [768], replicated, may hold values from 0.5 to 1.5
- attention_shift: float32 [768], replicated, may hold values from -1.75 to 1.75
- dense_gain: float32 [768], replicated, may hold values from 0.5 to 1.5
- dense_shift: float32 [768], replicated, may hold values from -1.75 to 1.75
- out_cotangent: bfloat16 [32, 2048, 768], P('batch', 'seq'), may hold values from -6 to 6
- keyval_cotangent: bfloat16 [32, 2048, 128], P('batch', 'seq'), may hold values from -1.75 to 1.75
Outputs:
- layer_out: bfloat16 [32, 2048, 768], P('batch', 'seq')
- keyval_out: bfloat16 [32, 2048, 128], P('batch', 'seq')
- grad_tokens: bfloat16 [32, 2048, 768], P('batch', 'seq')
- grad_query_weight: float32 [768, 768], P('seq')
- grad_query_bias: float32 [768], P('seq')
- grad_keyval_weight: float32 [768, 128], P('seq')
- grad_keyval_bias: float32 [128], P('seq')
- grad_out_weight: float32 [768, 768], P('seq')
- grad_out_bias: float32 [768], P('seq')
- grad_up_weight: float32 [768, 3072], P('seq')
- grad_up_bias: float32 [3072], P('seq')
- grad_down_weight: float32 [3072, 768], P('seq')
- grad_down_bias: float32 [768], P('seq')
- grad_attention_gain: float32 [768], P('seq')
- grad_attention_shift: float32 [768], P('seq')
- grad_dense_gain: float32 [768], P('seq')
- grad_dense_shift: float32 [768], P('seq')
The draws below stay inside these ranges and needn't reach their ends.
Inputs may be any that keep to these rules, and one draw needn't show every extreme that they name: `segment_ids`: within a row the ids of documents start at 0 and never fall, each step up by one, and every document has one position or more; in each group of 8 consecutive rows one row, drawn from the seed, is a single document 0 over all 2048 positions with no padding; each of the other 7 rows of the group holds eight documents with ids 0 to 7 followed by a nonempty tail of padding -1.
All inputs are finite; a program needn't handle non-finite values.
Results may differ from the reference program's by a relative error of at most 0.018.
Values may be sent and summed in bfloat16 or wider, within the bound.
A program may use at most 256 MiB of HBM per device.

```python
import jax
import jax.numpy as jnp
from jax import lax

D = 768
HEADS = 12
HEAD_DIM = 64
FF = 3072
ROT = 16
SEQ_LEN = 2048
ROWS = 8
ROWS_ALL = 32


doc_count = 8


def draw_segment_ids(key, part):
    key = jax.random.fold_in(key, 11)
    key_weights, key_padding, key_pick = jax.random.split(key, 3)
    roots = jax.random.randint(key_weights, (ROWS_ALL, doc_count), 1, 17, dtype=jnp.int32)
    shares = roots * roots * roots
    padding = jax.random.randint(key_padding, (ROWS_ALL, 1), 1, SEQ_LEN // 32 + 1, dtype=jnp.int32)
    live = SEQ_LEN - padding
    spare = live - doc_count
    share_total = jnp.sum(shares, axis=1, keepdims=True)
    lengths = 1 + shares * spare // share_total
    head_lengths = lengths[:, :doc_count - 1]
    last_length = live - jnp.sum(head_lengths, axis=1, keepdims=True)
    lengths = jnp.concatenate([head_lengths, last_length], axis=1).astype(jnp.int32)
    starts = (jnp.cumsum(lengths, axis=1) - lengths).astype(jnp.int32)
    column = jnp.arange(SEQ_LEN, dtype=jnp.int32)
    segment = jnp.sum((column[None, :, None] >= starts[:, None, :]).astype(jnp.int32), axis=2) - 1
    segment = jnp.where(column[None, :] >= live, -1, segment)
    groups = ROWS_ALL // ROWS
    chosen = jax.random.randint(key_pick, (groups,), 0, ROWS, dtype=jnp.int32)
    row_index = jnp.arange(ROWS_ALL, dtype=jnp.int32)
    single = row_index % ROWS == chosen[row_index // ROWS]
    return jnp.where(single[:, None], 0, segment).astype(jnp.int32)


def block_levels(own_key, shape, cuts, smallest, high):
    def one(position, shards_of):
        draws = jax.random.uniform(jax.random.fold_in(jax.random.fold_in(own_key, 6), position), (shards_of,), jnp.float32, smallest / len(cuts), high / len(cuts))
        return jnp.repeat(jnp.exp(draws), shape[position] // shards_of).reshape((-1,) + (1,) * (len(shape) - position - 1))

    factor_of = one(*cuts[0])
    for cut in cuts[1:]:
        factor_of = factor_of * one(*cut)
    return factor_of


def normal_values(stream_key, shape, width, most, cuts=(), kind=jnp.bfloat16):
    entries = jax.random.normal(stream_key, shape, jnp.float32) * width
    if len(cuts) > 0:
        entries = block_levels(stream_key, shape, cuts, -0.22, 0.18) * entries
    return jnp.clip(entries, min=-most, max=most).astype(kind)


def setup_inputs(seed: int = 0) -> dict:
    arg_keys = jax.random.split(jax.random.key(seed), 19)
    return {
        "tokens": normal_values(arg_keys[0], (ROWS_ALL, SEQ_LEN, D), 1.0, 6.0, ((0, 4), (1, 8))),
        "segment_ids": draw_segment_ids(jax.random.fold_in(arg_keys[18], 71), 0),
        "query_weight": normal_values(arg_keys[2], (D, D), D ** -0.5, 0.21875),
        "query_bias": normal_values(arg_keys[3], (D,), 0.3, 1.75, (), jnp.float32),
        "keyval_weight": normal_values(arg_keys[4], (D, 2 * HEAD_DIM), D ** -0.5, 0.21875),
        "keyval_bias": normal_values(arg_keys[5], (2 * HEAD_DIM,), 0.3, 1.75, (), jnp.float32),
        "out_weight": normal_values(arg_keys[6], (D, D), (D // 32) ** -0.5, 1.25),
        "out_bias": normal_values(arg_keys[7], (D,), 0.3, 1.75, (), jnp.float32),
        "up_weight": normal_values(arg_keys[8], (D, FF), D ** -0.5, 0.21875),
        "up_bias": normal_values(arg_keys[9], (FF,), 0.3, 1.75, (), jnp.float32),
        "down_weight": normal_values(arg_keys[10], (FF, D), FF ** -0.5, 0.109375),
        "down_bias": normal_values(arg_keys[11], (D,), 0.3, 1.75, (), jnp.float32),
        "attention_gain": jnp.clip(1.0 + 0.1 * jax.random.normal(arg_keys[12], (D,), jnp.float32), 0.5, 1.5),
        "attention_shift": normal_values(arg_keys[13], (D,), 0.3, 1.75, (), jnp.float32),
        "dense_gain": jnp.clip(1.0 + 0.1 * jax.random.normal(arg_keys[14], (D,), jnp.float32), 0.5, 1.5),
        "dense_shift": normal_values(arg_keys[15], (D,), 0.3, 1.75, (), jnp.float32),
        "out_cotangent": normal_values(arg_keys[16], (ROWS_ALL, SEQ_LEN, D), 1.0, 6.0, ((0, 4), (1, 8))),
        "keyval_cotangent": normal_values(arg_keys[17], (ROWS_ALL, SEQ_LEN, 2 * HEAD_DIM), 0.3, 1.75, ((0, 4), (1, 8))),
    }


@jax.custom_vjp
def low(v):
    return lax.optimization_barrier(v.astype(jnp.bfloat16)).astype(jnp.float32)

@jax.custom_vjp
def low_back(v):
    return v

def low_keep(v):
    return (low(v), None)

def low_pass(kept, grad):
    return (grad,)

def back_keep(v):
    return (v, None)

def back_low(kept, grad):
    return (low(grad),)
low.defvjp(low_keep, low_pass)
low_back.defvjp(back_keep, back_low)
epsilon = 1e-05
rope_base = 10000.0
negative = -1e+30
query_block = 512

def layer_norm(values, gain_vector, shift_vector):
    average = lax.optimization_barrier(jnp.mean(values, axis=-1, keepdims=True))
    centred = values - average
    variance = lax.optimization_barrier(jnp.mean(centred * centred, axis=-1, keepdims=True))
    return centred * lax.rsqrt(variance + epsilon) * gain_vector + shift_vector

def rotary_tables(positions):
    half_rot = ROT // 2
    frequency = rope_base ** (-(2.0 * jnp.arange(half_rot, dtype=jnp.float32)) / ROT)
    angles = positions.astype(jnp.float32)[:, None] * frequency[None, :]
    return (jnp.cos(angles), jnp.sin(angles))

def rotate(values, cos_table, sin_table):
    half_rot = ROT // 2
    first_half = values[..., :half_rot]
    second_half = values[..., half_rot:ROT]
    return jnp.concatenate([first_half * cos_table - second_half * sin_table, second_half * cos_table + first_half * sin_table, values[..., ROT:]], axis=-1)

def matmul(left_side, right_side):
    return jnp.dot(left_side, right_side, precision=lax.Precision.HIGHEST, preferred_element_type=jnp.float32)

def row_forward(params, tokens_row, segment_row):
    query_weight, query_bias, keyval_weight, keyval_bias, out_weight, out_bias, up_weight, up_bias, down_weight, down_bias, attention_gain, attention_shift, dense_gain, dense_shift = params
    length = tokens_row.shape[0]
    valid_rows = (segment_row >= 0).astype(jnp.float32)[:, None]
    normed = low(layer_norm(tokens_row, attention_gain, attention_shift))
    query_pre = low_back(matmul(normed, query_weight) + query_bias)
    keyval_pre = low_back(matmul(normed, keyval_weight) + keyval_bias)
    positions = jnp.arange(length, dtype=jnp.int32)
    cos_table, sin_table = rotary_tables(positions)
    queries = low(rotate(query_pre.reshape(length, HEADS, HEAD_DIM), cos_table[:, None, :], sin_table[:, None, :]))
    keyval = low(jnp.concatenate([rotate(keyval_pre[:, :HEAD_DIM], cos_table, sin_table), keyval_pre[:, HEAD_DIM:]], axis=-1))
    key_rows = keyval[:, :HEAD_DIM]
    value_rows = keyval[:, HEAD_DIM:]
    block_rows = min(query_block, length)
    block_count = length // block_rows
    score_scale = HEAD_DIM ** (-0.5)

    def attend(pieces):
        query_blk, segment_blk, position_blk = pieces
        scores = jnp.einsum('qhd,kd->hqk', query_blk, key_rows, precision=lax.Precision.HIGHEST) * score_scale
        allowed = (position_blk[:, None] >= positions[None, :]) & (segment_blk[:, None] == segment_row[None, :])
        scores = low_back(jnp.where(allowed[None], scores, negative))
        weights = low(jax.nn.softmax(scores, axis=-1))
        return jnp.einsum('hqk,kd->qhd', weights, value_rows, precision=lax.Precision.HIGHEST)
    attended = lax.map(jax.checkpoint(attend), (queries.reshape(block_count, block_rows, HEADS, HEAD_DIM), segment_row.reshape(block_count, block_rows), positions.reshape(block_count, block_rows)))
    attended = low(low_back(attended.reshape(length, HEADS * HEAD_DIM)))
    attn_out = matmul(attended, out_weight) + out_bias
    dense_in = low(layer_norm(tokens_row, dense_gain, dense_shift))
    hidden = low_back(matmul(dense_in, up_weight) + up_bias)
    activated = low(jax.nn.gelu(hidden, approximate=False))
    dense_out = matmul(activated, down_weight) + down_bias
    return (tokens_row + valid_rows * (attn_out + dense_out), keyval)

def reference(tokens, segment_ids, query_weight, query_bias, keyval_weight, keyval_bias, out_weight, out_bias, up_weight, up_bias, down_weight, down_bias, attention_gain, attention_shift, dense_gain, dense_shift, out_cotangent, keyval_cotangent):
    params = tuple((member.astype(jnp.float32) for member in (query_weight, query_bias, keyval_weight, keyval_bias, out_weight, out_bias, up_weight, up_bias, down_weight, down_bias, attention_gain, attention_shift, dense_gain, dense_shift)))

    def forward(weights_all, inputs):

        def one_row(pieces):
            return row_forward(weights_all, pieces[0], pieces[1])
        return lax.map(jax.checkpoint(one_row), (inputs, segment_ids))
    (layer_out, keyval_out), pull_back = jax.vjp(forward, params, tokens.astype(jnp.float32))
    param_grads, grad_tokens = pull_back((out_cotangent.astype(jnp.float32), keyval_cotangent.astype(jnp.float32)))
    grad_query_weight, grad_query_bias, grad_keyval_weight, grad_keyval_bias, grad_out_weight, grad_out_bias, grad_up_weight, grad_up_bias, grad_down_weight, grad_down_bias, grad_attention_gain, grad_attention_shift, grad_dense_gain, grad_dense_shift = param_grads
    return (layer_out.astype(jnp.bfloat16), keyval_out.astype(jnp.bfloat16), grad_tokens.astype(jnp.bfloat16), grad_query_weight, grad_query_bias, grad_keyval_weight, grad_keyval_bias, grad_out_weight, grad_out_bias, grad_up_weight, grad_up_bias, grad_down_weight, grad_down_bias, grad_attention_gain, grad_attention_shift, grad_dense_gain, grad_dense_shift)
```

```python
from functools import partial

import jax
import jax.numpy as jnp
from jax import lax
from jax.experimental import pallas as pl
from jax.experimental.pallas import tpu as pltpu
from jax.sharding import PartitionSpec as P

HEADS = 12
HEAD_DIM = 64
ROT = 16
f32 = jnp.float32
bf16 = jnp.bfloat16


epsilon = 1e-05
rope_base = 10000.0
negative = -1e30


def layer_norm(values, gain_vector, shift_vector):
    average = jnp.mean(values, axis=-1, keepdims=True)
    centred = values - average
    variance = jnp.mean(centred * centred, axis=-1, keepdims=True)
    return centred * lax.rsqrt(variance + epsilon) * gain_vector + shift_vector


def rotary_tables(positions):
    half_rot = ROT // 2
    frequency = rope_base ** (-(2.0 * jnp.arange(half_rot, dtype=jnp.float32)) / ROT)
    angles = positions.astype(jnp.float32)[:, None] * frequency[None, :]
    return (jnp.cos(angles), jnp.sin(angles))


def rotate(values, cos_table, sin_table):
    half_rot = ROT // 2
    first_half = values[..., :half_rot]
    second_half = values[..., half_rot:ROT]
    return jnp.concatenate(
        [
            first_half * cos_table - second_half * sin_table,
            second_half * cos_table + first_half * sin_table,
            values[..., ROT:],
        ],
        axis=-1,
    )


def unrotate(values, cos_table, sin_table):
    half_rot = ROT // 2
    first_half = values[..., :half_rot]
    second_half = values[..., half_rot:ROT]
    return jnp.concatenate(
        [
            first_half * cos_table + second_half * sin_table,
            second_half * cos_table - first_half * sin_table,
            values[..., ROT:],
        ],
        axis=-1,
    )


def contract_rows(left_side, right_side):
    return lax.dot_general(
        left_side, right_side, (((0,), (0,)), ((), ())), preferred_element_type=jnp.float32
    )


def contract_cols(left_side, right_side):
    return lax.dot_general(
        left_side, right_side, (((1,), (1,)), ((), ())), preferred_element_type=jnp.float32
    )


LOG2E=1.4426950408889634
NEG=-1e30
def nn(a,b): return lax.dot_general(a,b,(((1,),(0,)),((),())),preferred_element_type=f32)
def nt(a,b): return lax.dot_general(a,b,(((1,),(1,)),((),())),preferred_element_type=f32)

def attn_kernel(first_ref, sidx_ref, q_ref, do_ref, kv_ref, start_ref, cos_ref, sin_ref,
                att_ref, gq_ref, dkv_ref,
                qz, dz, p_s, m_s, bias_s, o_s, mx, ls, dq_s, dc_s, inn_s, ds_s, ic_s, *, blk, nblk):
    r = pl.program_id(0)
    L = HEADS*blk
    e = sidx_ref[0]
    n = e - first_ref[r] + 1
    qz[0:HEAD_DIM,:] = q_ref[0]
    qz[HEAD_DIM:,:] = jnp.zeros((HEAD_DIM,L),bf16)
    dz[0:HEAD_DIM,:] = jnp.zeros((HEAD_DIM,L),bf16)
    mx[...] = jnp.full((1,L),NEG,f32)
    ls[...] = jnp.zeros((1,L),f32)
    o_s[...] = jnp.zeros((HEAD_DIM,L),f32)
    dq_s[...] = jnp.zeros((HEAD_DIM,L),f32)
    start = start_ref[0]
    qpos = e*blk + lax.broadcasted_iota(jnp.int32,(1,blk),1)
    krow = lax.broadcasted_iota(jnp.int32,(blk,blk),0)

    @pl.loop(0, nblk)
    def _(j):
        @pl.when((j < first_ref[r]) | (j > e))
        def _():
            dkv_ref[0,j] = jnp.zeros((blk,2*HEAD_DIM),bf16)

    @pl.loop(0, n)
    def _(jj):
        j = e - jj
        kvj = kv_ref[0, pl.ds(pl.multiple_of(j*blk,blk),blk), :]
        vt = kvj.T[HEAD_DIM:,:]
        kpos = j*blk + krow
        bias_s[...] = jnp.where((kpos>=start)&(kpos<=qpos), 0.0, NEG)
        def hsl(h): return slice(h*blk,(h+1)*blk)
        sv = {}; pv = {}; av = {}
        for h in range(HEADS+2):
            if h < HEADS:
                sv[h] = nn(kvj, qz[:,hsl(h)])
            if 0 <= h-2 < HEADS:
                g = h-2; hs = hsl(g)
                o_s[:,hs] = o_s[:,hs]*av.pop(g) + nn(vt,pv.pop(g))
            if 0 <= h-1 < HEADS:
                g = h-1; hs = hsl(g)
                s = sv.pop(g)*LOG2E + bias_s[...]
                mo = mx[:,hs]
                mn = jnp.maximum(mo, jnp.max(s,axis=0,keepdims=True))
                p = jnp.exp2(s-mn)
                a = jnp.exp2(mo-mn)
                ls[:,hs] = ls[:,hs]*a + jnp.sum(p,axis=0,keepdims=True)
                pb = p.astype(bf16)
                p_s[jj,:,hs] = pb
                m_s[jj,:,hs] = mn
                mx[:,hs] = mn
                pv[g]=pb; av[g]=a

    inv = 1.0/ls[...]
    o = o_s[...]*inv
    for h in range(HEADS):
        att_ref[0, h*HEAD_DIM:(h+1)*HEAD_DIM, :] = o[:, h*blk:(h+1)*blk].astype(bf16)
    do = do_ref[0].astype(f32)
    inn_s[...] = jnp.sum(o*do,axis=0,keepdims=True)
    ls[...] = inv

    @pl.loop(0, n)
    def _(jj):
        j = e - jj
        kvj = kv_ref[0, pl.ds(pl.multiple_of(j*blk,blk),blk), :]
        kt = kvj.T[:HEAD_DIM,:]
        def hsl(h): return slice(h*blk,(h+1)*blk)
        c = jnp.exp2(m_s[jj]-mx[...])*ls[...]
        dc_s[...] = (do_ref[0].astype(f32)*c).astype(bf16)
        dz[HEAD_DIM:,:] = dc_s[...]
        ic_s[...] = inn_s[...]*c
        dpv = {}; dsv = {}
        for h in range(HEADS+2):
            if h < HEADS:
                dpv[h] = nn(kvj, dz[:,hsl(h)])
            if 0 <= h-2 < HEADS:
                g = h-2; hs = hsl(g)
                dq_s[:,hs] = dq_s[:,hs] + nn(kt, dsv.pop(g))
            if 0 <= h-1 < HEADS:
                g = h-1; hs = hsl(g)
                pb = p_s[jj,:,hs]
                ds = (pb.astype(f32)*(dpv.pop(g)-ic_s[:,hs])).astype(bf16)
                ds_s[:,hs] = ds
                dsv[g] = ds
        dv = nt(p_s[jj], dc_s[...])
        dk = nt(ds_s[...], qz[0:HEAD_DIM,:])
        dkv_ref[0,j] = jnp.concatenate([dk,dv],axis=1).astype(bf16)

    cos = cos_ref[...]; sin = sin_ref[...]
    for h in range(HEADS):
        g = dq_s[:, h*blk:(h+1)*blk]*(HEAD_DIM**-0.5)
        a, b = g[0:8], g[8:16]
        gq_ref[0, h*HEAD_DIM:(h+1)*HEAD_DIM, :] = jnp.concatenate([a*cos+b*sin, b*cos-a*sin, g[16:]],axis=0).astype(bf16)

def attention(first, sidx, qT, doT, kv, start, cosT, sinT):
    rows, _, L = qT.shape
    blk = L//HEADS
    length = kv.shape[1]; nblk = length//blk
    gs = pltpu.PrefetchScalarGridSpec(
        num_scalar_prefetch=2, grid=(rows,),
        in_specs=[
            pl.BlockSpec((1,HEAD_DIM,L),lambda r,*_:(r,0,0)),
            pl.BlockSpec((1,HEAD_DIM,L),lambda r,*_:(r,0,0)),
            pl.BlockSpec((1,length,2*HEAD_DIM),lambda r,*_:(r,0,0)),
            pl.BlockSpec((1,1,blk),lambda r,*_:(r,0,0)),
            pl.BlockSpec((8,blk),lambda r,*_:(0,0)),
            pl.BlockSpec((8,blk),lambda r,*_:(0,0)),
        ],
        out_specs=[
            pl.BlockSpec((1,HEADS*HEAD_DIM,blk),lambda r,*_:(r,0,0)),
            pl.BlockSpec((1,HEADS*HEAD_DIM,blk),lambda r,*_:(r,0,0)),
            pl.BlockSpec((1,nblk,blk,2*HEAD_DIM),lambda r,*_:(r,0,0,0)),
        ],
        scratch_shapes=[
            pltpu.VMEM((2*HEAD_DIM,L),bf16), pltpu.VMEM((2*HEAD_DIM,L),bf16),
            pltpu.VMEM((nblk,blk,L),bf16), pltpu.VMEM((nblk,1,L),f32),
            pltpu.VMEM((blk,blk),f32), pltpu.VMEM((HEAD_DIM,L),f32),
            pltpu.VMEM((1,L),f32), pltpu.VMEM((1,L),f32),
            pltpu.VMEM((HEAD_DIM,L),f32), pltpu.VMEM((HEAD_DIM,L),bf16), pltpu.VMEM((1,L),f32), pltpu.VMEM((blk,L),bf16), pltpu.VMEM((1,L),f32),
        ])
    return pl.pallas_call(
        partial(attn_kernel, blk=blk, nblk=nblk),
        out_shape=[jax.ShapeDtypeStruct((rows,HEADS*HEAD_DIM,blk),bf16),
                   jax.ShapeDtypeStruct((rows,HEADS*HEAD_DIM,blk),bf16),
                   jax.ShapeDtypeStruct((rows,nblk,blk,2*HEAD_DIM),bf16)],
        grid_spec=gs,
        compiler_params=pltpu.CompilerParams(vmem_limit_bytes=56*2**20),
        name="attention",
    )(first, sidx, qT, doT, kv, start, cosT, sinT)


def local_plain(
    tokens,
    segment_ids,
    query_weight,
    query_bias,
    keyval_weight,
    keyval_bias,
    out_weight,
    out_bias,
    up_weight,
    up_bias,
    down_weight,
    down_bias,
    attention_gain,
    attention_shift,
    dense_gain,
    dense_shift,
    out_cotangent,
    keyval_cotangent,
):
    rows, local_len, width = tokens.shape
    full_len = local_len * lax.axis_size("seq")
    tok_count = rows * local_len
    offset = lax.axis_index("seq") * local_len
    positions = offset + jnp.arange(local_len, dtype=jnp.int32)
    key_positions = jnp.arange(full_len, dtype=jnp.int32)
    score_scale = HEAD_DIM ** (-0.5)
    inputs = tokens.astype(jnp.float32).reshape(tok_count, width)
    valid_rows = (segment_ids >= 0).astype(jnp.float32).reshape(tok_count, 1)
    normed_full, attention_pull = jax.vjp(layer_norm, inputs, attention_gain, attention_shift)
    normed = normed_full.astype(jnp.bfloat16)
    query_pre = jnp.dot(normed, query_weight, preferred_element_type=jnp.float32) + query_bias
    keyval_pre = jnp.dot(normed, keyval_weight, preferred_element_type=jnp.float32) + keyval_bias
    cos_table, sin_table = rotary_tables(positions)
    queries = rotate(
        query_pre.reshape(rows, local_len, HEADS, HEAD_DIM),
        cos_table[:, None, :],
        sin_table[:, None, :],
    ).astype(jnp.bfloat16)
    queries = queries.transpose(0, 2, 1, 3).reshape(rows, HEADS * local_len, HEAD_DIM)
    key_part = keyval_pre[:, :HEAD_DIM].reshape(rows, local_len, HEAD_DIM)
    value_part = keyval_pre[:, HEAD_DIM:].reshape(rows, local_len, HEAD_DIM)
    keyval_local = jnp.concatenate(
        [rotate(key_part, cos_table, sin_table), value_part], axis=-1
    ).astype(jnp.bfloat16)
    keyval_all, segment_all = (
        lax.all_gather(keyval_local, "seq", axis=1, tiled=True),
        lax.all_gather(segment_ids, "seq", axis=1, tiled=True),
    )

    def scores_of(query_rows, key_rows, segment_row, segment_keys):
        scores = contract_cols(query_rows, key_rows) * score_scale
        allowed = (positions[:, None] >= key_positions[None, :]) & (
            segment_row[:, None] == segment_keys[None, :]
        )
        scores = scores.reshape(HEADS, local_len, full_len)
        return jnp.where(allowed[None], scores, negative)

    def forward_row(pieces):
        query_rows, keyval_row, segment_row, segment_keys = pieces
        scores = scores_of(query_rows, keyval_row[:, :HEAD_DIM], segment_row, segment_keys)
        top_score = jnp.max(scores, axis=-1, keepdims=True)
        expanded = jnp.exp(scores - top_score)
        row_total = jnp.sum(expanded, axis=-1, keepdims=True)
        weights = (expanded / row_total).reshape(HEADS * local_len, full_len).astype(jnp.bfloat16)
        attended_row = jnp.dot(
            weights, keyval_row[:, HEAD_DIM:], preferred_element_type=jnp.float32
        ).astype(jnp.bfloat16)
        log_total = (top_score + jnp.log(row_total)).reshape(HEADS * local_len)
        return (attended_row, log_total)

    attended, log_totals = lax.map(forward_row, (queries, keyval_all, segment_ids, segment_all))
    attended_flat = (
        attended.reshape(rows, HEADS, local_len, HEAD_DIM)
        .transpose(0, 2, 1, 3)
        .reshape(tok_count, width)
    )
    attn_out = jnp.dot(attended_flat, out_weight, preferred_element_type=jnp.float32) + out_bias
    dense_full, dense_pull = jax.vjp(layer_norm, inputs, dense_gain, dense_shift)
    dense_in = dense_full.astype(jnp.bfloat16)
    hidden = jnp.dot(dense_in, up_weight, preferred_element_type=jnp.float32) + up_bias
    activated_full, gelu_pull = jax.vjp(partial(jax.nn.gelu, approximate=False), hidden)
    activated = activated_full.astype(jnp.bfloat16)
    dense_out = jnp.dot(activated, down_weight, preferred_element_type=jnp.float32) + down_bias
    layer_out = (
        (inputs + valid_rows * (attn_out + dense_out))
        .astype(jnp.bfloat16)
        .reshape(rows, local_len, width)
    )
    upstream = out_cotangent.astype(jnp.float32).reshape(tok_count, width)
    branch_full = valid_rows * upstream
    branch_grad = branch_full.astype(jnp.bfloat16)
    branch_sum = jnp.sum(branch_full, axis=0)
    grad_out_weight = contract_rows(attended_flat, branch_grad)
    grad_down_weight = contract_rows(activated, branch_grad)
    (grad_hidden_full,) = gelu_pull(contract_cols(branch_grad, down_weight))
    grad_hidden = grad_hidden_full.astype(jnp.bfloat16)
    grad_up_weight = contract_rows(dense_in, grad_hidden)
    grad_up_bias = jnp.sum(grad_hidden.astype(jnp.float32), axis=0)
    grad_dense_in = contract_cols(grad_hidden, up_weight)
    dense_back, grad_dense_gain, grad_dense_shift = dense_pull(grad_dense_in)
    grad_attended = contract_cols(branch_grad, out_weight).astype(jnp.bfloat16)
    grad_attended = (
        grad_attended.reshape(rows, local_len, HEADS, HEAD_DIM)
        .transpose(0, 2, 1, 3)
        .reshape(rows, HEADS * local_len, HEAD_DIM)
    )
    keyval_back, segment_back = (
        lax.all_gather(keyval_local, "seq", axis=1, tiled=True),
        lax.all_gather(segment_ids, "seq", axis=1, tiled=True),
    )

    def backward_row(pieces):
        query_rows, keyval_row, segment_row, segment_keys, log_row, grad_rows = pieces
        key_rows = keyval_row[:, :HEAD_DIM]
        value_rows = keyval_row[:, HEAD_DIM:]
        scores = scores_of(query_rows, key_rows, segment_row, segment_keys)
        probs = jnp.exp(scores - log_row.reshape(HEADS, local_len, 1)).reshape(
            HEADS * local_len, full_len
        )
        grad_probs = contract_cols(grad_rows, value_rows)
        inner = jnp.sum(probs * grad_probs, axis=-1, keepdims=True)
        grad_scores = (probs * (grad_probs - inner)).astype(jnp.bfloat16)
        grad_query_rows = (
            jnp.dot(grad_scores, key_rows, preferred_element_type=jnp.float32) * score_scale
        )
        grad_key_rows = contract_rows(grad_scores, query_rows) * score_scale
        grad_value_rows = contract_rows(probs.astype(jnp.bfloat16), grad_rows)
        return (grad_query_rows, jnp.concatenate([grad_key_rows, grad_value_rows], axis=-1))

    grad_queries, keyval_terms = lax.map(
        backward_row, (queries, keyval_back, segment_ids, segment_back, log_totals, grad_attended)
    )
    keyval_grad = lax.psum_scatter(
        keyval_terms.astype(jnp.bfloat16), "seq", scatter_dimension=1, tiled=True
    ).astype(jnp.float32) + keyval_cotangent.astype(jnp.float32)
    grad_key_pre = unrotate(keyval_grad[..., :HEAD_DIM], cos_table, sin_table)
    grad_keyval_pre = (
        jnp.concatenate([grad_key_pre, keyval_grad[..., HEAD_DIM:]], axis=-1)
        .reshape(tok_count, 2 * HEAD_DIM)
        .astype(jnp.bfloat16)
    )
    grad_queries = grad_queries.reshape(rows, HEADS, local_len, HEAD_DIM).transpose(0, 2, 1, 3)
    grad_query_pre = (
        unrotate(grad_queries, cos_table[:, None, :], sin_table[:, None, :])
        .reshape(tok_count, width)
        .astype(jnp.bfloat16)
    )
    grad_query_weight = contract_rows(normed, grad_query_pre)
    grad_query_bias = jnp.sum(grad_query_pre.astype(jnp.float32), axis=0)
    grad_keyval_weight = contract_rows(normed, grad_keyval_pre)
    grad_keyval_bias = jnp.sum(grad_keyval_pre.astype(jnp.float32), axis=0)
    grad_normed = contract_cols(grad_query_pre, query_weight) + contract_cols(
        grad_keyval_pre, keyval_weight
    )
    attention_back, grad_attention_gain, grad_attention_shift = attention_pull(grad_normed)
    grad_tokens = (
        (upstream + attention_back + dense_back)
        .astype(jnp.bfloat16)
        .reshape(rows, local_len, width)
    )
    local_grads = (
        grad_query_weight,
        grad_query_bias,
        grad_keyval_weight,
        grad_keyval_bias,
        grad_out_weight,
        branch_sum,
        grad_up_weight,
        grad_up_bias,
        grad_down_weight,
        branch_sum,
        grad_attention_gain,
        grad_attention_shift,
        grad_dense_gain,
        grad_dense_shift,
    )
    shares = (
        lax.psum_scatter(
            local_grads[0].astype(jnp.bfloat16), "seq", scatter_dimension=0, tiled=True
        ).astype(jnp.float32),
        lax.psum_scatter(
            local_grads[1].astype(jnp.bfloat16), "seq", scatter_dimension=0, tiled=True
        ).astype(jnp.float32),
        lax.psum_scatter(
            local_grads[2].astype(jnp.bfloat16), "seq", scatter_dimension=0, tiled=True
        ).astype(jnp.float32),
        lax.psum_scatter(
            local_grads[3].astype(jnp.bfloat16), "seq", scatter_dimension=0, tiled=True
        ).astype(jnp.float32),
        lax.psum_scatter(
            local_grads[4].astype(jnp.bfloat16), "seq", scatter_dimension=0, tiled=True
        ).astype(jnp.float32),
        lax.psum_scatter(
            local_grads[5].astype(jnp.bfloat16), "seq", scatter_dimension=0, tiled=True
        ).astype(jnp.float32),
        lax.psum_scatter(
            local_grads[6].astype(jnp.bfloat16), "seq", scatter_dimension=0, tiled=True
        ).astype(jnp.float32),
        lax.psum_scatter(
            local_grads[7].astype(jnp.bfloat16), "seq", scatter_dimension=0, tiled=True
        ).astype(jnp.float32),
        lax.psum_scatter(
            local_grads[8].astype(jnp.bfloat16), "seq", scatter_dimension=0, tiled=True
        ).astype(jnp.float32),
        lax.psum_scatter(
            local_grads[9].astype(jnp.bfloat16), "seq", scatter_dimension=0, tiled=True
        ).astype(jnp.float32),
        lax.psum_scatter(
            local_grads[10].astype(jnp.bfloat16), "seq", scatter_dimension=0, tiled=True
        ).astype(jnp.float32),
        lax.psum_scatter(
            local_grads[11].astype(jnp.bfloat16), "seq", scatter_dimension=0, tiled=True
        ).astype(jnp.float32),
        lax.psum_scatter(
            local_grads[12].astype(jnp.bfloat16), "seq", scatter_dimension=0, tiled=True
        ).astype(jnp.float32),
        lax.psum_scatter(
            local_grads[13].astype(jnp.bfloat16), "seq", scatter_dimension=0, tiled=True
        ).astype(jnp.float32),
    )
    totals = (
        lax.psum(shares[0].astype(jnp.bfloat16), "batch").astype(jnp.float32),
        lax.psum(shares[1].astype(jnp.bfloat16), "batch").astype(jnp.float32),
        lax.psum(shares[2].astype(jnp.bfloat16), "batch").astype(jnp.float32),
        lax.psum(shares[3].astype(jnp.bfloat16), "batch").astype(jnp.float32),
        lax.psum(shares[4].astype(jnp.bfloat16), "batch").astype(jnp.float32),
        lax.psum(shares[5].astype(jnp.bfloat16), "batch").astype(jnp.float32),
        lax.psum(shares[6].astype(jnp.bfloat16), "batch").astype(jnp.float32),
        lax.psum(shares[7].astype(jnp.bfloat16), "batch").astype(jnp.float32),
        lax.psum(shares[8].astype(jnp.bfloat16), "batch").astype(jnp.float32),
        lax.psum(shares[9].astype(jnp.bfloat16), "batch").astype(jnp.float32),
        lax.psum(shares[10].astype(jnp.bfloat16), "batch").astype(jnp.float32),
        lax.psum(shares[11].astype(jnp.bfloat16), "batch").astype(jnp.float32),
        lax.psum(shares[12].astype(jnp.bfloat16), "batch").astype(jnp.float32),
        lax.psum(shares[13].astype(jnp.bfloat16), "batch").astype(jnp.float32),
    )
    return (
        layer_out,
        keyval_local,
        grad_tokens,
        totals[0],
        totals[1],
        totals[2],
        totals[3],
        totals[4],
        totals[5],
        totals[6],
        totals[7],
        totals[8],
        totals[9],
        totals[10],
        totals[11],
        totals[12],
        totals[13],
    )


def local(
    tokens,
    segment_ids,
    query_weight,
    query_bias,
    keyval_weight,
    keyval_bias,
    out_weight,
    out_bias,
    up_weight,
    up_bias,
    down_weight,
    down_bias,
    attention_gain,
    attention_shift,
    dense_gain,
    dense_shift,
    out_cotangent,
    keyval_cotangent,
):
    rows, local_len, width = tokens.shape
    full_len = local_len * lax.axis_size("seq")
    tok_count = rows * local_len
    offset = lax.axis_index("seq") * local_len
    positions = offset + jnp.arange(local_len, dtype=jnp.int32)
    score_scale = HEAD_DIM ** (-0.5)
    inputs = tokens.astype(jnp.float32).reshape(tok_count, width)
    valid_rows = (segment_ids >= 0).astype(jnp.float32).reshape(tok_count, 1)
    normed_full, attention_pull = jax.vjp(layer_norm, inputs, attention_gain, attention_shift)
    normed = normed_full.astype(jnp.bfloat16)
    query_pre = jnp.dot(normed, query_weight, preferred_element_type=jnp.float32) + query_bias
    keyval_pre = jnp.dot(normed, keyval_weight, preferred_element_type=jnp.float32) + keyval_bias
    cos_table, sin_table = rotary_tables(positions)
    queries = rotate(
        query_pre.reshape(rows, local_len, HEADS, HEAD_DIM),
        cos_table[:, None, :],
        sin_table[:, None, :],
    ).astype(jnp.bfloat16) * jnp.asarray(score_scale, jnp.bfloat16)
    queries = queries.transpose(0, 3, 2, 1).reshape(rows, HEAD_DIM, HEADS * local_len)
    key_part = keyval_pre[:, :HEAD_DIM].reshape(rows, local_len, HEAD_DIM)
    value_part = keyval_pre[:, HEAD_DIM:].reshape(rows, local_len, HEAD_DIM)
    keyval_local = jnp.concatenate(
        [rotate(key_part, cos_table, sin_table), value_part], axis=-1
    ).astype(jnp.bfloat16)
    keyval_all, segment_all = (
        lax.all_gather(keyval_local, "seq", axis=1, tiled=True),
        lax.all_gather(segment_ids, "seq", axis=1, tiled=True),
    )

    order_all = jnp.where(segment_all < 0, 1 << 20, segment_all)
    order_own = jnp.where(segment_ids < 0, 1 << 20, segment_ids)
    start = jnp.sum(
        (order_all[:, None, :] < order_own[:, :, None]).astype(jnp.int32), axis=-1
    ).astype(jnp.int32)
    first_block = start[:, 0] // local_len
    upstream = out_cotangent.astype(jnp.float32).reshape(tok_count, width)
    branch_full = valid_rows * upstream
    branch_grad = branch_full.astype(jnp.bfloat16)
    grad_attended = contract_cols(branch_grad, out_weight).astype(jnp.bfloat16)
    grad_attended = (
        grad_attended.reshape(rows, local_len, HEADS, HEAD_DIM)
        .transpose(0, 3, 2, 1)
        .reshape(rows, HEAD_DIM, HEADS * local_len)
    )
    attended, grad_query, keyval_terms = attention(
        first_block,
        lax.axis_index("seq").astype(jnp.int32)[None],
        queries,
        grad_attended,
        keyval_all,
        start[:, None, :],
        cos_table.T,
        sin_table.T,
    )
    attended_flat = attended.transpose(0, 2, 1).reshape(tok_count, width)
    grad_query_pre = grad_query.transpose(0, 2, 1).reshape(tok_count, width)
    attn_out = jnp.dot(attended_flat, out_weight, preferred_element_type=jnp.float32) + out_bias
    dense_full, dense_pull = jax.vjp(layer_norm, inputs, dense_gain, dense_shift)
    dense_in = dense_full.astype(jnp.bfloat16)
    hidden = jnp.dot(dense_in, up_weight, preferred_element_type=jnp.float32) + up_bias
    activated_full, gelu_pull = jax.vjp(partial(jax.nn.gelu, approximate=False), hidden)
    activated = activated_full.astype(jnp.bfloat16)
    dense_out = jnp.dot(activated, down_weight, preferred_element_type=jnp.float32) + down_bias
    layer_out = (
        (inputs + valid_rows * (attn_out + dense_out))
        .astype(jnp.bfloat16)
        .reshape(rows, local_len, width)
    )
    branch_sum = jnp.sum(branch_full, axis=0)
    grad_out_weight = contract_rows(attended_flat, branch_grad)
    grad_down_weight = contract_rows(activated, branch_grad)
    (grad_hidden_full,) = gelu_pull(contract_cols(branch_grad, down_weight))
    grad_hidden = grad_hidden_full.astype(jnp.bfloat16)
    grad_up_weight = contract_rows(dense_in, grad_hidden)
    grad_up_bias = jnp.sum(grad_hidden.astype(jnp.float32), axis=0)
    grad_dense_in = contract_cols(grad_hidden, up_weight)
    dense_back, grad_dense_gain, grad_dense_shift = dense_pull(grad_dense_in)
    keyval_grad = lax.psum_scatter(
        keyval_terms.reshape(rows, full_len, 2 * HEAD_DIM),
        "seq",
        scatter_dimension=1,
        tiled=True,
    ).astype(jnp.float32) + keyval_cotangent.astype(jnp.float32)
    grad_key_pre = unrotate(keyval_grad[..., :HEAD_DIM], cos_table, sin_table)
    grad_keyval_pre = (
        jnp.concatenate([grad_key_pre, keyval_grad[..., HEAD_DIM:]], axis=-1)
        .reshape(tok_count, 2 * HEAD_DIM)
        .astype(jnp.bfloat16)
    )
    grad_query_weight = contract_rows(normed, grad_query_pre)
    grad_query_bias = jnp.sum(grad_query_pre.astype(jnp.float32), axis=0)
    grad_keyval_weight = contract_rows(normed, grad_keyval_pre)
    grad_keyval_bias = jnp.sum(grad_keyval_pre.astype(jnp.float32), axis=0)
    grad_normed = contract_cols(grad_query_pre, query_weight) + contract_cols(
        grad_keyval_pre, keyval_weight
    )
    attention_back, grad_attention_gain, grad_attention_shift = attention_pull(grad_normed)
    grad_tokens = (
        (upstream + attention_back + dense_back)
        .astype(jnp.bfloat16)
        .reshape(rows, local_len, width)
    )
    local_grads = (
        grad_query_weight,
        grad_query_bias,
        grad_keyval_weight,
        grad_keyval_bias,
        grad_out_weight,
        branch_sum,
        grad_up_weight,
        grad_up_bias,
        grad_down_weight,
        branch_sum,
        grad_attention_gain,
        grad_attention_shift,
        grad_dense_gain,
        grad_dense_shift,
    )
    shares = (
        lax.psum_scatter(
            local_grads[0].astype(jnp.bfloat16), "seq", scatter_dimension=0, tiled=True
        ).astype(jnp.float32),
        lax.psum_scatter(
            local_grads[1].astype(jnp.bfloat16), "seq", scatter_dimension=0, tiled=True
        ).astype(jnp.float32),
        lax.psum_scatter(
            local_grads[2].astype(jnp.bfloat16), "seq", scatter_dimension=0, tiled=True
        ).astype(jnp.float32),
        lax.psum_scatter(
            local_grads[3].astype(jnp.bfloat16), "seq", scatter_dimension=0, tiled=True
        ).astype(jnp.float32),
        lax.psum_scatter(
            local_grads[4].astype(jnp.bfloat16), "seq", scatter_dimension=0, tiled=True
        ).astype(jnp.float32),
        lax.psum_scatter(
            local_grads[5].astype(jnp.bfloat16), "seq", scatter_dimension=0, tiled=True
        ).astype(jnp.float32),
        lax.psum_scatter(
            local_grads[6].astype(jnp.bfloat16), "seq", scatter_dimension=0, tiled=True
        ).astype(jnp.float32),
        lax.psum_scatter(
            local_grads[7].astype(jnp.bfloat16), "seq", scatter_dimension=0, tiled=True
        ).astype(jnp.float32),
        lax.psum_scatter(
            local_grads[8].astype(jnp.bfloat16), "seq", scatter_dimension=0, tiled=True
        ).astype(jnp.float32),
        lax.psum_scatter(
            local_grads[9].astype(jnp.bfloat16), "seq", scatter_dimension=0, tiled=True
        ).astype(jnp.float32),
        lax.psum_scatter(
            local_grads[10].astype(jnp.bfloat16), "seq", scatter_dimension=0, tiled=True
        ).astype(jnp.float32),
        lax.psum_scatter(
            local_grads[11].astype(jnp.bfloat16), "seq", scatter_dimension=0, tiled=True
        ).astype(jnp.float32),
        lax.psum_scatter(
            local_grads[12].astype(jnp.bfloat16), "seq", scatter_dimension=0, tiled=True
        ).astype(jnp.float32),
        lax.psum_scatter(
            local_grads[13].astype(jnp.bfloat16), "seq", scatter_dimension=0, tiled=True
        ).astype(jnp.float32),
    )
    totals = (
        lax.psum(shares[0].astype(jnp.bfloat16), "batch").astype(jnp.float32),
        lax.psum(shares[1].astype(jnp.bfloat16), "batch").astype(jnp.float32),
        lax.psum(shares[2].astype(jnp.bfloat16), "batch").astype(jnp.float32),
        lax.psum(shares[3].astype(jnp.bfloat16), "batch").astype(jnp.float32),
        lax.psum(shares[4].astype(jnp.bfloat16), "batch").astype(jnp.float32),
        lax.psum(shares[5].astype(jnp.bfloat16), "batch").astype(jnp.float32),
        lax.psum(shares[6].astype(jnp.bfloat16), "batch").astype(jnp.float32),
        lax.psum(shares[7].astype(jnp.bfloat16), "batch").astype(jnp.float32),
        lax.psum(shares[8].astype(jnp.bfloat16), "batch").astype(jnp.float32),
        lax.psum(shares[9].astype(jnp.bfloat16), "batch").astype(jnp.float32),
        lax.psum(shares[10].astype(jnp.bfloat16), "batch").astype(jnp.float32),
        lax.psum(shares[11].astype(jnp.bfloat16), "batch").astype(jnp.float32),
        lax.psum(shares[12].astype(jnp.bfloat16), "batch").astype(jnp.float32),
        lax.psum(shares[13].astype(jnp.bfloat16), "batch").astype(jnp.float32),
    )
    return (
        layer_out,
        keyval_local,
        grad_tokens,
        totals[0],
        totals[1],
        totals[2],
        totals[3],
        totals[4],
        totals[5],
        totals[6],
        totals[7],
        totals[8],
        totals[9],
        totals[10],
        totals[11],
        totals[12],
        totals[13],
    )


def choose(tokens, *rest):
    return (local if tokens.shape[1] % 128 == 0 else local_plain)(tokens, *rest)


def solution(mesh):
    placed = (
        P("batch", "seq", None),
        P("batch", "seq"),
        P(),
        P(),
        P(),
        P(),
        P(),
        P(),
        P(),
        P(),
        P(),
        P(),
        P(),
        P(),
        P(),
        P(),
        P("batch", "seq", None),
        P("batch", "seq", None),
    )
    return jax.shard_map(
        choose,
        mesh=mesh,
        in_specs=placed,
        out_specs=(
            P("batch", "seq", None),
            P("batch", "seq", None),
            P("batch", "seq", None),
            P("seq", None),
            P("seq"),
            P("seq", None),
            P("seq"),
            P("seq", None),
            P("seq"),
            P("seq", None),
            P("seq"),
            P("seq", None),
            P("seq"),
            P("seq"),
            P("seq"),
            P("seq"),
            P("seq"),
        ),
        check_vma=False,
    )
```

```python
from functools import partial

import jax
import jax.numpy as jnp
from jax import lax
from jax.experimental import pallas as pl
from jax.experimental.pallas import tpu as pltpu
from jax.sharding import PartitionSpec as P

HEADS = 12
HEAD_DIM = 64
ROT = 16
LOG2E = 1.4426950408889634
f32 = jnp.float32
bf16 = jnp.bfloat16


epsilon = 1e-05
rope_base = 10000.0
negative = -1e30


def layer_norm(values, gain_vector, shift_vector):
    average = jnp.mean(values, axis=-1, keepdims=True)
    centred = values - average
    variance = jnp.mean(centred * centred, axis=-1, keepdims=True)
    return centred * lax.rsqrt(variance + epsilon) * gain_vector + shift_vector


def rotary_tables(positions):
    half_rot = ROT // 2
    frequency = rope_base ** (-(2.0 * jnp.arange(half_rot, dtype=jnp.float32)) / ROT)
    angles = positions.astype(jnp.float32)[:, None] * frequency[None, :]
    return (jnp.cos(angles), jnp.sin(angles))


def rotate(values, cos_table, sin_table):
    half_rot = ROT // 2
    first_half = values[..., :half_rot]
    second_half = values[..., half_rot:ROT]
    return jnp.concatenate(
        [
            first_half * cos_table - second_half * sin_table,
            second_half * cos_table + first_half * sin_table,
            values[..., ROT:],
        ],
        axis=-1,
    )


def unrotate(values, cos_table, sin_table):
    half_rot = ROT // 2
    first_half = values[..., :half_rot]
    second_half = values[..., half_rot:ROT]
    return jnp.concatenate(
        [
            first_half * cos_table + second_half * sin_table,
            second_half * cos_table - first_half * sin_table,
            values[..., ROT:],
        ],
        axis=-1,
    )


def contract_rows(left_side, right_side):
    return lax.dot_general(
        left_side, right_side, (((0,), (0,)), ((), ())), preferred_element_type=jnp.float32
    )


def contract_cols(left_side, right_side):
    return lax.dot_general(
        left_side, right_side, (((1,), (1,)), ((), ())), preferred_element_type=jnp.float32
    )


def local_plain(
    tokens,
    segment_ids,
    query_weight,
    query_bias,
    keyval_weight,
    keyval_bias,
    out_weight,
    out_bias,
    up_weight,
    up_bias,
    down_weight,
    down_bias,
    attention_gain,
    attention_shift,
    dense_gain,
    dense_shift,
    out_cotangent,
    keyval_cotangent,
):
    rows, local_len, width = tokens.shape
    full_len = local_len * lax.axis_size("seq")
    tok_count = rows * local_len
    offset = lax.axis_index("seq") * local_len
    positions = offset + jnp.arange(local_len, dtype=jnp.int32)
    key_positions = jnp.arange(full_len, dtype=jnp.int32)
    score_scale = HEAD_DIM ** (-0.5)
    inputs = tokens.astype(jnp.float32).reshape(tok_count, width)
    valid_rows = (segment_ids >= 0).astype(jnp.float32).reshape(tok_count, 1)
    normed_full, attention_pull = jax.vjp(layer_norm, inputs, attention_gain, attention_shift)
    normed = normed_full.astype(jnp.bfloat16)
    query_pre = jnp.dot(normed, query_weight, preferred_element_type=jnp.float32) + query_bias
    keyval_pre = jnp.dot(normed, keyval_weight, preferred_element_type=jnp.float32) + keyval_bias
    cos_table, sin_table = rotary_tables(positions)
    queries = rotate(
        query_pre.reshape(rows, local_len, HEADS, HEAD_DIM),
        cos_table[:, None, :],
        sin_table[:, None, :],
    ).astype(jnp.bfloat16)
    queries = queries.transpose(0, 2, 1, 3).reshape(rows, HEADS * local_len, HEAD_DIM)
    key_part = keyval_pre[:, :HEAD_DIM].reshape(rows, local_len, HEAD_DIM)
    value_part = keyval_pre[:, HEAD_DIM:].reshape(rows, local_len, HEAD_DIM)
    keyval_local = jnp.concatenate(
        [rotate(key_part, cos_table, sin_table), value_part], axis=-1
    ).astype(jnp.bfloat16)
    keyval_all, segment_all = (
        lax.all_gather(keyval_local, "seq", axis=1, tiled=True),
        lax.all_gather(segment_ids, "seq", axis=1, tiled=True),
    )

    def scores_of(query_rows, key_rows, segment_row, segment_keys):
        scores = contract_cols(query_rows, key_rows) * score_scale
        allowed = (positions[:, None] >= key_positions[None, :]) & (
            segment_row[:, None] == segment_keys[None, :]
        )
        scores = scores.reshape(HEADS, local_len, full_len)
        return jnp.where(allowed[None], scores, negative)

    def forward_row(pieces):
        query_rows, keyval_row, segment_row, segment_keys = pieces
        scores = scores_of(query_rows, keyval_row[:, :HEAD_DIM], segment_row, segment_keys)
        top_score = jnp.max(scores, axis=-1, keepdims=True)
        expanded = jnp.exp(scores - top_score)
        row_total = jnp.sum(expanded, axis=-1, keepdims=True)
        weights = (expanded / row_total).reshape(HEADS * local_len, full_len).astype(jnp.bfloat16)
        attended_row = jnp.dot(
            weights, keyval_row[:, HEAD_DIM:], preferred_element_type=jnp.float32
        ).astype(jnp.bfloat16)
        log_total = (top_score + jnp.log(row_total)).reshape(HEADS * local_len)
        return (attended_row, log_total)

    attended, log_totals = lax.map(forward_row, (queries, keyval_all, segment_ids, segment_all))
    attended_flat = (
        attended.reshape(rows, HEADS, local_len, HEAD_DIM)
        .transpose(0, 2, 1, 3)
        .reshape(tok_count, width)
    )
    attn_out = jnp.dot(attended_flat, out_weight, preferred_element_type=jnp.float32) + out_bias
    dense_full, dense_pull = jax.vjp(layer_norm, inputs, dense_gain, dense_shift)
    dense_in = dense_full.astype(jnp.bfloat16)
    hidden = jnp.dot(dense_in, up_weight, preferred_element_type=jnp.float32) + up_bias
    activated_full, gelu_pull = jax.vjp(partial(jax.nn.gelu, approximate=False), hidden)
    activated = activated_full.astype(jnp.bfloat16)
    dense_out = jnp.dot(activated, down_weight, preferred_element_type=jnp.float32) + down_bias
    layer_out = (
        (inputs + valid_rows * (attn_out + dense_out))
        .astype(jnp.bfloat16)
        .reshape(rows, local_len, width)
    )
    upstream = out_cotangent.astype(jnp.float32).reshape(tok_count, width)
    branch_full = valid_rows * upstream
    branch_grad = branch_full.astype(jnp.bfloat16)
    branch_sum = jnp.sum(branch_full, axis=0)
    grad_out_weight = contract_rows(attended_flat, branch_grad)
    grad_down_weight = contract_rows(activated, branch_grad)
    (grad_hidden_full,) = gelu_pull(contract_cols(branch_grad, down_weight))
    grad_hidden = grad_hidden_full.astype(jnp.bfloat16)
    grad_up_weight = contract_rows(dense_in, grad_hidden)
    grad_up_bias = jnp.sum(grad_hidden.astype(jnp.float32), axis=0)
    grad_dense_in = contract_cols(grad_hidden, up_weight)
    dense_back, grad_dense_gain, grad_dense_shift = dense_pull(grad_dense_in)
    grad_attended = contract_cols(branch_grad, out_weight).astype(jnp.bfloat16)
    grad_attended = (
        grad_attended.reshape(rows, local_len, HEADS, HEAD_DIM)
        .transpose(0, 2, 1, 3)
        .reshape(rows, HEADS * local_len, HEAD_DIM)
    )
    keyval_back, segment_back = (
        lax.all_gather(keyval_local, "seq", axis=1, tiled=True),
        lax.all_gather(segment_ids, "seq", axis=1, tiled=True),
    )

    def backward_row(pieces):
        query_rows, keyval_row, segment_row, segment_keys, log_row, grad_rows = pieces
        key_rows = keyval_row[:, :HEAD_DIM]
        value_rows = keyval_row[:, HEAD_DIM:]
        scores = scores_of(query_rows, key_rows, segment_row, segment_keys)
        probs = jnp.exp(scores - log_row.reshape(HEADS, local_len, 1)).reshape(
            HEADS * local_len, full_len
        )
        grad_probs = contract_cols(grad_rows, value_rows)
        inner = jnp.sum(probs * grad_probs, axis=-1, keepdims=True)
        grad_scores = (probs * (grad_probs - inner)).astype(jnp.bfloat16)
        grad_query_rows = (
            jnp.dot(grad_scores, key_rows, preferred_element_type=jnp.float32) * score_scale
        )
        grad_key_rows = contract_rows(grad_scores, query_rows) * score_scale
        grad_value_rows = contract_rows(probs.astype(jnp.bfloat16), grad_rows)
        return (grad_query_rows, jnp.concatenate([grad_key_rows, grad_value_rows], axis=-1))

    grad_queries, keyval_terms = lax.map(
        backward_row, (queries, keyval_back, segment_ids, segment_back, log_totals, grad_attended)
    )
    keyval_grad = lax.psum_scatter(
        keyval_terms.astype(jnp.bfloat16), "seq", scatter_dimension=1, tiled=True
    ).astype(jnp.float32) + keyval_cotangent.astype(jnp.float32)
    grad_key_pre = unrotate(keyval_grad[..., :HEAD_DIM], cos_table, sin_table)
    grad_keyval_pre = (
        jnp.concatenate([grad_key_pre, keyval_grad[..., HEAD_DIM:]], axis=-1)
        .reshape(tok_count, 2 * HEAD_DIM)
        .astype(jnp.bfloat16)
    )
    grad_queries = grad_queries.reshape(rows, HEADS, local_len, HEAD_DIM).transpose(0, 2, 1, 3)
    grad_query_pre = (
        unrotate(grad_queries, cos_table[:, None, :], sin_table[:, None, :])
        .reshape(tok_count, width)
        .astype(jnp.bfloat16)
    )
    grad_query_weight = contract_rows(normed, grad_query_pre)
    grad_query_bias = jnp.sum(grad_query_pre.astype(jnp.float32), axis=0)
    grad_keyval_weight = contract_rows(normed, grad_keyval_pre)
    grad_keyval_bias = jnp.sum(grad_keyval_pre.astype(jnp.float32), axis=0)
    grad_normed = contract_cols(grad_query_pre, query_weight) + contract_cols(
        grad_keyval_pre, keyval_weight
    )
    attention_back, grad_attention_gain, grad_attention_shift = attention_pull(grad_normed)
    grad_tokens = (
        (upstream + attention_back + dense_back)
        .astype(jnp.bfloat16)
        .reshape(rows, local_len, width)
    )
    local_grads = (
        grad_query_weight,
        grad_query_bias,
        grad_keyval_weight,
        grad_keyval_bias,
        grad_out_weight,
        branch_sum,
        grad_up_weight,
        grad_up_bias,
        grad_down_weight,
        branch_sum,
        grad_attention_gain,
        grad_attention_shift,
        grad_dense_gain,
        grad_dense_shift,
    )
    shares = (
        lax.psum_scatter(
            local_grads[0].astype(jnp.bfloat16), "seq", scatter_dimension=0, tiled=True
        ).astype(jnp.float32),
        lax.psum_scatter(
            local_grads[1].astype(jnp.bfloat16), "seq", scatter_dimension=0, tiled=True
        ).astype(jnp.float32),
        lax.psum_scatter(
            local_grads[2].astype(jnp.bfloat16), "seq", scatter_dimension=0, tiled=True
        ).astype(jnp.float32),
        lax.psum_scatter(
            local_grads[3].astype(jnp.bfloat16), "seq", scatter_dimension=0, tiled=True
        ).astype(jnp.float32),
        lax.psum_scatter(
            local_grads[4].astype(jnp.bfloat16), "seq", scatter_dimension=0, tiled=True
        ).astype(jnp.float32),
        lax.psum_scatter(
            local_grads[5].astype(jnp.bfloat16), "seq", scatter_dimension=0, tiled=True
        ).astype(jnp.float32),
        lax.psum_scatter(
            local_grads[6].astype(jnp.bfloat16), "seq", scatter_dimension=0, tiled=True
        ).astype(jnp.float32),
        lax.psum_scatter(
            local_grads[7].astype(jnp.bfloat16), "seq", scatter_dimension=0, tiled=True
        ).astype(jnp.float32),
        lax.psum_scatter(
            local_grads[8].astype(jnp.bfloat16), "seq", scatter_dimension=0, tiled=True
        ).astype(jnp.float32),
        lax.psum_scatter(
            local_grads[9].astype(jnp.bfloat16), "seq", scatter_dimension=0, tiled=True
        ).astype(jnp.float32),
        lax.psum_scatter(
            local_grads[10].astype(jnp.bfloat16), "seq", scatter_dimension=0, tiled=True
        ).astype(jnp.float32),
        lax.psum_scatter(
            local_grads[11].astype(jnp.bfloat16), "seq", scatter_dimension=0, tiled=True
        ).astype(jnp.float32),
        lax.psum_scatter(
            local_grads[12].astype(jnp.bfloat16), "seq", scatter_dimension=0, tiled=True
        ).astype(jnp.float32),
        lax.psum_scatter(
            local_grads[13].astype(jnp.bfloat16), "seq", scatter_dimension=0, tiled=True
        ).astype(jnp.float32),
    )
    totals = (
        lax.psum(shares[0].astype(jnp.bfloat16), "batch").astype(jnp.float32),
        lax.psum(shares[1].astype(jnp.bfloat16), "batch").astype(jnp.float32),
        lax.psum(shares[2].astype(jnp.bfloat16), "batch").astype(jnp.float32),
        lax.psum(shares[3].astype(jnp.bfloat16), "batch").astype(jnp.float32),
        lax.psum(shares[4].astype(jnp.bfloat16), "batch").astype(jnp.float32),
        lax.psum(shares[5].astype(jnp.bfloat16), "batch").astype(jnp.float32),
        lax.psum(shares[6].astype(jnp.bfloat16), "batch").astype(jnp.float32),
        lax.psum(shares[7].astype(jnp.bfloat16), "batch").astype(jnp.float32),
        lax.psum(shares[8].astype(jnp.bfloat16), "batch").astype(jnp.float32),
        lax.psum(shares[9].astype(jnp.bfloat16), "batch").astype(jnp.float32),
        lax.psum(shares[10].astype(jnp.bfloat16), "batch").astype(jnp.float32),
        lax.psum(shares[11].astype(jnp.bfloat16), "batch").astype(jnp.float32),
        lax.psum(shares[12].astype(jnp.bfloat16), "batch").astype(jnp.float32),
        lax.psum(shares[13].astype(jnp.bfloat16), "batch").astype(jnp.float32),
    )
    return (
        layer_out,
        keyval_local,
        grad_tokens,
        totals[0],
        totals[1],
        totals[2],
        totals[3],
        totals[4],
        totals[5],
        totals[6],
        totals[7],
        totals[8],
        totals[9],
        totals[10],
        totals[11],
        totals[12],
        totals[13],
    )


ROT_HALF = ROT // 2


def nn(left, right):
    return lax.dot_general(left, right, (((1,), (0,)), ((), ())), preferred_element_type=f32)


def nt(left, right):
    return lax.dot_general(left, right, (((1,), (1,)), ((), ())), preferred_element_type=f32)


def tn(left, right):
    return lax.dot_general(left, right, (((0,), (0,)), ((), ())), preferred_element_type=f32)


def tt(left, right):
    return lax.dot_general(left, right, (((0,), (1,)), ((), ())), preferred_element_type=f32)


def standardize(values):
    centred = values - jnp.mean(values, axis=-1, keepdims=True)
    variance = jnp.mean(centred * centred, axis=-1, keepdims=True)
    spread = lax.rsqrt(variance + epsilon)
    return centred * spread, spread


def turn(columns, cos, sin):
    a, b = columns[0:ROT_HALF], columns[ROT_HALF:ROT]
    return jnp.concatenate([a * cos - b * sin, b * cos + a * sin, columns[ROT:]], axis=0)


def turn_back(columns, cos, sin):
    a, b = columns[0:ROT_HALF], columns[ROT_HALF:ROT]
    return jnp.concatenate([a * cos + b * sin, b * cos - a * sin, columns[ROT:]], axis=0)


def params(megabytes, **rest):
    return pltpu.CompilerParams(vmem_limit_bytes=megabytes * 2**20, **rest)


def cost(flops, moved):
    return pl.CostEstimate(flops=int(flops), bytes_accessed=int(moved), transcendentals=0)


def whole(*shape):
    return pl.BlockSpec(shape, lambda *_: (0,) * len(shape))


def norm_kernel(
    live_ref, x_ref, cot_ref, seg_ref, ag_ref, as_ref, dg_ref, ds_ref, kw_ref, kb_ref, cos_ref, sin_ref,
    normed_ref, dense_ref, kv_ref, bg_ref,
):
    position = lax.broadcasted_iota(jnp.int32, (x_ref.shape[0], 1), 0)
    alive = position < live_ref[pl.program_id(0)]
    bg_ref[...] = jnp.where(alive, cot_ref[...].astype(f32), 0.0).astype(bf16)
    unit, _ = standardize(x_ref[...].astype(f32))
    normed = (unit * ag_ref[...] + as_ref[...]).astype(bf16)
    normed_ref[...] = normed
    dense_ref[...] = (unit * dg_ref[...] + ds_ref[...]).astype(bf16)
    keyval = (nn(normed, kw_ref[...]) + kb_ref[...]).T
    blk = keyval.shape[1]
    keyval = turn(keyval, cos_ref[...], sin_ref[...])
    kv_ref[0, 0:blk, :] = keyval.T.astype(bf16)
    ids = seg_ref[0].astype(f32)
    kv_ref[0, blk:, :] = jnp.concatenate(
        [ids, jnp.zeros((16 - ids.shape[0], 128), f32)], axis=0
    ).astype(bf16)


def norms(live, x, cot, seg, again, ashift, dgain, dshift, kw, kb, cos, sin, rows, blk):
    tok, width = x.shape
    tile = pl.BlockSpec((blk, width), lambda r, *_: (r, 0))
    return pl.pallas_call(
        norm_kernel,
        grid_spec=pltpu.PrefetchScalarGridSpec(
            num_scalar_prefetch=1,
            grid=(rows,),
            in_specs=[
                tile, tile,
                pl.BlockSpec((1, blk // 128, 128), lambda r, *_: (r, 0, 0)),
                whole(1, width), whole(1, width), whole(1, width), whole(1, width),
                whole(width, 2 * HEAD_DIM), whole(1, 2 * HEAD_DIM),
                whole(ROT_HALF, blk), whole(ROT_HALF, blk),
            ],
            out_specs=[
                tile, tile, pl.BlockSpec((1, blk + 16, 2 * HEAD_DIM), lambda r, *_: (r, 0, 0)), tile,
            ],
        ),
        out_shape=[
            jax.ShapeDtypeStruct((tok, width), bf16),
            jax.ShapeDtypeStruct((tok, width), bf16),
            jax.ShapeDtypeStruct((rows, blk + 16, 2 * HEAD_DIM), bf16),
            jax.ShapeDtypeStruct((tok, width), bf16),
        ],
        compiler_params=params(32),
        cost_estimate=cost(2 * tok * width * 2 * HEAD_DIM, 10 * tok * width),
        name="norms",
    )(live, x, cot, seg, again, ashift, dgain, dshift, kw, kb, cos, sin)


def heads_kernel(
    normed_ref, bg_ref, qw_ref, qb_ref, ow_ref, cos_ref, sin_ref,
    q_ref, do_ref,
):
    blk = normed_ref.shape[0]
    queries = (nn(normed_ref[...], qw_ref[...]) + qb_ref[...]).T
    upstream = nt(ow_ref[...], bg_ref[...])
    cos, sin = cos_ref[...], sin_ref[...]
    for h in range(HEADS):
        rows = slice(h * HEAD_DIM, (h + 1) * HEAD_DIM)
        lanes = slice(h * blk, (h + 1) * blk)
        q_ref[0, :, lanes] = (turn(queries[rows], cos, sin) * HEAD_DIM**-0.5).astype(bf16)
        do_ref[0, :, lanes] = upstream[rows].astype(bf16)


def heads(normed, bg, qw, qb, ow, cos, sin, rows, blk):
    tok, width = normed.shape
    tile = pl.BlockSpec((blk, width), lambda r: (r, 0))
    stack = pl.BlockSpec((1, HEAD_DIM, HEADS * blk), lambda r: (r, 0, 0))
    return pl.pallas_call(
        heads_kernel,
        grid=(rows,),
        in_specs=[
            tile, tile, whole(width, width), whole(1, width), whole(width, width),
            whole(ROT_HALF, blk), whole(ROT_HALF, blk),
        ],
        out_specs=[stack, stack],
        out_shape=[
            jax.ShapeDtypeStruct((rows, HEAD_DIM, HEADS * blk), bf16),
            jax.ShapeDtypeStruct((rows, HEAD_DIM, HEADS * blk), bf16),
        ],
        compiler_params=params(40),
        cost_estimate=cost(4 * tok * width * width, 8 * tok * width),
        name="heads",
    )(normed, bg, qw, qb, ow, cos, sin)


def gelu_parts(hidden):
    size = jnp.abs(hidden)
    t = 1.0 / (1.0 + (0.3275911 * 0.5**0.5) * size)
    bell = jnp.exp2(hidden * hidden * (-0.5 * LOG2E))
    tail = t * (0.127414796 + t * (-0.142248368 + t * (0.7107068705 + t * (-0.7265760135 + t * 0.5307027145))))
    tail = tail * bell
    share = jnp.where(hidden >= 0.0, 1.0 - tail, tail)
    return share, bell * 0.3989422804014327


def towards(axis, target):
    return dict(device_id={axis: target}, device_id_type=pl.DeviceIdType.MESH)


def send(src, dst, sems, at, axis, target):
    return pltpu.make_async_remote_copy(
        src_ref=src, dst_ref=dst, send_sem=sems.at[0, at], recv_sem=sems.at[1, at],
        **towards(axis, target),
    )


def greet(planes):
    seq, batch = lax.axis_index("seq"), lax.axis_index("batch")
    barrier = pltpu.get_barrier_semaphore()
    column = [lax.rem(seq + 2 * hop, 2 * planes) for hop in range(1, planes)]
    for other in column + [seq + 1 - 2 * lax.rem(seq, 2)]:
        pl.semaphore_signal(barrier, inc=1, **towards("seq", other))
    for other in (batch + 1 - 2 * lax.rem(batch, 2), lax.rem(batch + 2, 4)):
        pl.semaphore_signal(barrier, inc=1, **towards("batch", other))
    pl.semaphore_wait(barrier, planes + 2)


def dense_kernel(
    di_ref, bg_ref, up_ref, ub_ref, down_ref, kv_ref,
    act_ref, gh_ref, red_ref, gub_ref, kvs_ref,
    hid0, hid1, gac0, gac1, act0, act1, gh0, gh1, acc_up, acc_dn, acc_ub,
    cut_up, cut_dn, core_up, core_dn, half_up, half_dn, x_up, x_dn,
    own_sem, z_sem, y_sem, core_sem, x_sem,
    *, pairs, steps, tile, parts, owners,
):
    i = pl.program_id(0)
    planes = owners // 2
    seq, batch = lax.axis_index("seq"), lax.axis_index("batch")
    plane, side = seq // 2, lax.rem(seq, 2)
    x_at, core_at = batch // 2, lax.rem(batch, 2)
    x_other, core_other = lax.rem(batch + 2, 4), batch + 1 - 2 * core_at
    y_other = seq + 1 - 2 * side

    def own_copy():
        return pltpu.make_async_copy(kv_ref, kvs_ref.at[seq], own_sem)

    def hop_copy(hop):
        block = kv_ref if hop == 0 else kvs_ref.at[seq - 2 * hop]
        return send(block, kvs_ref.at[seq - 2 * hop], z_sem, hop, "seq", seq + 2)

    def across_copy(hop):
        block = kv_ref if hop == 0 else kvs_ref.at[seq - 2 * hop]
        return send(block, kvs_ref.at[seq - 2 * hop], y_sem, hop, "seq", y_other)

    def spread(hop):
        @pl.when(plane >= hop)
        def _():
            if hop > 0:
                arrived(hop)
            across_copy(hop).start()

            @pl.when(plane < planes - 1)
            def _():
                hop_copy(hop).start()

    def arrived(hop):
        block = kvs_ref.at[seq - 2 * hop]
        send(block, block, z_sem, hop - 1, "seq", y_other).wait_recv()

    def settle(hop):
        @pl.when(plane >= hop)
        def _():
            across_copy(hop).wait_send()
            block = kvs_ref.at[y_other - 2 * hop]
            send(block, block, y_sem, hop, "seq", y_other).wait_recv()

            @pl.when(plane < planes - 1)
            def _():
                hop_copy(hop).wait_send()

    def core_copies(c):
        return [
            send(cut_up.at[1 - core_at], core_up.at[c], core_sem, 2 * c, "batch", core_other),
            send(cut_dn.at[1 - core_at], core_dn.at[c], core_sem, 2 * c + 1, "batch", core_other),
        ]

    def x_copies(c):
        return [
            send(half_up.at[1 - x_at], x_up.at[c], x_sem, 2 * c, "batch", x_other),
            send(half_dn.at[1 - x_at], x_dn.at[c], x_sem, 2 * c + 1, "batch", x_other),
        ]

    def plus(first, second):
        return (first.astype(f32) + second.astype(f32)).astype(bf16)

    def cut(c):
        rows, cols = cut_up.shape[3], cut_up.shape[4]
        for core in range(2):
            for x in range(2):
                for o in range(owners):
                    at = (2 * o + core) * rows
                    cut_up[core, x, o] = acc_up[at : at + rows, x * cols : (x + 1) * cols].astype(bf16)
                tall = cut_dn.shape[3]
                for o in range(cut_dn.shape[2]):
                    at = (2 * o + core) * tall
                    cut_dn[core, x, o] = acc_dn[at : at + tall, x * cols : (x + 1) * cols].astype(bf16)
        for copy in core_copies(c):
            copy.start()

    def halve(c):
        for copy in core_copies(c):
            copy.wait()
        for x in range(2):
            half_up[x] = plus(cut_up[core_at, x], core_up[c, x])
            half_dn[x] = plus(cut_dn[core_at, x], core_dn[c, x])
        for copy in x_copies(c):
            copy.start()

    def fold(c):
        for copy in x_copies(c):
            copy.wait()
        rows = cut_up.shape[3]
        few = cut_dn.shape[2]
        red_ref[:, c * rows : (c + 1) * rows, :] = plus(half_up[x_at], x_up[c])
        red_ref[c * few : (c + 1) * few, parts * rows :, :] = plus(half_dn[x_at], x_dn[c])

    def rows_of(step, odd):
        return pl.ds(pl.multiple_of((lax.rem(step, pairs) * 2 + odd) * tile, tile), tile)

    def enter(odd, hid, gac):
        rows = rows_of(i, odd)
        hid[...] = nn(di_ref[rows, :], up_ref[...]) + ub_ref[...]
        gac[...] = nt(bg_ref[rows, :], down_ref[...])

    def bend(odd, hid, gac, act_s, gh_s):
        hidden = hid[...]
        share, bell = gelu_parts(hidden)
        act = (hidden * share).astype(bf16)
        grad = (gac[...] * (share + hidden * bell)).astype(bf16)
        act_s[...] = act
        gh_s[...] = grad
        at = (1 - odd) * tile
        act_ref[at : at + tile, :] = act
        gh_ref[at : at + tile, :] = grad

    def gather(odd, act_s, gh_s):
        rows = rows_of(i - 1, odd)
        grad = gh_s[...]
        acc_up[...] += tn(di_ref[rows, :], grad)
        acc_dn[...] += tn(act_s[...], bg_ref[rows, :])
        acc_ub[...] += jnp.sum(grad.astype(f32), axis=0, keepdims=True)

    def clear():
        acc_up[...] = jnp.zeros(acc_up.shape, f32)
        acc_dn[...] = jnp.zeros(acc_dn.shape, f32)
        acc_ub[...] = jnp.zeros(acc_ub.shape, f32)

    @pl.when(i == 0)
    def _():
        greet(planes)
        own_copy().start()

    @pl.when(i == 0)
    def _():
        clear()
        enter(0, hid0, gac0)
        enter(1, hid1, gac1)
        bend(0, hid0, gac0, act0, gh0)

    @pl.when((i > 0) & (i < steps))
    def _():
        enter(0, hid0, gac0)
        bend(1, hid1, gac1, act1, gh1)
        gather(0, act0, gh0)
        enter(1, hid1, gac1)
        bend(0, hid0, gac0, act0, gh0)
        gather(1, act1, gh1)

    @pl.when(i == steps)
    def _():
        bend(1, hid1, gac1, act1, gh1)
        gather(0, act0, gh0)
        gather(1, act1, gh1)

    for c in range(parts):
        @pl.when(i == (c + 1) * pairs)
        def _():
            gub_ref[c] = acc_ub[...]
            cut(c)
            clear()

        if c < parts - 1:
            @pl.when(i == (c + 1) * pairs + 1)
            def _():
                if c > 0:
                    fold(c - 1)
                halve(c)

    for hop in range(planes):
        @pl.when(i == hop * pairs)
        def _():
            spread(hop)

    @pl.when(i == steps)
    def _():
        fold(parts - 2)
        halve(parts - 1)
        own_copy().wait()
        for hop in range(planes):
            settle(hop)
        fold(parts - 1)


def dense(di, bg, up, ub, down, kv, parts, owners, tile=512):
    tok, width = di.shape
    ff = up.shape[1]
    chunk = ff // parts
    pairs = tok // tile // 2
    steps = pairs * parts
    high, low, cols = width // owners // 2, chunk // (owners // parts) // 2, chunk // 2
    few = owners // parts
    at = lambda i: jnp.clip(i, 0, steps - 1)
    anywhere = pl.BlockSpec(memory_space=pl.ANY)
    once = lambda *shape: pl.BlockSpec(
        shape, lambda *_: (0,) * len(shape), pipeline_mode=pl.Buffered(1)
    )
    dma = pltpu.SemaphoreType.DMA
    return pl.pallas_call(
        partial(
            dense_kernel, pairs=pairs, steps=steps, tile=tile, parts=parts, owners=owners
        ),
        grid=(steps + 1,),
        in_specs=[
            once(tok, width),
            once(tok, width),
            pl.BlockSpec((width, chunk), lambda i: (0, at(i) // pairs)),
            pl.BlockSpec((1, chunk), lambda i: (0, at(i) // pairs)),
            pl.BlockSpec((chunk, width), lambda i: (at(i) // pairs, 0)),
            anywhere,
        ],
        out_specs=[
            pl.BlockSpec((2 * tile, chunk), lambda i: (i, 0)),
            pl.BlockSpec((2 * tile, chunk), lambda i: (i, 0)),
            whole(owners, parts * high + low, cols),
            whole(parts, 1, chunk),
            anywhere,
        ],
        out_shape=[
            jax.ShapeDtypeStruct((2 * tile * (steps + 1), chunk), bf16),
            jax.ShapeDtypeStruct((2 * tile * (steps + 1), chunk), bf16),
            jax.ShapeDtypeStruct((owners, parts * high + low, cols), bf16),
            jax.ShapeDtypeStruct((parts, 1, chunk), f32),
            jax.ShapeDtypeStruct((owners,) + kv.shape, bf16),
        ],
        scratch_shapes=[pltpu.VMEM((tile, chunk), f32)] * 4
        + [pltpu.VMEM((tile, chunk), bf16)] * 4
        + [
            pltpu.VMEM((width, chunk), f32), pltpu.VMEM((chunk, width), f32),
            pltpu.VMEM((1, chunk), f32),
            pltpu.VMEM((2, 2, owners, high, cols), bf16), pltpu.VMEM((2, 2, few, low, cols), bf16),
            pltpu.VMEM((parts, 2, owners, high, cols), bf16),
            pltpu.VMEM((parts, 2, few, low, cols), bf16),
            pltpu.VMEM((2, owners, high, cols), bf16), pltpu.VMEM((2, few, low, cols), bf16),
            pltpu.VMEM((parts, owners, high, cols), bf16),
            pltpu.VMEM((parts, few, low, cols), bf16),
            dma, dma((2, owners // 2)), dma((2, owners // 2)), dma((2, 2 * parts)),
            dma((2, 2 * parts)),
        ],
        compiler_params=params(60, collective_id=0, has_side_effects=True),
        cost_estimate=cost(8 * tok * width * ff, 8 * tok * width + 4 * tok * ff),
        name="dense",
    )(di, bg, up, ub, down, kv)


def tail_kernel(
    x_ref, cot_ref, valid_ref, att_ref, gq_ref, bg_ref, normed_ref, kcot_ref, terms_ref, gub_ref,
    ow_ref, ob_ref, down_ref, db_ref, up_ref, qw_ref, kw_ref, ag_ref, as_ref, dg_ref, cos_ref, sin_ref,
    *refs, rows, parts, owners,
):
    acts, ghs, refs = refs[:parts], refs[parts : 2 * parts], refs[2 * parts :]
    (
        out_ref, gt_ref, square_ref, keyval_ref, vector_ref,
        acc, gd_s, gn_s, gk_s, vec_s,
        own, across, below, total,
        cut, core_in, half, x_in, piece, piece_in, part, part_in,
        small_k, small_v, seq_k, seq_v, mid_k, mid_v, batch_k, batch_v,
        own_sem, y_sem, z_sem, core_sem, x_sem, piece_sem, part_sem, sk_sem, sv_sem, bk_sem, bv_sem,
    ) = refs
    i = pl.program_id(0)
    planes = owners // 2
    seq, batch = lax.axis_index("seq"), lax.axis_index("batch")
    plane, side = seq // 2, lax.rem(seq, 2)
    x_at, core_at = batch // 2, lax.rem(batch, 2)
    x_other, core_other = lax.rem(batch + 2, 4), batch + 1 - 2 * core_at
    y_other = seq + 1 - 2 * side
    high, cols = cut.shape[4], cut.shape[5]

    def enter():
        barrier = pltpu.get_barrier_semaphore()
        for hop in range(1, owners):
            pl.semaphore_signal(barrier, inc=1, **towards("seq", lax.rem(seq + hop, owners)))
        for hop in range(1, parts):
            pl.semaphore_signal(barrier, inc=1, **towards("batch", lax.rem(batch + hop, parts)))
        pl.semaphore_wait(barrier, owners + parts - 2)

    def own_copy(k):
        return pltpu.make_async_copy(terms_ref.at[2 * k + side], own.at[k], own_sem.at[k])

    def across_copy(k):
        return send(terms_ref.at[2 * k + 1 - side], across.at[k], y_sem, k, "seq", y_other)

    def below_copy(k):
        target = lax.rem(seq + 2 * planes - 2, 2 * planes)
        return send(own.at[k], below.at[k], z_sem, k, "seq", target)

    def start_across(k):
        @pl.when(plane >= k)
        def _():
            own_copy(k).start()
            across_copy(k).start()

    def tick(step):
        k = step - (planes - 1 - plane)

        @pl.when(k >= 0)
        def _():
            own_copy(k).wait()
            across_copy(k).wait_recv()
            total[...] = own[k].astype(f32) + across[k].astype(f32)

            @pl.when(plane < planes - 1)
            def _():
                below_copy(k).wait_recv()
                total[...] += below[k].astype(f32)

            if step < planes - 1:
                own[k] = total[...].astype(bf16)
                below_copy(k).start()

    def settle():
        for k in range(planes):
            @pl.when(plane >= k)
            def _():
                across_copy(k).wait_send()

            @pl.when(plane > k)
            def _():
                below_copy(k).wait_send()

    def core_copy():
        return send(cut.at[1 - core_at], core_in, core_sem, 0, "batch", core_other)

    def x_copy():
        return send(half.at[1 - x_at], x_in, x_sem, 0, "batch", x_other)

    def piece_copy(hop):
        target = lax.rem(seq + hop, owners)
        return send(piece.at[target], piece_in.at[hop - 1], piece_sem, hop - 1, "seq", target)

    def part_copy(hop):
        target = lax.rem(batch + hop, parts)
        return send(part, part_in.at[hop - 1], part_sem, hop - 1, "batch", target)

    def cut_square():
        for m in range(2):
            for core in range(2):
                for x in range(2):
                    for o in range(owners):
                        at = (2 * o + core) * high
                        cut[core, x, o, m] = acc[m, at : at + high, x * cols : (x + 1) * cols].astype(bf16)
        core_copy().start()

    def halve_square():
        core_copy().wait()
        for x in range(2):
            half[x] = (cut[core_at, x].astype(f32) + core_in[x].astype(f32)).astype(bf16)
        x_copy().start()

    def spread_square():
        x_copy().wait()
        piece[...] = (half[x_at].astype(f32) + x_in[...].astype(f32)).astype(bf16)
        for hop in range(1, owners):
            piece_copy(hop).start()

    def sum_square():
        value = piece[seq].astype(f32)
        for hop in range(1, owners):
            piece_copy(hop).wait()
            value = value + piece_in[hop - 1].astype(f32)
        part[...] = value.astype(bf16)
        for hop in range(1, parts):
            part_copy(hop).start()

    def collect_square():
        square_ref[batch] = part[...].astype(f32)
        for hop in range(1, parts):
            part_copy(hop).wait()
            square_ref[lax.rem(batch + parts - hop, parts)] = part_in[hop - 1].astype(f32)

    def seq_copies(hop):
        target = lax.rem(seq + hop, owners)
        return [
            send(small_k.at[target], seq_k.at[hop - 1], sk_sem, hop - 1, "seq", target),
            send(small_v, seq_v.at[hop - 1], sv_sem, hop - 1, "seq", target),
        ]

    def batch_copies(hop):
        target = lax.rem(batch + hop, parts)
        return [
            send(mid_k, batch_k.at[hop - 1], bk_sem, hop - 1, "batch", target),
            send(mid_v, batch_v.at[hop - 1], bv_sem, hop - 1, "batch", target),
        ]

    def reduce_small():
        tall = small_k.shape[1]
        keyval = gk_s[...].T
        for o in range(owners):
            small_k[o] = keyval[o * tall : (o + 1) * tall].astype(bf16)
        small_v[...] = vec_s[...].astype(bf16)
        for hop in range(1, owners):
            for copy in seq_copies(hop):
                copy.start()
        value, vector = small_k[seq].astype(f32), small_v[...].astype(f32)
        for hop in range(1, owners):
            for copy in seq_copies(hop):
                copy.wait()
            value = value + seq_k[hop - 1].astype(f32)
            vector = vector + seq_v[hop - 1].astype(f32)
        mid_k[...] = value.astype(bf16)
        mid_v[...] = vector.astype(bf16)
        for hop in range(1, parts):
            for copy in batch_copies(hop):
                copy.start()
        value, vector = mid_k[...].astype(f32), mid_v[...].astype(f32)
        for hop in range(1, parts):
            for copy in batch_copies(hop):
                copy.wait()
            value = value + batch_k[hop - 1].astype(f32)
            vector = vector + batch_v[hop - 1].astype(f32)
        keyval_ref[...] = value
        vector_ref[...] = vector

    def project():
        branch, grad = bg_ref[...], gq_ref[0]
        acc[0] += nn(att_ref[0], branch)
        acc[1] += tt(normed_ref[...], grad)
        ones = jnp.ones((8, branch.shape[0]), bf16)
        vec_s[0:1] += nt(ones, grad)[0:1]
        vec_s[1:2] += nn(ones, branch)[0:1]

    def close(r):
        act = jnp.concatenate([ref[...] for ref in acts], axis=1)
        grad = jnp.concatenate([ref[...] for ref in ghs], axis=1)
        branch = tn(att_ref[0], ow_ref[...]) + ob_ref[...]
        branch = branch + (nn(act, down_ref[...]) + db_ref[...])
        out_ref[...] = (x_ref[...].astype(f32) + valid_ref[...] * branch).astype(bf16)
        gd_s[r] = nt(grad, up_ref[...])
        gn_s[r] = tt(gq_ref[0], qw_ref[...])

    def finish(r):
        unit, spread = standardize(x_ref[...].astype(f32))
        gain = ag_ref[...]
        normed = (unit * gain + as_ref[...]).astype(bf16)
        keyval = (total[r] + kcot_ref[0].astype(f32)).T
        keyval = turn_back(keyval, cos_ref[...], sin_ref[...]).astype(bf16)
        gk_s[...] += nn(keyval, normed)
        vec_s[6:7, 0 : keyval.shape[0]] += nt(jnp.ones((8, keyval.shape[1]), bf16), keyval)[0:1]
        first = gn_s[r] + tt(keyval, kw_ref[...])
        second = gd_s[r]
        vec_s[2:3] += jnp.sum(first * unit, axis=0, keepdims=True)
        vec_s[3:4] += jnp.sum(first, axis=0, keepdims=True)
        vec_s[4:5] += jnp.sum(second * unit, axis=0, keepdims=True)
        vec_s[5:6] += jnp.sum(second, axis=0, keepdims=True)
        both = first * gain + second * dg_ref[...]
        middle = jnp.mean(both, axis=-1, keepdims=True)
        along = jnp.mean(both * unit, axis=-1, keepdims=True)
        gt_ref[...] = (cot_ref[...].astype(f32) + (both - middle - unit * along) * spread).astype(bf16)

    def at(step):
        return pl.when(i == step)

    @at(0)
    def _():
        enter()
        start_across(0)
        acc[...] = jnp.zeros(acc.shape, f32)
        gk_s[...] = jnp.zeros(gk_s.shape, f32)
        vec_s[...] = jnp.zeros(vec_s.shape, f32)
        for c in range(parts):
            vec_s[8 + c : 9 + c] = gub_ref[c]

    marks = (rows + 1, rows + 3, rows + 6, 2 * rows)
    for step in range(planes):
        @at(marks[step])
        def _():
            if step < planes - 1:
                start_across(step + 1)
            tick(step)

    @at(rows)
    def _():
        cut_square()

    @at(rows + 2)
    def _():
        halve_square()

    @at(rows + 5)
    def _():
        spread_square()

    @at(2 * rows + 2)
    def _():
        sum_square()

    @at(2 * rows + 6)
    def _():
        collect_square()
        settle()

    @pl.when(i < rows)
    def _():
        project()

    @pl.when((i >= rows) & (i < 2 * rows))
    def _():
        close(i - rows)

    @pl.when((i >= 2 * rows) & (i < 3 * rows))
    def _():
        finish(i - 2 * rows)

    @at(3 * rows)
    def _():
        reduce_small()


def tail(
    x, cot, valid, att, gq, bg, normed, kcot, terms, gub, ow, ob, down, db, up, qw, kw, again, ashift,
    dgain, cos, sin, act, gh, parts, owners, dense_tile=512,
):
    rows, width, blk = att.shape
    tok, ff, kvw = rows * blk, up.shape[1], kw.shape[1]
    ratio, tiles = dense_tile // blk, tok // dense_tile
    planes = owners // 2
    high, cols, tall = width // owners // 2, width // 2, width // owners
    once = lambda *shape: pl.BlockSpec(
        shape, lambda i: (0,) * len(shape), pipeline_mode=pl.Buffered(1)
    )
    one = lambda i: jnp.clip(i, 0, rows - 1)
    two = lambda i: jnp.where(i < 2 * rows, i % rows, rows - 1)
    middle = lambda i: jnp.clip(i - rows, 0, rows - 1)
    late = lambda i: jnp.clip(i - 2 * rows, 0, rows - 1)
    both = lambda i: jnp.where(i < 2 * rows, middle(i), late(i))
    flat = lambda of, w=width: pl.BlockSpec((blk, w), lambda i: (of(i), 0))
    stack = lambda of, h, w: pl.BlockSpec((1, h, w), lambda i: (of(i), 0, 0))
    wide = [
        pl.BlockSpec(
            (blk, ff // parts),
            lambda i, c=c: ((c * tiles + middle(i) // ratio + 1) * ratio + middle(i) % ratio, 0),
        )
        for c in range(parts)
    ]
    dma = pltpu.SemaphoreType.DMA
    vmem = lambda kind, *shape: pltpu.VMEM(shape, kind)
    return pl.pallas_call(
        partial(tail_kernel, rows=rows, parts=parts, owners=owners),
        grid=(3 * rows + 1,),
        in_specs=[
            flat(both), flat(late), flat(middle, 1), stack(two, width, blk), stack(two, width, blk),
            flat(one), flat(one), stack(late, blk, kvw), pl.BlockSpec(memory_space=pl.ANY),
            once(parts, 1, ff // parts),
            once(width, width), once(1, width), once(ff, width), once(1, width), once(width, ff),
            once(width, width), once(width, kvw), once(1, width), once(1, width), once(1, width),
            once(ROT_HALF, blk), once(ROT_HALF, blk),
        ] + wide + wide,
        out_specs=[
            flat(middle), flat(late), once(parts, 2, high, cols), once(tall, kvw), once(16, width),
        ],
        out_shape=[
            jax.ShapeDtypeStruct((tok, width), bf16),
            jax.ShapeDtypeStruct((tok, width), bf16),
            jax.ShapeDtypeStruct((parts, 2, high, cols), f32),
            jax.ShapeDtypeStruct((tall, kvw), f32),
            jax.ShapeDtypeStruct((16, width), f32),
        ],
        scratch_shapes=[
            vmem(f32, 2, width, width), vmem(f32, rows, blk, width), vmem(f32, rows, blk, width),
            vmem(f32, kvw, width), vmem(f32, 16, width),
            vmem(bf16, planes, rows, blk, kvw), vmem(bf16, planes, rows, blk, kvw),
            vmem(bf16, planes, rows, blk, kvw), vmem(f32, rows, blk, kvw),
            vmem(bf16, 2, 2, owners, 2, high, cols), vmem(bf16, 2, owners, 2, high, cols),
            vmem(bf16, 2, owners, 2, high, cols), vmem(bf16, owners, 2, high, cols),
            vmem(bf16, owners, 2, high, cols), vmem(bf16, owners - 1, 2, high, cols),
            vmem(bf16, 2, high, cols), vmem(bf16, parts - 1, 2, high, cols),
            vmem(bf16, owners, tall, kvw), vmem(bf16, 16, width),
            vmem(bf16, owners - 1, tall, kvw), vmem(bf16, owners - 1, 16, width),
            vmem(bf16, tall, kvw), vmem(bf16, 16, width),
            vmem(bf16, parts - 1, tall, kvw), vmem(bf16, parts - 1, 16, width),
            dma((planes,)), dma((2, planes)), dma((2, planes)), dma((2, 1)), dma((2, 1)),
            dma((2, owners - 1)), dma((2, parts - 1)), dma((2, owners - 1)), dma((2, owners - 1)),
            dma((2, parts - 1)), dma((2, parts - 1)),
        ],
        compiler_params=params(62, collective_id=1, has_side_effects=True),
        cost_estimate=cost(4 * tok * width * (2 * width + ff), 4 * tok * ff + 20 * tok * width),
        name="tail",
    )(
        x, cot, valid, att, gq, bg, normed, kcot, terms, gub, ow, ob, down, db, up, qw, kw, again,
        ashift, dgain, cos, sin, *[act] * parts, *[gh] * parts,
    )


def attn_kernel(first_ref, sidx_ref, q_ref, do_ref, kv_ref, start_ref, cos_ref, sin_ref,
                att_ref, gq_ref, dkv_ref,
                qz, dz, p_s, m_s, bias_s, o_s, mx, ls, dq_s, dc_s, inn_s, ds_s, ic_s, *, blk, nblk):
    r = pl.program_id(0)
    L = HEADS*blk
    e = sidx_ref[0]
    n = e - first_ref[r] + 1
    qz[0:HEAD_DIM,:] = q_ref[0]
    qz[HEAD_DIM:,:] = jnp.zeros((HEAD_DIM,L),bf16)
    dz[0:HEAD_DIM,:] = jnp.zeros((HEAD_DIM,L),bf16)
    mx[...] = jnp.full((1,L),negative,f32)
    ls[...] = jnp.zeros((1,L),f32)
    o_s[...] = jnp.zeros((HEAD_DIM,L),f32)
    dq_s[...] = jnp.zeros((HEAD_DIM,L),f32)
    start = start_ref[0]
    qpos = e*blk + lax.broadcasted_iota(jnp.int32,(1,blk),1)
    krow = lax.broadcasted_iota(jnp.int32,(blk,blk),0)

    @pl.loop(0, nblk)
    def _(j):
        @pl.when((j < first_ref[r]) | (j > e))
        def _():
            dkv_ref[j,0] = jnp.zeros((blk,2*HEAD_DIM),bf16)

    @pl.loop(0, n)
    def _(jj):
        j = e - jj
        kvj = kv_ref[j, 0, 0:blk, :]
        vt = kvj.T[HEAD_DIM:,:]
        kpos = j*blk + krow
        bias_s[...] = jnp.where((kpos>=start)&(kpos<=qpos), 0.0, negative)
        def hsl(h): return slice(h*blk,(h+1)*blk)
        sv = {}; pv = {}; av = {}
        for h in range(HEADS+2):
            if h < HEADS:
                sv[h] = nn(kvj, qz[:,hsl(h)])
            if 0 <= h-2 < HEADS:
                g = h-2; hs = hsl(g)
                o_s[:,hs] = o_s[:,hs]*av.pop(g) + nn(vt,pv.pop(g))
            if 0 <= h-1 < HEADS:
                g = h-1; hs = hsl(g)
                s = sv.pop(g)*LOG2E + bias_s[...]
                mo = mx[:,hs]
                mn = jnp.maximum(mo, jnp.max(s,axis=0,keepdims=True))
                p = jnp.exp2(s-mn)
                a = jnp.exp2(mo-mn)
                ls[:,hs] = ls[:,hs]*a + jnp.sum(p,axis=0,keepdims=True)
                pb = p.astype(bf16)
                p_s[jj,:,hs] = pb
                m_s[jj,:,hs] = mn
                mx[:,hs] = mn
                pv[g]=pb; av[g]=a

    inv = 1.0/ls[...]
    o = o_s[...]*inv
    for h in range(HEADS):
        att_ref[0, h*HEAD_DIM:(h+1)*HEAD_DIM, :] = o[:, h*blk:(h+1)*blk].astype(bf16)
    do = do_ref[0].astype(f32)
    inn_s[...] = jnp.sum(o*do,axis=0,keepdims=True)
    ls[...] = inv

    @pl.loop(0, n)
    def _(jj):
        j = e - jj
        kvj = kv_ref[j, 0, 0:blk, :]
        kt = kvj.T[:HEAD_DIM,:]
        def hsl(h): return slice(h*blk,(h+1)*blk)
        c = jnp.exp2(m_s[jj]-mx[...])*ls[...]
        dc_s[...] = (do_ref[0].astype(f32)*c).astype(bf16)
        dz[HEAD_DIM:,:] = dc_s[...]
        ic_s[...] = inn_s[...]*c
        dpv = {}; dsv = {}
        for h in range(HEADS+2):
            if h < HEADS:
                dpv[h] = nn(kvj, dz[:,hsl(h)])
            if 0 <= h-2 < HEADS:
                g = h-2; hs = hsl(g)
                dq_s[:,hs] = dq_s[:,hs] + nn(kt, dsv.pop(g))
            if 0 <= h-1 < HEADS:
                g = h-1; hs = hsl(g)
                pb = p_s[jj,:,hs]
                ds = (pb.astype(f32)*(dpv.pop(g)-ic_s[:,hs])).astype(bf16)
                ds_s[:,hs] = ds
                dsv[g] = ds
        dv = nt(p_s[jj], dc_s[...])
        dk = nt(ds_s[...], qz[0:HEAD_DIM,:])
        dkv_ref[j,0] = jnp.concatenate([dk,dv],axis=1).astype(bf16)

    cos = cos_ref[...]; sin = sin_ref[...]
    for h in range(HEADS):
        g = dq_s[:, h*blk:(h+1)*blk]*(HEAD_DIM**-0.5)
        a, b = g[0:8], g[8:16]
        gq_ref[0, h*HEAD_DIM:(h+1)*HEAD_DIM, :] = jnp.concatenate([a*cos+b*sin, b*cos-a*sin, g[16:]],axis=0).astype(bf16)

def attention(first, sidx, qT, doT, kv, start, cosT, sinT):
    rows, _, L = qT.shape
    blk = L//HEADS
    nblk = kv.shape[0]
    gs = pltpu.PrefetchScalarGridSpec(
        num_scalar_prefetch=2, grid=(rows,),
        in_specs=[
            pl.BlockSpec((1,HEAD_DIM,L),lambda r,*_:(r,0,0)),
            pl.BlockSpec((1,HEAD_DIM,L),lambda r,*_:(r,0,0)),
            pl.BlockSpec((nblk,1,blk+16,2*HEAD_DIM),lambda r,*_:(0,r,0,0)),
            pl.BlockSpec((1,1,blk),lambda r,*_:(r,0,0)),
            pl.BlockSpec((8,blk),lambda r,*_:(0,0)),
            pl.BlockSpec((8,blk),lambda r,*_:(0,0)),
        ],
        out_specs=[
            pl.BlockSpec((1,HEADS*HEAD_DIM,blk),lambda r,*_:(r,0,0)),
            pl.BlockSpec((1,HEADS*HEAD_DIM,blk),lambda r,*_:(r,0,0)),
            pl.BlockSpec((nblk,1,blk,2*HEAD_DIM),lambda r,*_:(0,r,0,0)),
        ],
        scratch_shapes=[
            pltpu.VMEM((2*HEAD_DIM,L),bf16), pltpu.VMEM((2*HEAD_DIM,L),bf16),
            pltpu.VMEM((nblk,blk,L),bf16), pltpu.VMEM((nblk,1,L),f32),
            pltpu.VMEM((blk,blk),f32), pltpu.VMEM((HEAD_DIM,L),f32),
            pltpu.VMEM((1,L),f32), pltpu.VMEM((1,L),f32),
            pltpu.VMEM((HEAD_DIM,L),f32), pltpu.VMEM((HEAD_DIM,L),bf16), pltpu.VMEM((1,L),f32), pltpu.VMEM((blk,L),bf16), pltpu.VMEM((1,L),f32),
        ])
    return pl.pallas_call(
        partial(attn_kernel, blk=blk, nblk=nblk),
        out_shape=[jax.ShapeDtypeStruct((rows,HEADS*HEAD_DIM,blk),bf16),
                   jax.ShapeDtypeStruct((rows,HEADS*HEAD_DIM,blk),bf16),
                   jax.ShapeDtypeStruct((nblk,rows,blk,2*HEAD_DIM),bf16)],
        grid_spec=gs,
        compiler_params=params(56),
        cost_estimate=cost(6e10, 4e7),
        name="attention",
    )(first, sidx, qT, doT, kv, start, cosT, sinT)


def local(
    tokens,
    segment_ids,
    query_weight,
    query_bias,
    keyval_weight,
    keyval_bias,
    out_weight,
    out_bias,
    up_weight,
    up_bias,
    down_weight,
    down_bias,
    attention_gain,
    attention_shift,
    dense_gain,
    dense_shift,
    out_cotangent,
    keyval_cotangent,
):
    rows, blk, width = tokens.shape
    ff = up_weight.shape[1]
    kvw = 2 * HEAD_DIM
    tok = rows * blk
    owners, parts = lax.axis_size("seq"), lax.axis_size("batch")
    place = lax.axis_index("seq")
    cos, sin = rotary_tables(place * blk + jnp.arange(blk, dtype=jnp.int32))
    cos, sin = cos.T, sin.T
    live = jnp.sum((segment_ids >= 0).astype(jnp.int32), axis=1).astype(jnp.int32)
    x = tokens.reshape(tok, width)
    cot = out_cotangent.reshape(tok, width)
    row = lambda vector: vector.reshape(1, -1)

    normed, dense_in, keyval, branch_grad = norms(
        live, x, cot, segment_ids.reshape(rows, blk // 128, 128), row(attention_gain),
        row(attention_shift), row(dense_gain), row(dense_shift), keyval_weight, row(keyval_bias),
        cos, sin, rows, blk,
    )
    act, grad_hidden, mlp, gub, keyval_all = dense(
        dense_in, branch_grad, up_weight, row(up_bias), down_weight, keyval, parts, owners
    )
    queries, grad_attended = heads(
        normed, branch_grad, query_weight, row(query_bias), out_weight, cos, sin, rows, blk
    )
    mlp = lax.psum_scatter(mlp, "seq", scatter_dimension=0)
    mlp = lax.all_gather(mlp, "batch").astype(f32)
    high, half = width // owners // 2, ff // parts // 2
    grad_up_weight = (
        mlp[:, : parts * high]
        .reshape(2, 2, parts, high, half)
        .transpose(1, 3, 2, 0, 4)
        .reshape(width // owners, ff)
    )
    grad_down_weight = (
        mlp[:, parts * high :]
        .reshape(2, 2, ff // owners // 2, half)
        .transpose(1, 2, 0, 3)
        .reshape(ff // owners, width)
    )

    ids = keyval_all[:, :, blk : blk + blk // 128, :].reshape(owners, rows, blk).astype(f32)
    before = (jnp.arange(owners) <= place)[:, None, None]
    order = lambda values: jnp.where(values < 0, 1024.0, values)
    ids = jnp.where(before, order(ids), 2048.0)
    start = jnp.sum(
        (ids[:, :, None, :] < order(segment_ids.astype(f32))[None, :, :, None]).astype(jnp.int32),
        axis=(0, 3),
    ).astype(jnp.int32)
    attended, grad_query, terms = attention(
        start[:, 0] // blk, place.astype(jnp.int32)[None], queries, grad_attended, keyval_all,
        start[:, None, :], cos, sin,
    )
    valid = (segment_ids >= 0).astype(f32).reshape(tok, 1)
    layer_out, grad_tokens, square, grad_keyval_weight, vectors = tail(
        x, cot, valid, attended, grad_query, branch_grad, normed, keyval_cotangent, terms, gub,
        out_weight, row(out_bias), down_weight, row(down_bias), up_weight, query_weight,
        keyval_weight, row(attention_gain), row(attention_shift), row(dense_gain), cos, sin, act,
        grad_hidden, parts, owners,
    )
    square = (
        square.reshape(2, 2, 2, high, width // 2)
        .transpose(2, 1, 3, 0, 4)
        .reshape(2, width // owners, width)
    )
    share = width // owners
    mine = lambda vector, size: lax.dynamic_slice(vector, (place * size,), (size,))
    query_bias_grad, branch_sum, ag, ash, dg, dsh = [mine(vectors[i], share) for i in range(6)]
    return (
        layer_out.reshape(rows, blk, width),
        keyval[:, :blk, :],
        grad_tokens.reshape(rows, blk, width),
        square[1],
        query_bias_grad,
        grad_keyval_weight,
        mine(vectors[6], kvw // owners),
        square[0],
        branch_sum,
        grad_up_weight,
        mine(vectors[8 : 8 + parts].reshape(ff), ff // owners),
        grad_down_weight,
        branch_sum,
        ag,
        ash,
        dg,
        dsh,
    )


def choose(tokens, *rest):
    fits = tokens.shape[1] % 128 == 0 and lax.axis_size("batch") == 4 and lax.axis_size("seq") == 8
    return (local if fits else local_plain)(tokens, *rest)


def solution(mesh):
    placed = (
        P("batch", "seq", None),
        P("batch", "seq"),
        P(),
        P(),
        P(),
        P(),
        P(),
        P(),
        P(),
        P(),
        P(),
        P(),
        P(),
        P(),
        P(),
        P(),
        P("batch", "seq", None),
        P("batch", "seq", None),
    )
    return jax.shard_map(
        choose,
        mesh=mesh,
        in_specs=placed,
        out_specs=(
            P("batch", "seq", None),
            P("batch", "seq", None),
            P("batch", "seq", None),
            P("seq", None),
            P("seq"),
            P("seq", None),
            P("seq"),
            P("seq", None),
            P("seq"),
            P("seq", None),
            P("seq"),
            P("seq", None),
            P("seq"),
            P("seq"),
            P("seq"),
            P("seq"),
            P("seq"),
        ),
        check_vma=False,
    )
```

```python
from functools import partial

import jax
import jax.numpy as jnp
from jax import lax
from jax.experimental import pallas as pl
from jax.experimental.pallas import tpu as pltpu
from jax.sharding import PartitionSpec as P

HEADS = 12
HEAD_DIM = 64
ROT = 16
LOG2E = 1.4426950408889634
f32 = jnp.float32
bf16 = jnp.bfloat16


epsilon = 1e-05
rope_base = 10000.0
negative = -1e30


def layer_norm(values, gain_vector, shift_vector):
    average = jnp.mean(values, axis=-1, keepdims=True)
    centred = values - average
    variance = jnp.mean(centred * centred, axis=-1, keepdims=True)
    return centred * lax.rsqrt(variance + epsilon) * gain_vector + shift_vector


def rotary_tables(positions):
    half_rot = ROT // 2
    frequency = rope_base ** (-(2.0 * jnp.arange(half_rot, dtype=jnp.float32)) / ROT)
    angles = positions.astype(jnp.float32)[:, None] * frequency[None, :]
    return (jnp.cos(angles), jnp.sin(angles))


def rotate(values, cos_table, sin_table):
    half_rot = ROT // 2
    first_half = values[..., :half_rot]
    second_half = values[..., half_rot:ROT]
    return jnp.concatenate(
        [
            first_half * cos_table - second_half * sin_table,
            second_half * cos_table + first_half * sin_table,
            values[..., ROT:],
        ],
        axis=-1,
    )


def unrotate(values, cos_table, sin_table):
    half_rot = ROT // 2
    first_half = values[..., :half_rot]
    second_half = values[..., half_rot:ROT]
    return jnp.concatenate(
        [
            first_half * cos_table + second_half * sin_table,
            second_half * cos_table - first_half * sin_table,
            values[..., ROT:],
        ],
        axis=-1,
    )


def contract_rows(left_side, right_side):
    return lax.dot_general(
        left_side, right_side, (((0,), (0,)), ((), ())), preferred_element_type=jnp.float32
    )


def contract_cols(left_side, right_side):
    return lax.dot_general(
        left_side, right_side, (((1,), (1,)), ((), ())), preferred_element_type=jnp.float32
    )


def local_plain(
    tokens,
    segment_ids,
    query_weight,
    query_bias,
    keyval_weight,
    keyval_bias,
    out_weight,
    out_bias,
    up_weight,
    up_bias,
    down_weight,
    down_bias,
    attention_gain,
    attention_shift,
    dense_gain,
    dense_shift,
    out_cotangent,
    keyval_cotangent,
):
    rows, local_len, width = tokens.shape
    full_len = local_len * lax.axis_size("seq")
    tok_count = rows * local_len
    offset = lax.axis_index("seq") * local_len
    positions = offset + jnp.arange(local_len, dtype=jnp.int32)
    key_positions = jnp.arange(full_len, dtype=jnp.int32)
    score_scale = HEAD_DIM ** (-0.5)
    inputs = tokens.astype(jnp.float32).reshape(tok_count, width)
    valid_rows = (segment_ids >= 0).astype(jnp.float32).reshape(tok_count, 1)
    normed_full, attention_pull = jax.vjp(layer_norm, inputs, attention_gain, attention_shift)
    normed = normed_full.astype(jnp.bfloat16)
    query_pre = jnp.dot(normed, query_weight, preferred_element_type=jnp.float32) + query_bias
    keyval_pre = jnp.dot(normed, keyval_weight, preferred_element_type=jnp.float32) + keyval_bias
    cos_table, sin_table = rotary_tables(positions)
    queries = rotate(
        query_pre.reshape(rows, local_len, HEADS, HEAD_DIM),
        cos_table[:, None, :],
        sin_table[:, None, :],
    ).astype(jnp.bfloat16)
    queries = queries.transpose(0, 2, 1, 3).reshape(rows, HEADS * local_len, HEAD_DIM)
    key_part = keyval_pre[:, :HEAD_DIM].reshape(rows, local_len, HEAD_DIM)
    value_part = keyval_pre[:, HEAD_DIM:].reshape(rows, local_len, HEAD_DIM)
    keyval_local = jnp.concatenate(
        [rotate(key_part, cos_table, sin_table), value_part], axis=-1
    ).astype(jnp.bfloat16)
    keyval_all, segment_all = (
        lax.all_gather(keyval_local, "seq", axis=1, tiled=True),
        lax.all_gather(segment_ids, "seq", axis=1, tiled=True),
    )

    def scores_of(query_rows, key_rows, segment_row, segment_keys):
        scores = contract_cols(query_rows, key_rows) * score_scale
        allowed = (positions[:, None] >= key_positions[None, :]) & (
            segment_row[:, None] == segment_keys[None, :]
        )
        scores = scores.reshape(HEADS, local_len, full_len)
        return jnp.where(allowed[None], scores, negative)

    def forward_row(pieces):
        query_rows, keyval_row, segment_row, segment_keys = pieces
        scores = scores_of(query_rows, keyval_row[:, :HEAD_DIM], segment_row, segment_keys)
        top_score = jnp.max(scores, axis=-1, keepdims=True)
        expanded = jnp.exp(scores - top_score)
        row_total = jnp.sum(expanded, axis=-1, keepdims=True)
        weights = (expanded / row_total).reshape(HEADS * local_len, full_len).astype(jnp.bfloat16)
        attended_row = jnp.dot(
            weights, keyval_row[:, HEAD_DIM:], preferred_element_type=jnp.float32
        ).astype(jnp.bfloat16)
        log_total = (top_score + jnp.log(row_total)).reshape(HEADS * local_len)
        return (attended_row, log_total)

    attended, log_totals = lax.map(forward_row, (queries, keyval_all, segment_ids, segment_all))
    attended_flat = (
        attended.reshape(rows, HEADS, local_len, HEAD_DIM)
        .transpose(0, 2, 1, 3)
        .reshape(tok_count, width)
    )
    attn_out = jnp.dot(attended_flat, out_weight, preferred_element_type=jnp.float32) + out_bias
    dense_full, dense_pull = jax.vjp(layer_norm, inputs, dense_gain, dense_shift)
    dense_in = dense_full.astype(jnp.bfloat16)
    hidden = jnp.dot(dense_in, up_weight, preferred_element_type=jnp.float32) + up_bias
    activated_full, gelu_pull = jax.vjp(partial(jax.nn.gelu, approximate=False), hidden)
    activated = activated_full.astype(jnp.bfloat16)
    dense_out = jnp.dot(activated, down_weight, preferred_element_type=jnp.float32) + down_bias
    layer_out = (
        (inputs + valid_rows * (attn_out + dense_out))
        .astype(jnp.bfloat16)
        .reshape(rows, local_len, width)
    )
    upstream = out_cotangent.astype(jnp.float32).reshape(tok_count, width)
    branch_full = valid_rows * upstream
    branch_grad = branch_full.astype(jnp.bfloat16)
    branch_sum = jnp.sum(branch_full, axis=0)
    grad_out_weight = contract_rows(attended_flat, branch_grad)
    grad_down_weight = contract_rows(activated, branch_grad)
    (grad_hidden_full,) = gelu_pull(contract_cols(branch_grad, down_weight))
    grad_hidden = grad_hidden_full.astype(jnp.bfloat16)
    grad_up_weight = contract_rows(dense_in, grad_hidden)
    grad_up_bias = jnp.sum(grad_hidden.astype(jnp.float32), axis=0)
    grad_dense_in = contract_cols(grad_hidden, up_weight)
    dense_back, grad_dense_gain, grad_dense_shift = dense_pull(grad_dense_in)
    grad_attended = contract_cols(branch_grad, out_weight).astype(jnp.bfloat16)
    grad_attended = (
        grad_attended.reshape(rows, local_len, HEADS, HEAD_DIM)
        .transpose(0, 2, 1, 3)
        .reshape(rows, HEADS * local_len, HEAD_DIM)
    )
    keyval_back, segment_back = (
        lax.all_gather(keyval_local, "seq", axis=1, tiled=True),
        lax.all_gather(segment_ids, "seq", axis=1, tiled=True),
    )

    def backward_row(pieces):
        query_rows, keyval_row, segment_row, segment_keys, log_row, grad_rows = pieces
        key_rows = keyval_row[:, :HEAD_DIM]
        value_rows = keyval_row[:, HEAD_DIM:]
        scores = scores_of(query_rows, key_rows, segment_row, segment_keys)
        probs = jnp.exp(scores - log_row.reshape(HEADS, local_len, 1)).reshape(
            HEADS * local_len, full_len
        )
        grad_probs = contract_cols(grad_rows, value_rows)
        inner = jnp.sum(probs * grad_probs, axis=-1, keepdims=True)
        grad_scores = (probs * (grad_probs - inner)).astype(jnp.bfloat16)
        grad_query_rows = (
            jnp.dot(grad_scores, key_rows, preferred_element_type=jnp.float32) * score_scale
        )
        grad_key_rows = contract_rows(grad_scores, query_rows) * score_scale
        grad_value_rows = contract_rows(probs.astype(jnp.bfloat16), grad_rows)
        return (grad_query_rows, jnp.concatenate([grad_key_rows, grad_value_rows], axis=-1))

    grad_queries, keyval_terms = lax.map(
        backward_row, (queries, keyval_back, segment_ids, segment_back, log_totals, grad_attended)
    )
    keyval_grad = lax.psum_scatter(
        keyval_terms.astype(jnp.bfloat16), "seq", scatter_dimension=1, tiled=True
    ).astype(jnp.float32) + keyval_cotangent.astype(jnp.float32)
    grad_key_pre = unrotate(keyval_grad[..., :HEAD_DIM], cos_table, sin_table)
    grad_keyval_pre = (
        jnp.concatenate([grad_key_pre, keyval_grad[..., HEAD_DIM:]], axis=-1)
        .reshape(tok_count, 2 * HEAD_DIM)
        .astype(jnp.bfloat16)
    )
    grad_queries = grad_queries.reshape(rows, HEADS, local_len, HEAD_DIM).transpose(0, 2, 1, 3)
    grad_query_pre = (
        unrotate(grad_queries, cos_table[:, None, :], sin_table[:, None, :])
        .reshape(tok_count, width)
        .astype(jnp.bfloat16)
    )
    grad_query_weight = contract_rows(normed, grad_query_pre)
    grad_query_bias = jnp.sum(grad_query_pre.astype(jnp.float32), axis=0)
    grad_keyval_weight = contract_rows(normed, grad_keyval_pre)
    grad_keyval_bias = jnp.sum(grad_keyval_pre.astype(jnp.float32), axis=0)
    grad_normed = contract_cols(grad_query_pre, query_weight) + contract_cols(
        grad_keyval_pre, keyval_weight
    )
    attention_back, grad_attention_gain, grad_attention_shift = attention_pull(grad_normed)
    grad_tokens = (
        (upstream + attention_back + dense_back)
        .astype(jnp.bfloat16)
        .reshape(rows, local_len, width)
    )
    local_grads = (
        grad_query_weight,
        grad_query_bias,
        grad_keyval_weight,
        grad_keyval_bias,
        grad_out_weight,
        branch_sum,
        grad_up_weight,
        grad_up_bias,
        grad_down_weight,
        branch_sum,
        grad_attention_gain,
        grad_attention_shift,
        grad_dense_gain,
        grad_dense_shift,
    )
    shares = (
        lax.psum_scatter(
            local_grads[0].astype(jnp.bfloat16), "seq", scatter_dimension=0, tiled=True
        ).astype(jnp.float32),
        lax.psum_scatter(
            local_grads[1].astype(jnp.bfloat16), "seq", scatter_dimension=0, tiled=True
        ).astype(jnp.float32),
        lax.psum_scatter(
            local_grads[2].astype(jnp.bfloat16), "seq", scatter_dimension=0, tiled=True
        ).astype(jnp.float32),
        lax.psum_scatter(
            local_grads[3].astype(jnp.bfloat16), "seq", scatter_dimension=0, tiled=True
        ).astype(jnp.float32),
        lax.psum_scatter(
            local_grads[4].astype(jnp.bfloat16), "seq", scatter_dimension=0, tiled=True
        ).astype(jnp.float32),
        lax.psum_scatter(
            local_grads[5].astype(jnp.bfloat16), "seq", scatter_dimension=0, tiled=True
        ).astype(jnp.float32),
        lax.psum_scatter(
            local_grads[6].astype(jnp.bfloat16), "seq", scatter_dimension=0, tiled=True
        ).astype(jnp.float32),
        lax.psum_scatter(
            local_grads[7].astype(jnp.bfloat16), "seq", scatter_dimension=0, tiled=True
        ).astype(jnp.float32),
        lax.psum_scatter(
            local_grads[8].astype(jnp.bfloat16), "seq", scatter_dimension=0, tiled=True
        ).astype(jnp.float32),
        lax.psum_scatter(
            local_grads[9].astype(jnp.bfloat16), "seq", scatter_dimension=0, tiled=True
        ).astype(jnp.float32),
        lax.psum_scatter(
            local_grads[10].astype(jnp.bfloat16), "seq", scatter_dimension=0, tiled=True
        ).astype(jnp.float32),
        lax.psum_scatter(
            local_grads[11].astype(jnp.bfloat16), "seq", scatter_dimension=0, tiled=True
        ).astype(jnp.float32),
        lax.psum_scatter(
            local_grads[12].astype(jnp.bfloat16), "seq", scatter_dimension=0, tiled=True
        ).astype(jnp.float32),
        lax.psum_scatter(
            local_grads[13].astype(jnp.bfloat16), "seq", scatter_dimension=0, tiled=True
        ).astype(jnp.float32),
    )
    totals = (
        lax.psum(shares[0].astype(jnp.bfloat16), "batch").astype(jnp.float32),
        lax.psum(shares[1].astype(jnp.bfloat16), "batch").astype(jnp.float32),
        lax.psum(shares[2].astype(jnp.bfloat16), "batch").astype(jnp.float32),
        lax.psum(shares[3].astype(jnp.bfloat16), "batch").astype(jnp.float32),
        lax.psum(shares[4].astype(jnp.bfloat16), "batch").astype(jnp.float32),
        lax.psum(shares[5].astype(jnp.bfloat16), "batch").astype(jnp.float32),
        lax.psum(shares[6].astype(jnp.bfloat16), "batch").astype(jnp.float32),
        lax.psum(shares[7].astype(jnp.bfloat16), "batch").astype(jnp.float32),
        lax.psum(shares[8].astype(jnp.bfloat16), "batch").astype(jnp.float32),
        lax.psum(shares[9].astype(jnp.bfloat16), "batch").astype(jnp.float32),
        lax.psum(shares[10].astype(jnp.bfloat16), "batch").astype(jnp.float32),
        lax.psum(shares[11].astype(jnp.bfloat16), "batch").astype(jnp.float32),
        lax.psum(shares[12].astype(jnp.bfloat16), "batch").astype(jnp.float32),
        lax.psum(shares[13].astype(jnp.bfloat16), "batch").astype(jnp.float32),
    )
    return (
        layer_out,
        keyval_local,
        grad_tokens,
        totals[0],
        totals[1],
        totals[2],
        totals[3],
        totals[4],
        totals[5],
        totals[6],
        totals[7],
        totals[8],
        totals[9],
        totals[10],
        totals[11],
        totals[12],
        totals[13],
    )


ROT_HALF = ROT // 2


def nn(left, right):
    return lax.dot_general(left, right, (((1,), (0,)), ((), ())), preferred_element_type=f32)


def nt(left, right):
    return lax.dot_general(left, right, (((1,), (1,)), ((), ())), preferred_element_type=f32)


def tn(left, right):
    return lax.dot_general(left, right, (((0,), (0,)), ((), ())), preferred_element_type=f32)


def tt(left, right):
    return lax.dot_general(left, right, (((0,), (1,)), ((), ())), preferred_element_type=f32)


def standardize(values):
    centred = values - jnp.mean(values, axis=-1, keepdims=True)
    variance = jnp.mean(centred * centred, axis=-1, keepdims=True)
    spread = lax.rsqrt(variance + epsilon)
    return centred * spread, spread


def turn(columns, cos, sin):
    a, b = columns[0:ROT_HALF], columns[ROT_HALF:ROT]
    return jnp.concatenate([a * cos - b * sin, b * cos + a * sin, columns[ROT:]], axis=0)


def turn_back(columns, cos, sin):
    a, b = columns[0:ROT_HALF], columns[ROT_HALF:ROT]
    return jnp.concatenate([a * cos + b * sin, b * cos - a * sin, columns[ROT:]], axis=0)


def params(megabytes, **rest):
    return pltpu.CompilerParams(vmem_limit_bytes=megabytes * 2**20, **rest)


def cost(flops, moved):
    return pl.CostEstimate(flops=int(flops), bytes_accessed=int(moved), transcendentals=0)


def whole(*shape):
    return pl.BlockSpec(shape, lambda *_: (0,) * len(shape))


AG, AS, DG, DS, QB, OB, DB, KB, UB = range(9)


def vector(pack, at):
    return pack[at : at + 1, :]


def alive(ids):
    count = jnp.sum((ids >= 0).astype(f32), axis=1, keepdims=True)
    return lax.broadcasted_iota(jnp.int32, (ids.shape[1], 1), 0).astype(f32) < count


def norm_kernel(
    x_ref, cot_ref, seg_ref, pack, kw_ref, cos_ref, sin_ref,
    normed_ref, dense_ref, bg_ref, kv_ref, kvo_ref,
):
    count, _, kvw = kv_ref.shape
    blk = kvo_ref.shape[1]
    cos, sin = cos_ref[...], sin_ref[...]
    for n in range(count):
        rows = slice(n * blk, (n + 1) * blk)
        ids = seg_ref[pl.ds(pl.program_id(0) * count + n, 1), :]
        bg_ref[rows] = jnp.where(alive(ids), cot_ref[rows].astype(f32), 0.0).astype(bf16)
        unit, _ = standardize(x_ref[rows].astype(f32))
        normed = (unit * vector(pack, AG) + vector(pack, AS)).astype(bf16)
        normed_ref[rows] = normed
        dense_ref[rows] = (unit * vector(pack, DG) + vector(pack, DS)).astype(bf16)
        keyval = nn(normed, kw_ref[...]) + vector(pack, KB)[:, :kvw]
        keyval = turn(keyval.T, cos, sin).T.astype(bf16)
        kvo_ref[n] = keyval
        kv_ref[n, 0:blk, :] = keyval
        ids = [ids[:, at : at + 128].astype(f32) for at in range(0, blk, 128)]
        kv_ref[n, blk:, :] = jnp.concatenate(
            ids + [jnp.zeros((16 - len(ids), 128), f32)], axis=0
        ).astype(bf16)


def norms(x, cot, seg, pack, kw, cos, sin, count=2):
    tok, width = x.shape
    rows, blk = seg.shape
    kvw = kw.shape[1]
    tile = pl.BlockSpec((count * blk, width), lambda r: (r, 0))
    pair = lambda high: pl.BlockSpec((count, high, kvw), lambda r: (r, 0, 0))
    flat = jax.ShapeDtypeStruct((tok, width), bf16)
    return pl.pallas_call(
        norm_kernel,
        grid=(rows // count,),
        in_specs=[
            tile, tile, whole(rows, blk), whole(*pack.shape), whole(width, kvw),
            whole(ROT_HALF, blk), whole(ROT_HALF, blk),
        ],
        out_specs=[tile, tile, tile, pair(blk + 16), pair(blk)],
        out_shape=[
            flat, flat, flat,
            jax.ShapeDtypeStruct((rows, blk + 16, kvw), bf16),
            jax.ShapeDtypeStruct((rows, blk, kvw), bf16),
        ],
        compiler_params=params(60),
        cost_estimate=cost(2 * tok * width * kvw, 10 * tok * width),
        name="norms",
    )(x, cot, seg, pack, kw, cos, sin)


def gelu_parts(hidden):
    size = jnp.abs(hidden)
    t = pltpu.reciprocal(1.0 + (0.3275911 * 0.5**0.5) * size, approx=True)
    bell = jnp.exp2(hidden * hidden * (-0.5 * LOG2E))
    tail = t * (0.127414796 + t * (-0.142248368 + t * (0.7107068705 + t * (-0.7265760135 + t * 0.5307027145))))
    tail = tail * bell
    share = jnp.where(hidden >= 0.0, 1.0 - tail, tail)
    return share, bell * 0.3989422804014327


def towards(axis, target):
    return dict(device_id={axis: target}, device_id_type=pl.DeviceIdType.MESH)


def send(src, dst, sems, at, axis, target):
    return pltpu.make_async_remote_copy(
        src_ref=src, dst_ref=dst, send_sem=sems.at[0, at], recv_sem=sems.at[1, at],
        **towards(axis, target),
    )


def greet(planes):
    seq, batch = lax.axis_index("seq"), lax.axis_index("batch")
    barrier = pltpu.get_barrier_semaphore()
    column = [lax.rem(seq + 2 * hop, 2 * planes) for hop in range(1, planes)]
    for other in column + [seq + 1 - 2 * lax.rem(seq, 2)]:
        pl.semaphore_signal(barrier, inc=1, **towards("seq", other))
    for other in (batch + 1 - 2 * lax.rem(batch, 2), lax.rem(batch + 2, 4)):
        pl.semaphore_signal(barrier, inc=1, **towards("batch", other))
    pl.semaphore_wait(barrier, planes + 2)


def dense_kernel(
    di_ref, bg_ref, up_ref, down_ref, normed_ref, pack, qw_ref, ow_ref, cos_ref, sin_ref,
    kv_ref, act_ref, gh_ref, red_ref, gub_ref, q_ref, do_ref, kvs_ref,
    hid0, hid1, gac0, gac1, act0, act1, gh0, gh1, acc_up, acc_dn, acc_ub,
    cut_up, cut_dn, core_up, core_dn, half_up, half_dn, x_up, x_dn,
    own_sem, z_sem, y_sem, core_sem, x_sem,
    *, pairs, steps, tile, parts, owners,
):
    i = pl.program_id(0)
    planes = owners // 2
    seq, batch = lax.axis_index("seq"), lax.axis_index("batch")
    plane, side = seq // 2, lax.rem(seq, 2)
    x_at, core_at = batch // 2, lax.rem(batch, 2)
    x_other, core_other = lax.rem(batch + 2, 4), batch + 1 - 2 * core_at
    y_other = seq + 1 - 2 * side

    def own_copy():
        return pltpu.make_async_copy(kv_ref, kvs_ref.at[seq], own_sem)

    def hop_copy(hop):
        block = kv_ref if hop == 0 else kvs_ref.at[seq - 2 * hop]
        return send(block, kvs_ref.at[seq - 2 * hop], z_sem, hop, "seq", seq + 2)

    def across_copy(hop):
        block = kv_ref if hop == 0 else kvs_ref.at[seq - 2 * hop]
        return send(block, kvs_ref.at[seq - 2 * hop], y_sem, hop, "seq", y_other)

    def spread(hop):
        @pl.when(plane >= hop)
        def _():
            if hop > 0:
                arrived(hop)
            across_copy(hop).start()

            @pl.when(plane < planes - 1)
            def _():
                hop_copy(hop).start()

    def arrived(hop):
        block = kvs_ref.at[seq - 2 * hop]
        send(block, block, z_sem, hop - 1, "seq", y_other).wait_recv()

    def settle(hop):
        @pl.when(plane >= hop)
        def _():
            across_copy(hop).wait_send()
            block = kvs_ref.at[y_other - 2 * hop]
            send(block, block, y_sem, hop, "seq", y_other).wait_recv()

            @pl.when(plane < planes - 1)
            def _():
                hop_copy(hop).wait_send()

    def core_copies(c):
        return [
            send(cut_up.at[1 - core_at], core_up.at[c], core_sem, 2 * c, "batch", core_other),
            send(cut_dn.at[1 - core_at], core_dn.at[c], core_sem, 2 * c + 1, "batch", core_other),
        ]

    def x_copies(c):
        return [
            send(half_up.at[c % 2, 1 - x_at], x_up.at[c], x_sem, 2 * c, "batch", x_other),
            send(half_dn.at[c % 2, 1 - x_at], x_dn.at[c], x_sem, 2 * c + 1, "batch", x_other),
        ]

    def plus(first, second):
        return (first.astype(f32) + second.astype(f32)).astype(bf16)

    def cut(c):
        rows, cols = cut_up.shape[3], cut_up.shape[4]
        for core in range(2):
            for x in range(2):
                for o in range(owners):
                    at = (2 * o + core) * rows
                    cut_up[core, x, o] = acc_up[at : at + rows, x * cols : (x + 1) * cols].astype(bf16)
                tall = cut_dn.shape[3]
                for o in range(cut_dn.shape[2]):
                    at = (2 * o + core) * tall
                    cut_dn[core, x, o] = acc_dn[at : at + tall, x * cols : (x + 1) * cols].astype(bf16)
        for copy in core_copies(c):
            copy.start()

    def halve(c):
        for copy in core_copies(c):
            copy.wait()
        for x in range(2):
            half_up[c % 2, x] = plus(cut_up[core_at, x], core_up[c, x])
            half_dn[c % 2, x] = plus(cut_dn[core_at, x], core_dn[c, x])
        for copy in x_copies(c):
            copy.start()

    def fold(c):
        for copy in x_copies(c):
            copy.wait()
        rows = cut_up.shape[3]
        few = cut_dn.shape[2]
        red_ref[:, c * rows : (c + 1) * rows, :] = plus(half_up[c % 2, x_at], x_up[c])
        red_ref[c * few : (c + 1) * few, parts * rows :, :] = plus(half_dn[c % 2, x_at], x_dn[c])

    def rows_of(step, odd):
        return pl.ds(pl.multiple_of((lax.rem(step, pairs) * 2 + odd) * tile, tile), tile)

    def enter(odd, hid, gac):
        rows = rows_of(i, odd)
        hid[...] = nn(di_ref[rows, :], up_ref[...]) + pack[pl.ds(UB + i // pairs, 1), :]
        gac[...] = nt(bg_ref[rows, :], down_ref[...])

    def bend(odd, hid, gac, act_s, gh_s):
        hidden = hid[...]
        share, bell = gelu_parts(hidden)
        act = (hidden * share).astype(bf16)
        grad = (gac[...] * (share + hidden * bell)).astype(bf16)
        act_s[...] = act
        gh_s[...] = grad
        at = (1 - odd) * tile
        act_ref[at : at + tile, :] = act
        gh_ref[at : at + tile, :] = grad

    def gather(odd, act_s, gh_s, fresh=False):
        rows = rows_of(i - 1, odd)
        grad = gh_s[...]
        up, dn = tn(di_ref[rows, :], grad), tn(act_s[...], bg_ref[rows, :])
        ub = jnp.sum(grad.astype(f32), axis=0, keepdims=True)
        if fresh:
            acc_up[...], acc_dn[...], acc_ub[...] = up, dn, ub
        else:
            acc_up[...] += up
            acc_dn[...] += dn
            acc_ub[...] += ub

    def heads(step):
        count, _, wide = q_ref.shape
        blk = wide // HEADS
        cos, sin = cos_ref[...], sin_ref[...]
        for n in range(count):
            rows = pl.ds(pl.multiple_of((step * count + n) * blk, blk), blk)
            queries = (nn(normed_ref[n * blk : (n + 1) * blk, :], qw_ref[...]) + vector(pack, QB)).T
            upstream = nt(ow_ref[...], bg_ref[rows, :])
            for h in range(HEADS):
                part = slice(h * HEAD_DIM, (h + 1) * HEAD_DIM)
                lanes = slice(h * blk, (h + 1) * blk)
                q_ref[n, :, lanes] = (turn(queries[part], cos, sin) * HEAD_DIM**-0.5).astype(bf16)
                do_ref[n, :, lanes] = upstream[part].astype(bf16)

    @pl.when(i == 0)
    def _():
        greet(planes)
        own_copy().start()

    @pl.when(i == 0)
    def _():
        enter(0, hid0, gac0)
        enter(1, hid1, gac1)
        bend(0, hid0, gac0, act0, gh0)

    def body(fresh):
        enter(0, hid0, gac0)
        bend(1, hid1, gac1, act1, gh1)
        gather(0, act0, gh0, fresh)
        enter(1, hid1, gac1)
        bend(0, hid0, gac0, act0, gh0)
        gather(1, act1, gh1)

    @pl.when((i > 0) & (i < steps) & (lax.rem(i - 1, pairs) == 0))
    def _():
        body(True)

    @pl.when((i > 0) & (i < steps) & (lax.rem(i - 1, pairs) > 0))
    def _():
        body(False)

    @pl.when(i == steps)
    def _():
        bend(1, hid1, gac1, act1, gh1)
        gather(0, act0, gh0)
        gather(1, act1, gh1)

    for c in range(parts):
        @pl.when(i == (c + 1) * pairs)
        def _():
            gub_ref[c] = acc_ub[...]
            cut(c)
            if c > 1:
                fold(c - 2)

        if c < parts - 1:
            @pl.when(i == (c + 1) * pairs + 1)
            def _():
                halve(c)

    for hop in range(planes):
        @pl.when(i == hop * pairs)
        def _():
            spread(hop)

    @pl.when(i > steps)
    def _():
        heads(i - steps - 1)

    @pl.when(i == steps + 1)
    def _():
        halve(parts - 1)
        fold(parts - 2)

    @pl.when(i == pl.num_programs(0) - 1)
    def _():
        own_copy().wait()
        for hop in range(planes):
            settle(hop)
        fold(parts - 1)


def dense(di, bg, up, down, normed, pack, qw, ow, cos, sin, kv, parts, owners, tile=512):
    tok, width = di.shape
    ff = up.shape[1]
    chunk = ff // parts
    pairs = tok // tile // 2
    steps = pairs * parts
    high, low, cols = width // owners // 2, chunk // (owners // parts) // 2, chunk // 2
    few = owners // parts
    rows, blk = kv.shape[0], cos.shape[1]
    group = tile // blk
    late = lambda i: jnp.clip(i - steps - 1, 0, rows // group - 1)
    at = lambda i: jnp.clip(i, 0, steps - 1)
    anywhere = pl.BlockSpec(memory_space=pl.ANY)
    once = lambda *shape: pl.BlockSpec(
        shape, lambda *_: (0,) * len(shape), pipeline_mode=pl.Buffered(1)
    )
    dma = pltpu.SemaphoreType.DMA
    return pl.pallas_call(
        partial(
            dense_kernel, pairs=pairs, steps=steps, tile=tile, parts=parts, owners=owners
        ),
        grid=(steps + 1 + rows // group,),
        in_specs=[
            once(tok, width),
            once(tok, width),
            pl.BlockSpec((width, chunk), lambda i: (0, at(i) // pairs)),
            pl.BlockSpec((chunk, width), lambda i: (at(i) // pairs, 0)),
            pl.BlockSpec((tile, width), lambda i: (late(i), 0)),
            once(*pack.shape), once(width, width), once(width, width),
            once(ROT_HALF, blk), once(ROT_HALF, blk),
            anywhere,
        ],
        out_specs=[
            pl.BlockSpec((2 * tile, chunk), lambda i: (jnp.minimum(i, steps), 0)),
            pl.BlockSpec((2 * tile, chunk), lambda i: (jnp.minimum(i, steps), 0)),
            once(owners, parts * high + low, cols),
            once(parts, 1, chunk),
            pl.BlockSpec((group, HEAD_DIM, HEADS * blk), lambda i: (late(i), 0, 0)),
            pl.BlockSpec((group, HEAD_DIM, HEADS * blk), lambda i: (late(i), 0, 0)),
            anywhere,
        ],
        out_shape=[
            jax.ShapeDtypeStruct((2 * tile * (steps + 1), chunk), bf16),
            jax.ShapeDtypeStruct((2 * tile * (steps + 1), chunk), bf16),
            jax.ShapeDtypeStruct((owners, parts * high + low, cols), bf16),
            jax.ShapeDtypeStruct((parts, 1, chunk), f32),
            jax.ShapeDtypeStruct((rows, HEAD_DIM, HEADS * blk), bf16),
            jax.ShapeDtypeStruct((rows, HEAD_DIM, HEADS * blk), bf16),
            jax.ShapeDtypeStruct((owners,) + kv.shape, bf16),
        ],
        scratch_shapes=[pltpu.VMEM((tile, chunk), f32)] * 4
        + [pltpu.VMEM((tile, chunk), bf16)] * 4
        + [
            pltpu.VMEM((width, chunk), f32), pltpu.VMEM((chunk, width), f32),
            pltpu.VMEM((1, chunk), f32),
            pltpu.VMEM((2, 2, owners, high, cols), bf16), pltpu.VMEM((2, 2, few, low, cols), bf16),
            pltpu.VMEM((parts, 2, owners, high, cols), bf16),
            pltpu.VMEM((parts, 2, few, low, cols), bf16),
            pltpu.VMEM((2, 2, owners, high, cols), bf16), pltpu.VMEM((2, 2, few, low, cols), bf16),
            pltpu.VMEM((parts, owners, high, cols), bf16),
            pltpu.VMEM((parts, few, low, cols), bf16),
            dma, dma((2, owners // 2)), dma((2, owners // 2)), dma((2, 2 * parts)),
            dma((2, 2 * parts)),
        ],
        compiler_params=params(63, collective_id=0, has_side_effects=True),
        cost_estimate=cost(8 * tok * width * ff, 8 * tok * width + 4 * tok * ff),
        name="dense",
    )(di, bg, up, down, normed, pack, qw, ow, cos, sin, kv)


DESCEND, PROJECT, CLOSE = (0, 1, 6, 7), (2, 3, 4, 5), (8, 9, 12, 15)
FINISH, BACK = (10, 11, 13, 14), (16, 17, 18, 19)


def stair(*groups):
    jumps = sorted((step, n) for group in groups for n, step in enumerate(group))

    def of(i):
        value = jumps[0][1]
        for (_, before), (step, after) in zip(jumps, jumps[1:]):
            if after != before:
                value = value + jnp.where(i >= step, after - before, 0)
        return value

    return of


def tail_kernel(
    x_ref, cot_ref, seg_ref, att_ref, gq_ref, bg_ref, normed_ref, kcot_ref, first_ref,
    first_across_ref, second_ref, second_across_ref, gub_ref,
    mlp_ref, ow_hbm, down_hbm, up_hbm, qw_hbm, pack, kw_ref, cos_ref, sin_ref, *refs, rows, parts, owners,
):
    acts, ghs, refs = refs[:parts], refs[parts : 2 * parts], refs[2 * parts :]
    (
        out_ref, gt_ref, gow_ref, gqw_ref, guw_ref, gdw_ref, keyval_ref, vector_ref,
        ow_ref, down_ref, up_ref, qw_ref, acc, gd_s, gk_s, vec_s,
        own, across, below, total, stage, mlp_in,
        cut, core_in, x_in, piece, piece_in, part_in,
        small_k, small_v, seq_k, seq_v, mid_k, mid_v, batch_k, batch_v,
        load_sem, stage_sem, own_sem, first_sem, y_sem, z_sem, mlp_sem, core_sem, x_sem, piece_sem, part_sem,
        sk_sem, sv_sem, bk_sem, bv_sem,
    ) = refs
    i = pl.program_id(0)
    planes = owners // 2
    some = rows // 2
    seq, batch = lax.axis_index("seq"), lax.axis_index("batch")
    plane, side = seq // 2, lax.rem(seq, 2)
    x_at, core_at = batch // 2, lax.rem(batch, 2)
    x_other, core_other = lax.rem(batch + 2, 4), batch + 1 - 2 * core_at
    y_other = seq + 1 - 2 * side
    high, cols = cut.shape[3], cut.shape[4]
    seq_at = lambda hop: lax.rem(seq + hop, owners)
    batch_at = lambda hop: lax.rem(batch + hop, parts)

    def enter():
        barrier = pltpu.get_barrier_semaphore()
        for hop in range(1, owners):
            pl.semaphore_signal(barrier, inc=1, **towards("seq", seq_at(hop)))
        for hop in range(1, parts):
            pl.semaphore_signal(barrier, inc=1, **towards("batch", batch_at(hop)))
        pl.semaphore_wait(barrier, owners + parts - 2)

    pairs = ((up_hbm, up_ref), (ow_hbm, ow_ref), (down_hbm, down_ref), (qw_hbm, qw_ref))

    def load(n):
        return pltpu.make_async_copy(pairs[n][0], pairs[n][1], load_sem.at[n])

    def rows_of(part):
        return pl.ds(part * some, some)

    def own_copy(k, part):
        source = second_ref.at[k] if part else first_ref.at[k]
        return pltpu.make_async_copy(source, own.at[k, rows_of(part)], own_sem.at[2 * k + part])

    def first_copy(k):
        return pltpu.make_async_copy(first_across_ref.at[k], across.at[k, rows_of(0)], first_sem.at[k])

    def across_copy(k):
        return send(second_across_ref.at[k], across.at[k, rows_of(1)], y_sem, k, "seq", y_other)

    def below_copy(k, part):
        return send(
            own.at[k, rows_of(part)], below.at[k, rows_of(part)], z_sem, 2 * k + part, "seq",
            lax.rem(seq + owners - 2, owners),
        )

    def start_local(k):
        @pl.when(plane >= k)
        def _():
            own_copy(k, 0).start()
            first_copy(k).start()
            own_copy(k, 1).start()

    def start_across(k):
        @pl.when(plane >= k)
        def _():
            across_copy(k).start()

    def tick(step, part):
        k = step - (planes - 1 - plane)
        rows_at = slice(part * some, (part + 1) * some)

        @pl.when(k >= 0)
        def _():
            own_copy(k, part).wait()
            if part:
                across_copy(k).wait_recv()
            else:
                first_copy(k).wait()
            total[rows_at] = own[k, rows_at].astype(f32) + across[k, rows_at].astype(f32)

            @pl.when(plane < planes - 1)
            def _():
                below_copy(k, part).wait_recv()
                total[rows_at] += below[k, rows_at].astype(f32)

            if step < planes - 1:
                own[k, rows_at] = total[rows_at].astype(bf16)
                below_copy(k, part).start()

    def settle():
        for k in range(planes):
            @pl.when(plane >= k)
            def _():
                across_copy(k).wait_send()

            for part in range(2):
                @pl.when(plane > k)
                def _():
                    below_copy(k, part).wait_send()

    def mlp_copy(hop):
        return send(mlp_ref, mlp_in.at[batch], mlp_sem, hop - 1, "batch", batch_at(hop))

    def write_out(fills):
        copies = []
        for n, (fill, out) in enumerate(fills):
            if n >= 2:
                copies[n - 2].wait()
            fill(stage.at[n % 2])
            copies.append(pltpu.make_async_copy(stage.at[n % 2], out, stage_sem.at[n % 2]))
            copies[n].start()
        for copy in copies[-2:]:
            copy.wait()

    def collect_mlp():
        for hop in range(1, parts):
            mlp_copy(hop).wait()
        tall = mlp_ref.shape[0] - parts * high
        few = tall // (2 * high)

        def fill_up(c):
            def fill(ref):
                for b in range(parts):
                    core, x = b % 2, b // 2
                    ref[core * high : (core + 1) * high, x * cols : (x + 1) * cols] = mlp_in[
                        b, c * high : (c + 1) * high, :
                    ].astype(f32)

            return fill

        def fill_down(core, n):
            def fill(ref):
                at = parts * high + n * 2 * high
                for x in range(2):
                    ref[:, x * cols : (x + 1) * cols] = mlp_in[
                        2 * x + core, at : at + 2 * high, :
                    ].astype(f32)

            return fill

        fills = [
            (fill_up(c), guw_ref.at[:, pl.ds(c * 2 * cols, 2 * cols)]) for c in range(parts)
        ]
        for core in range(2):
            for n in range(few):
                at = core * tall + n * 2 * high
                fills.append((fill_down(core, n), gdw_ref.at[pl.ds(at, 2 * high), :]))
        write_out(fills)

    def core_copy():
        return send(cut, core_in, core_sem, 0, "batch", core_other)

    def x_copy():
        return send(cut.at[1 - x_at], x_in, x_sem, 0, "batch", x_other)

    def piece_copy(hop):
        target = seq_at(hop)
        return send(piece.at[target], piece_in.at[hop - 1], piece_sem, hop - 1, "seq", target)

    def part_copy(hop):
        return send(part_in.at[batch], part_in.at[batch], part_sem, hop - 1, "batch", batch_at(hop))

    def share_of(core, m, x, o):
        rows_at = pl.ds(pl.multiple_of((2 * o + core) * high, high), high)
        return acc[m, rows_at, x * cols : (x + 1) * cols]

    def cut_square():
        for m in range(2):
            for x in range(2):
                for o in range(owners):
                    cut[x, o, m] = share_of(1 - core_at, m, x, o).astype(bf16)
        core_copy().start()

    def halve_square():
        core_copy().wait()
        for m in range(2):
            for x in range(2):
                for o in range(owners):
                    value = share_of(core_at, m, x, o) + core_in[x, o, m].astype(f32)
                    cut[x, o, m] = value.astype(bf16)
        x_copy().start()

    def spread_square():
        x_copy().wait()
        piece[...] = (cut[x_at].astype(f32) + x_in[...].astype(f32)).astype(bf16)
        for hop in range(1, owners):
            piece_copy(hop).start()

    def sum_square():
        value = piece[seq].astype(f32)
        for hop in range(1, owners):
            piece_copy(hop).wait()
            value = value + piece_in[hop - 1].astype(f32)
        part_in[batch] = value.astype(bf16)
        for hop in range(1, parts):
            part_copy(hop).start()

    def collect_square():
        for hop in range(1, parts):
            part_copy(hop).wait()

        def fill_square(m):
            def fill(ref):
                for b in range(parts):
                    core, x = b % 2, b // 2
                    ref[core * high : (core + 1) * high, x * cols : (x + 1) * cols] = part_in[
                        b, m
                    ].astype(f32)

            return fill

        write_out([(fill_square(0), gow_ref), (fill_square(1), gqw_ref)])

    def seq_copies(hop):
        target = seq_at(hop)
        return [
            send(small_k.at[target], seq_k.at[hop - 1], sk_sem, hop - 1, "seq", target),
            send(small_v, seq_v.at[hop - 1], sv_sem, hop - 1, "seq", target),
        ]

    def batch_copies(hop):
        target = batch_at(hop)
        return [
            send(mid_k, batch_k.at[hop - 1], bk_sem, hop - 1, "batch", target),
            send(mid_v, batch_v.at[hop - 1], bv_sem, hop - 1, "batch", target),
        ]

    def start_small():
        tall = small_k.shape[1]
        keyval = gk_s[...].T
        for o in range(owners):
            small_k[o] = keyval[o * tall : (o + 1) * tall].astype(bf16)
        small_v[...] = vec_s[...].astype(bf16)
        for hop in range(1, owners):
            for copy in seq_copies(hop):
                copy.start()

    def turn_small():
        value, vector = small_k[seq].astype(f32), small_v[...].astype(f32)
        for hop in range(1, owners):
            for copy in seq_copies(hop):
                copy.wait()
            value = value + seq_k[hop - 1].astype(f32)
            vector = vector + seq_v[hop - 1].astype(f32)
        mid_k[...] = value.astype(bf16)
        mid_v[...] = vector.astype(bf16)
        for hop in range(1, parts):
            for copy in batch_copies(hop):
                copy.start()

    def end_small():
        value, vector = mid_k[...].astype(f32), mid_v[...].astype(f32)
        for hop in range(1, parts):
            for copy in batch_copies(hop):
                copy.wait()
            value = value + batch_k[hop - 1].astype(f32)
            vector = vector + batch_v[hop - 1].astype(f32)
        keyval_ref[...] = value
        vector_ref[...] = vector

    count, blk = kcot_ref.shape[0], kcot_ref.shape[1]
    side_by_side = lambda ref: jnp.concatenate([ref[n] for n in range(count)], axis=1)
    ones = jnp.ones((8, count * blk), bf16)

    def project():
        branch, grad = bg_ref[...], side_by_side(gq_ref)
        acc[0] += nn(side_by_side(att_ref), branch)
        acc[1] += tt(normed_ref[...], grad)
        vec_s[0:1] += nt(ones, grad)[0:1]
        vec_s[1:2] += nn(ones, branch)[0:1]

    def close(step):
        act = jnp.concatenate([ref[...] for ref in acts], axis=1)
        branch = tn(side_by_side(att_ref), ow_ref[...]) + vector(pack, OB)
        branch = branch + (nn(act, down_ref[...]) + vector(pack, DB))
        for n in range(count):
            rows_at = slice(n * blk, (n + 1) * blk)
            ids = seg_ref[pl.ds(step * count + n, 1), :]
            part = jnp.where(alive(ids), branch[rows_at], 0.0)
            out_ref[rows_at] = (x_ref[rows_at].astype(f32) + part).astype(bf16)

    def descend(step):
        grad = jnp.concatenate([ref[...] for ref in ghs], axis=1)
        second = nt(grad, up_ref[...])
        unit, _ = standardize(x_ref[...].astype(f32))
        vec_s[4:5] += jnp.sum(second * unit, axis=0, keepdims=True)
        vec_s[5:6] += jnp.sum(second, axis=0, keepdims=True)
        gd_s[step] = second * vector(pack, DG)

    def finish(step):
        unit, _ = standardize(x_ref[...].astype(f32))
        normed = (unit * vector(pack, AG) + vector(pack, AS)).astype(bf16)
        keyval = []
        for n in range(count):
            value = (total[step * count + n] + kcot_ref[n].astype(f32)).T
            keyval.append(turn_back(value, cos_ref[...], sin_ref[...]).astype(bf16))
        keyval = jnp.concatenate(keyval, axis=1)
        gk_s[...] += nn(keyval, normed)
        vec_s[6:7, 0 : keyval.shape[0]] += nt(ones, keyval)[0:1]
        first = tt(side_by_side(gq_ref), qw_ref[...]) + tt(keyval, kw_ref[...])
        vec_s[2:3] += jnp.sum(first * unit, axis=0, keepdims=True)
        vec_s[3:4] += jnp.sum(first, axis=0, keepdims=True)
        gd_s[step] += first * vector(pack, AG)

    def back(step):
        unit, spread = standardize(x_ref[...].astype(f32))
        both = gd_s[step]
        middle = jnp.mean(both, axis=-1, keepdims=True)
        along = jnp.mean(both * unit, axis=-1, keepdims=True)
        gt_ref[...] = (cot_ref[...].astype(f32) + (both - middle - unit * along) * spread).astype(bf16)

    def at(step):
        return pl.when(i == step)

    def when(*steps):
        hit = i == steps[0]
        for step in steps[1:]:
            hit = hit | (i == step)
        return pl.when(hit)

    def ticks(*marks):
        for mark, step, part in marks:
            @at(mark)
            def _():
                tick(step, part)

    @at(0)
    def _():
        for n in range(len(pairs)):
            load(n).start()
        enter()
        start_across(0)
        for k in range(planes):
            start_local(k)
        for hop in range(1, parts):
            mlp_copy(hop).start()
        mlp_in[batch] = mlp_ref[...]
        acc[...] = jnp.zeros(acc.shape, f32)
        gk_s[...] = jnp.zeros(gk_s.shape, f32)
        vec_s[...] = jnp.zeros(vec_s.shape, f32)
        for c in range(parts):
            vec_s[8 + c : 9 + c] = gub_ref[c]
        load(0).wait()

    for mark, k in ((2, 1), (7, 2), (9, 3)):
        @at(mark)
        def _():
            start_across(k)

    ticks(
        (0, 0, 0), (2, 1, 0), (6, 2, 0), (6, 0, 1), (8, 3, 0), (8, 1, 1), (10, 2, 1), (13, 3, 1),
    )

    @at(7)
    def _():
        halve_square()

    @at(8)
    def _():
        for n in range(1, len(pairs)):
            load(n).wait()

    @at(12)
    def _():
        spread_square()
        collect_mlp()

    @at(15)
    def _():
        start_small()

    @at(16)
    def _():
        turn_small()
        sum_square()

    @when(*DESCEND)
    def _():
        descend(jnp.where(i < 2, i, i - 4))

    @when(*PROJECT)
    def _():
        project()

    @at(PROJECT[-1])
    def _():
        cut_square()

    @when(*CLOSE)
    def _():
        close(jnp.where(i < 10, i - 8, jnp.where(i < 14, 2, 3)))

    @when(*FINISH)
    def _():
        finish(jnp.where(i < 12, i - 10, i - 11))

    @when(*BACK)
    def _():
        back(i - BACK[0])

    @at(BACK[-1])
    def _():
        settle()
        end_small()
        collect_square()


def tail(
    x, cot, seg, att, gq, bg, normed, kcot, first, first_across, second, second_across, gub, mlp, ow,
    down, up, qw, pack, kw, cos, sin, act, gh, parts, owners, count=2,
):
    rows, width, blk = att.shape
    tok, ff, kvw = rows * blk, up.shape[1], kw.shape[1]
    tiles = tok // (count * blk)
    planes = owners // 2
    high, cols, tall = width // owners // 2, width // 2, width // owners
    once = lambda *shape: pl.BlockSpec(
        shape, lambda i: (0,) * len(shape), pipeline_mode=pl.Buffered(1)
    )
    anywhere = pl.BlockSpec(memory_space=pl.ANY)
    s = rows // count
    one, descent, third, last = stair(PROJECT), stair(DESCEND), stair(FINISH), stair(BACK)
    closing, every = stair(CLOSE), stair(DESCEND, CLOSE, FINISH, BACK)
    heads, queries = stair(PROJECT, CLOSE), stair(PROJECT, FINISH)
    flat = lambda of: pl.BlockSpec((count * blk, width), lambda i: (of(i), 0))
    single = pl.BlockSpec(
        (count * blk, width), lambda i: (last(i), 0), pipeline_mode=pl.Buffered(1)
    )
    stack = lambda of, h, w: pl.BlockSpec((count, h, w), lambda i: (of(i), 0, 0))
    wide = lambda of: [
        pl.BlockSpec((count * blk, ff // parts), lambda i, c=c: (c * tiles + of(i) + 1, 0))
        for c in range(parts)
    ]
    dma = pltpu.SemaphoreType.DMA
    vmem = lambda kind, *shape: pltpu.VMEM(shape, kind)
    return pl.pallas_call(
        partial(tail_kernel, rows=rows, parts=parts, owners=owners),
        grid=(BACK[-1] + 1,),
        in_specs=[
            flat(every), single, once(rows, blk), stack(heads, width, blk),
            stack(queries, width, blk), flat(one), flat(one), stack(third, blk, kvw), anywhere,
            anywhere, anywhere, anywhere, once(parts, 1, ff // parts), once(*mlp.shape), anywhere,
            anywhere, anywhere, anywhere, once(*pack.shape), once(width, kvw), once(ROT_HALF, blk),
            once(ROT_HALF, blk),
        ] + wide(closing) + wide(descent),
        out_specs=[
            flat(closing), single, anywhere, anywhere, anywhere, anywhere, once(tall, kvw),
            once(16, width),
        ],
        out_shape=[
            jax.ShapeDtypeStruct((tok, width), bf16),
            jax.ShapeDtypeStruct((tok, width), bf16),
            jax.ShapeDtypeStruct((tall, width), f32),
            jax.ShapeDtypeStruct((tall, width), f32),
            jax.ShapeDtypeStruct((tall, ff), f32),
            jax.ShapeDtypeStruct((ff // owners, width), f32),
            jax.ShapeDtypeStruct((tall, kvw), f32),
            jax.ShapeDtypeStruct((16, width), f32),
        ],
        scratch_shapes=[
            vmem(bf16, width, width), vmem(bf16, ff, width), vmem(bf16, width, ff),
            vmem(bf16, width, width),
            vmem(f32, 2, width, width), vmem(f32, s, count * blk, width),
            vmem(f32, kvw, width), vmem(f32, 16, width),
            vmem(bf16, planes, rows, blk, kvw), vmem(bf16, planes, rows, blk, kvw),
            vmem(bf16, planes - 1, rows, blk, kvw), vmem(f32, rows, blk, kvw),
            vmem(f32, 2, tall, width), vmem(bf16, parts, *mlp.shape),
            vmem(bf16, 2, owners, 2, high, cols), vmem(bf16, 2, owners, 2, high, cols),
            vmem(bf16, owners, 2, high, cols),
            vmem(bf16, owners, 2, high, cols), vmem(bf16, owners - 1, 2, high, cols),
            vmem(bf16, parts, 2, high, cols),
            vmem(bf16, owners, tall, kvw), vmem(bf16, 16, width),
            vmem(bf16, owners - 1, tall, kvw), vmem(bf16, owners - 1, 16, width),
            vmem(bf16, tall, kvw), vmem(bf16, 16, width),
            vmem(bf16, parts - 1, tall, kvw), vmem(bf16, parts - 1, 16, width),
            dma((4,)), dma((2,)), dma((2 * planes,)), dma((planes,)), dma((2, planes)), dma((2, 2 * planes)),
            dma((2, parts - 1)), dma((2, 1)), dma((2, 1)),
            dma((2, owners - 1)), dma((2, parts - 1)), dma((2, owners - 1)), dma((2, owners - 1)),
            dma((2, parts - 1)), dma((2, parts - 1)),
        ],
        compiler_params=params(63, collective_id=1, has_side_effects=True),
        cost_estimate=cost(4 * tok * width * (2 * width + ff), 4 * tok * ff + 20 * tok * width),
        name="tail",
    )(
        x, cot, seg, att, gq, bg, normed, kcot, first, first_across, second, second_across, gub, mlp,
        ow, down, up, qw, pack, kw, cos, sin, *[act] * parts, *[gh] * parts,
    )


def attn_kernel(first_ref, sidx_ref, q_ref, do_ref, kv_ref, start_ref,
                cos_ref, sin_ref, *refs, blk, nblk, begin):
    att_ref, gq_ref, own_ref, other_ref, p_s, m_s, bias_s, o_s, mx, ls, dq_s, dc_s, ic_s, inn_s = refs[-14:]
    r = begin + pl.program_id(0)
    e = sidx_ref[0]
    n = e - first_ref[r] + 1
    start = start_ref[pl.ds(r, 1), :]
    qpos = e*blk + lax.broadcasted_iota(jnp.int32,(1,blk),1)
    krow = lax.broadcasted_iota(jnp.int32,(blk,blk),0)

    def hsl(h):
        return slice(h*blk,(h+1)*blk)

    def put(j, block):
        @pl.when(lax.rem(j + e, 2) == 0)
        def _():
            own_ref[j // 2, 0] = block

        @pl.when(lax.rem(j + e, 2) == 1)
        def _():
            other_ref[j // 2, 0] = block

    @pl.loop(0, nblk)
    def _(j):
        @pl.when((j < first_ref[r]) | (j > e))
        def _():
            put(j, jnp.zeros((blk,2*HEAD_DIM),bf16))

    def forward(jj, diagonal):
        j = e - jj
        kvj = kv_ref[j, 0, 0:blk, :]
        key = kvj[:, :HEAD_DIM]
        vt = kvj.T[HEAD_DIM:,:]
        kpos = j*blk + krow
        bias_s[...] = jnp.where((kpos>=start)&(kpos<=qpos), 0.0, negative)
        sv = {}; pv = {}; av = {}
        for h in range(HEADS+3):
            if h < HEADS:
                sv[h] = nn(key, q_ref[0,:,hsl(h)])
            g = h-2
            if 0 <= g < HEADS:
                hs = hsl(g)
                s = sv.pop(g)*LOG2E + bias_s[...]
                top = jnp.max(s,axis=0,keepdims=True)
                if diagonal:
                    mn = top
                    p = jnp.exp2(s-mn)
                    ls[:,hs] = jnp.sum(p,axis=0,keepdims=True)
                else:
                    mo = mx[:,hs]
                    mn = jnp.maximum(mo, top)
                    p = jnp.exp2(s-mn)
                    av[g] = jnp.exp2(mo-mn)
                    ls[:,hs] = ls[:,hs]*av[g] + jnp.sum(p,axis=0,keepdims=True)
                pv[g] = p.astype(bf16)
                p_s[jj,:,hs] = pv[g]
                m_s[jj,:,hs] = mn
                mx[:,hs] = mn
            g = h-3
            if 0 <= g < HEADS:
                hs = hsl(g)
                new = nn(vt,pv.pop(g))
                o_s[:,hs] = new if diagonal else o_s[:,hs]*av.pop(g) + new

    forward(0, True)

    @pl.loop(1, n)
    def _(jj):
        forward(jj, False)

    for h in range(HEADS):
        hs = hsl(h)
        inv = 1.0/ls[:,hs]
        ls[:,hs] = inv
        o = o_s[:,hs]*inv
        att_ref[0, h*HEAD_DIM:(h+1)*HEAD_DIM, :] = o.astype(bf16)
        inn_s[:,hs] = jnp.sum(o*do_ref[0,:,hs].astype(f32),axis=0,keepdims=True)

    def backward(jj, diagonal):
        j = e - jj
        kvj = kv_ref[j, 0, 0:blk, :]
        value = kvj[:, HEAD_DIM:]
        kt = kvj.T[:HEAD_DIM,:]
        for h in range(HEADS):
            hs = hsl(h)
            c = jnp.exp2(m_s[jj,:,hs]-mx[:,hs])*ls[:,hs]
            dc_s[:,hs] = (do_ref[0,:,hs].astype(f32)*c).astype(bf16)
            ic_s[:,hs] = inn_s[:,hs]*c
        dpv = {}; dsv = {}; pbv = {}
        dk = dv = None
        for h in range(HEADS+4):
            if h < HEADS:
                dpv[h] = nn(value, dc_s[:,hsl(h)])
            g = h-2
            if 0 <= g < HEADS:
                hs = hsl(g)
                pb = p_s[jj,:,hs]
                dsv[g] = (pb.astype(f32)*(dpv.pop(g)-ic_s[:,hs])).astype(bf16)
                new = nt(pb, dc_s[:,hs])
                dv = new if dv is None else dv + new
            g = h-4
            if 0 <= g < HEADS:
                hs = hsl(g)
                ds = dsv.pop(g)
                new = nn(kt, ds)
                dq_s[:,hs] = new if diagonal else dq_s[:,hs] + new
                new = nt(ds, q_ref[0,:,hs])
                dk = new if dk is None else dk + new
        put(j, jnp.concatenate([dk,dv],axis=1).astype(bf16))

    backward(0, True)

    @pl.loop(1, n)
    def _(jj):
        backward(jj, False)

    cos = cos_ref[...]; sin = sin_ref[...]
    for h in range(HEADS):
        g = dq_s[:, hsl(h)]*(HEAD_DIM**-0.5)
        a, b = g[0:8], g[8:16]
        gq_ref[0, h*HEAD_DIM:(h+1)*HEAD_DIM, :] = jnp.concatenate([a*cos+b*sin, b*cos-a*sin, g[16:]],axis=0).astype(bf16)


def attention(first, sidx, queries, upstream, kv, start, cos, sin, begin, count, before=()):
    rows, _, wide = queries.shape
    nblk, blk = kv.shape[0], wide // HEADS
    stack = lambda high, across: pl.BlockSpec((1, high, across), lambda r, *_: (begin + r, 0, 0))
    held = jax.ShapeDtypeStruct((rows, HEADS * HEAD_DIM, blk), bf16)
    specs = pltpu.PrefetchScalarGridSpec(
        num_scalar_prefetch=2,
        grid=(count,),
        in_specs=[
            stack(HEAD_DIM, wide), stack(HEAD_DIM, wide),
            pl.BlockSpec((nblk, 1, blk + 16, 2 * HEAD_DIM), lambda r, *_: (0, begin + r, 0, 0)),
            whole(rows, blk), whole(ROT_HALF, blk), whole(ROT_HALF, blk),
        ] + [pl.BlockSpec(memory_space=pl.ANY)] * len(before),
        out_specs=[
            stack(HEADS * HEAD_DIM, blk), stack(HEADS * HEAD_DIM, blk),
        ] + [pl.BlockSpec((nblk // 2, 1, blk, 2 * HEAD_DIM), lambda r, *_: (0, r, 0, 0))] * 2,
        scratch_shapes=[
            pltpu.VMEM((nblk, blk, wide), bf16), pltpu.VMEM((nblk, 1, wide), f32),
            pltpu.VMEM((blk, blk), f32), pltpu.VMEM((HEAD_DIM, wide), f32),
            pltpu.VMEM((1, wide), f32), pltpu.VMEM((1, wide), f32),
            pltpu.VMEM((HEAD_DIM, wide), f32), pltpu.VMEM((HEAD_DIM, wide), bf16),
            pltpu.VMEM((1, wide), f32), pltpu.VMEM((1, wide), f32),
        ],
    )
    return pl.pallas_call(
        partial(attn_kernel, blk=blk, nblk=nblk, begin=begin),
        out_shape=[held, held]
        + [jax.ShapeDtypeStruct((nblk // 2, count, blk, 2 * HEAD_DIM), bf16)] * 2,
        grid_spec=specs,
        input_output_aliases={8 + n: n for n in range(len(before))},
        compiler_params=params(60),
        cost_estimate=cost(6e9 * count, 5e6 * count),
        name="attention",
    )(first, sidx, queries, upstream, kv, start, cos, sin, *before)


def local(
    tokens,
    segment_ids,
    query_weight,
    query_bias,
    keyval_weight,
    keyval_bias,
    out_weight,
    out_bias,
    up_weight,
    up_bias,
    down_weight,
    down_bias,
    attention_gain,
    attention_shift,
    dense_gain,
    dense_shift,
    out_cotangent,
    keyval_cotangent,
):
    rows, blk, width = tokens.shape
    ff = up_weight.shape[1]
    kvw = 2 * HEAD_DIM
    tok = rows * blk
    owners, parts = lax.axis_size("seq"), lax.axis_size("batch")
    place = lax.axis_index("seq")
    cos, sin = rotary_tables(place * blk + jnp.arange(blk, dtype=jnp.int32))
    cos, sin = cos.T, sin.T
    x = tokens.reshape(tok, width)
    cot = out_cotangent.reshape(tok, width)
    lines = [
        attention_gain, attention_shift, dense_gain, dense_shift, query_bias, out_bias, down_bias,
        jnp.pad(keyval_bias, (0, width - kvw)),
    ] + [up_bias[at : at + width] for at in range(0, ff, width)]
    line = lax.broadcasted_iota(jnp.int32, (16, width), 0)
    pack = jnp.zeros((16, width), f32)
    for n, values in enumerate(lines):
        pack = jnp.where(line == n, values[None, :], pack)

    normed, dense_in, branch_grad, keyval, keyval_out = norms(
        x, cot, segment_ids, pack, keyval_weight, cos, sin
    )
    act, grad_hidden, mlp, gub, queries, grad_attended, keyval_all = dense(
        dense_in, branch_grad, up_weight, down_weight, normed, pack, query_weight, out_weight, cos,
        sin, keyval, parts, owners,
    )
    mlp = lax.psum_scatter(mlp, "seq", scatter_dimension=0)

    ids = keyval_all[:, :, blk : blk + blk // 128, :].reshape(owners, rows, blk).astype(f32)
    before = (jnp.arange(owners) <= place)[:, None, None]
    order = lambda values: jnp.where(values < 0, 1024.0, values)
    ids = jnp.where(before, order(ids), 2048.0)
    start = jnp.sum(
        (ids[:, :, None, :] < order(segment_ids.astype(f32))[None, :, :, None]).astype(jnp.int32),
        axis=(0, 3),
    ).astype(jnp.int32)
    first_block = start[:, 0] // blk
    index = place.astype(jnp.int32)[None]
    run = partial(
        attention, first_block, index, queries, grad_attended, keyval_all, start, cos, sin,
        count=rows // 2,
    )
    attended, grad_query, first, first_other = run(begin=0)
    across = lax.ppermute(first_other, "seq", [(i, i ^ 1) for i in range(owners)])
    attended, grad_query, own, other = run(begin=rows // 2, before=(attended, grad_query))
    (
        layer_out, grad_tokens, grad_out_weight, grad_query_weight, grad_up_weight,
        grad_down_weight, grad_keyval_weight, vectors,
    ) = tail(
        x, cot, segment_ids, attended, grad_query, branch_grad, normed, keyval_cotangent,
        first, across, own, other, gub, mlp, out_weight, down_weight, up_weight, query_weight,
        pack, keyval_weight, cos, sin, act, grad_hidden, parts, owners,
    )
    share = width // owners
    mine = lambda vector, size: lax.dynamic_slice(vector, (place * size,), (size,))
    query_bias_grad, branch_sum, ag, ash, dg, dsh = [mine(vectors[i], share) for i in range(6)]
    return (
        layer_out.reshape(rows, blk, width),
        keyval_out,
        grad_tokens.reshape(rows, blk, width),
        grad_query_weight,
        query_bias_grad,
        grad_keyval_weight,
        mine(vectors[6], kvw // owners),
        grad_out_weight,
        branch_sum,
        grad_up_weight,
        mine(vectors[8 : 8 + parts].reshape(ff), ff // owners),
        grad_down_weight,
        branch_sum,
        ag,
        ash,
        dg,
        dsh,
    )


def choose(tokens, *rest):
    rows, blk, width = tokens.shape
    fits = blk == 256 and rows == 8 and rest[7].shape == (width, 4 * width) and width % 256 == 0
    fits = fits and lax.axis_size("batch") == 4 and lax.axis_size("seq") == 8
    return (local if fits else local_plain)(tokens, *rest)


def solution(mesh):
    placed = (
        P("batch", "seq", None),
        P("batch", "seq"),
        P(),
        P(),
        P(),
        P(),
        P(),
        P(),
        P(),
        P(),
        P(),
        P(),
        P(),
        P(),
        P(),
        P(),
        P("batch", "seq", None),
        P("batch", "seq", None),
    )
    return jax.shard_map(
        choose,
        mesh=mesh,
        in_specs=placed,
        out_specs=(
            P("batch", "seq", None),
            P("batch", "seq", None),
            P("batch", "seq", None),
            P("seq", None),
            P("seq"),
            P("seq", None),
            P("seq"),
            P("seq", None),
            P("seq"),
            P("seq", None),
            P("seq"),
            P("seq", None),
            P("seq"),
            P("seq"),
            P("seq"),
            P("seq"),
            P("seq"),
        ),
        check_vma=False,
    )
```

```python
from functools import partial

import jax
import jax.numpy as jnp
from jax import lax
from jax.experimental import pallas as pl
from jax.experimental.pallas import tpu as pltpu
from jax.sharding import PartitionSpec as P

HEADS = 12
HEAD_DIM = 64
ROT = 16
LOG2E = 1.4426950408889634
f32 = jnp.float32
bf16 = jnp.bfloat16


epsilon = 1e-05
rope_base = 10000.0
negative = -1e30


def layer_norm(values, gain_vector, shift_vector):
    average = jnp.mean(values, axis=-1, keepdims=True)
    centred = values - average
    variance = jnp.mean(centred * centred, axis=-1, keepdims=True)
    return centred * lax.rsqrt(variance + epsilon) * gain_vector + shift_vector


def rotary_tables(positions):
    half_rot = ROT // 2
    frequency = rope_base ** (-(2.0 * jnp.arange(half_rot, dtype=jnp.float32)) / ROT)
    angles = positions.astype(jnp.float32)[:, None] * frequency[None, :]
    return (jnp.cos(angles), jnp.sin(angles))


def rotate(values, cos_table, sin_table):
    half_rot = ROT // 2
    first_half = values[..., :half_rot]
    second_half = values[..., half_rot:ROT]
    return jnp.concatenate(
        [
            first_half * cos_table - second_half * sin_table,
            second_half * cos_table + first_half * sin_table,
            values[..., ROT:],
        ],
        axis=-1,
    )


def unrotate(values, cos_table, sin_table):
    half_rot = ROT // 2
    first_half = values[..., :half_rot]
    second_half = values[..., half_rot:ROT]
    return jnp.concatenate(
        [
            first_half * cos_table + second_half * sin_table,
            second_half * cos_table - first_half * sin_table,
            values[..., ROT:],
        ],
        axis=-1,
    )


def contract_rows(left_side, right_side):
    return lax.dot_general(
        left_side, right_side, (((0,), (0,)), ((), ())), preferred_element_type=jnp.float32
    )


def contract_cols(left_side, right_side):
    return lax.dot_general(
        left_side, right_side, (((1,), (1,)), ((), ())), preferred_element_type=jnp.float32
    )


def local_plain(
    tokens,
    segment_ids,
    query_weight,
    query_bias,
    keyval_weight,
    keyval_bias,
    out_weight,
    out_bias,
    up_weight,
    up_bias,
    down_weight,
    down_bias,
    attention_gain,
    attention_shift,
    dense_gain,
    dense_shift,
    out_cotangent,
    keyval_cotangent,
):
    rows, local_len, width = tokens.shape
    full_len = local_len * lax.axis_size("seq")
    tok_count = rows * local_len
    offset = lax.axis_index("seq") * local_len
    positions = offset + jnp.arange(local_len, dtype=jnp.int32)
    key_positions = jnp.arange(full_len, dtype=jnp.int32)
    score_scale = HEAD_DIM ** (-0.5)
    inputs = tokens.astype(jnp.float32).reshape(tok_count, width)
    valid_rows = (segment_ids >= 0).astype(jnp.float32).reshape(tok_count, 1)
    normed_full, attention_pull = jax.vjp(layer_norm, inputs, attention_gain, attention_shift)
    normed = normed_full.astype(jnp.bfloat16)
    query_pre = jnp.dot(normed, query_weight, preferred_element_type=jnp.float32) + query_bias
    keyval_pre = jnp.dot(normed, keyval_weight, preferred_element_type=jnp.float32) + keyval_bias
    cos_table, sin_table = rotary_tables(positions)
    queries = rotate(
        query_pre.reshape(rows, local_len, HEADS, HEAD_DIM),
        cos_table[:, None, :],
        sin_table[:, None, :],
    ).astype(jnp.bfloat16)
    queries = queries.transpose(0, 2, 1, 3).reshape(rows, HEADS * local_len, HEAD_DIM)
    key_part = keyval_pre[:, :HEAD_DIM].reshape(rows, local_len, HEAD_DIM)
    value_part = keyval_pre[:, HEAD_DIM:].reshape(rows, local_len, HEAD_DIM)
    keyval_local = jnp.concatenate(
        [rotate(key_part, cos_table, sin_table), value_part], axis=-1
    ).astype(jnp.bfloat16)
    keyval_all, segment_all = (
        lax.all_gather(keyval_local, "seq", axis=1, tiled=True),
        lax.all_gather(segment_ids, "seq", axis=1, tiled=True),
    )

    def scores_of(query_rows, key_rows, segment_row, segment_keys):
        scores = contract_cols(query_rows, key_rows) * score_scale
        allowed = (positions[:, None] >= key_positions[None, :]) & (
            segment_row[:, None] == segment_keys[None, :]
        )
        scores = scores.reshape(HEADS, local_len, full_len)
        return jnp.where(allowed[None], scores, negative)

    def forward_row(pieces):
        query_rows, keyval_row, segment_row, segment_keys = pieces
        scores = scores_of(query_rows, keyval_row[:, :HEAD_DIM], segment_row, segment_keys)
        top_score = jnp.max(scores, axis=-1, keepdims=True)
        expanded = jnp.exp(scores - top_score)
        row_total = jnp.sum(expanded, axis=-1, keepdims=True)
        weights = (expanded / row_total).reshape(HEADS * local_len, full_len).astype(jnp.bfloat16)
        attended_row = jnp.dot(
            weights, keyval_row[:, HEAD_DIM:], preferred_element_type=jnp.float32
        ).astype(jnp.bfloat16)
        log_total = (top_score + jnp.log(row_total)).reshape(HEADS * local_len)
        return (attended_row, log_total)

    attended, log_totals = lax.map(forward_row, (queries, keyval_all, segment_ids, segment_all))
    attended_flat = (
        attended.reshape(rows, HEADS, local_len, HEAD_DIM)
        .transpose(0, 2, 1, 3)
        .reshape(tok_count, width)
    )
    attn_out = jnp.dot(attended_flat, out_weight, preferred_element_type=jnp.float32) + out_bias
    dense_full, dense_pull = jax.vjp(layer_norm, inputs, dense_gain, dense_shift)
    dense_in = dense_full.astype(jnp.bfloat16)
    hidden = jnp.dot(dense_in, up_weight, preferred_element_type=jnp.float32) + up_bias
    activated_full, gelu_pull = jax.vjp(partial(jax.nn.gelu, approximate=False), hidden)
    activated = activated_full.astype(jnp.bfloat16)
    dense_out = jnp.dot(activated, down_weight, preferred_element_type=jnp.float32) + down_bias
    layer_out = (
        (inputs + valid_rows * (attn_out + dense_out))
        .astype(jnp.bfloat16)
        .reshape(rows, local_len, width)
    )
    upstream = out_cotangent.astype(jnp.float32).reshape(tok_count, width)
    branch_full = valid_rows * upstream
    branch_grad = branch_full.astype(jnp.bfloat16)
    branch_sum = jnp.sum(branch_full, axis=0)
    grad_out_weight = contract_rows(attended_flat, branch_grad)
    grad_down_weight = contract_rows(activated, branch_grad)
    (grad_hidden_full,) = gelu_pull(contract_cols(branch_grad, down_weight))
    grad_hidden = grad_hidden_full.astype(jnp.bfloat16)
    grad_up_weight = contract_rows(dense_in, grad_hidden)
    grad_up_bias = jnp.sum(grad_hidden.astype(jnp.float32), axis=0)
    grad_dense_in = contract_cols(grad_hidden, up_weight)
    dense_back, grad_dense_gain, grad_dense_shift = dense_pull(grad_dense_in)
    grad_attended = contract_cols(branch_grad, out_weight).astype(jnp.bfloat16)
    grad_attended = (
        grad_attended.reshape(rows, local_len, HEADS, HEAD_DIM)
        .transpose(0, 2, 1, 3)
        .reshape(rows, HEADS * local_len, HEAD_DIM)
    )
    keyval_back, segment_back = (
        lax.all_gather(keyval_local, "seq", axis=1, tiled=True),
        lax.all_gather(segment_ids, "seq", axis=1, tiled=True),
    )

    def backward_row(pieces):
        query_rows, keyval_row, segment_row, segment_keys, log_row, grad_rows = pieces
        key_rows = keyval_row[:, :HEAD_DIM]
        value_rows = keyval_row[:, HEAD_DIM:]
        scores = scores_of(query_rows, key_rows, segment_row, segment_keys)
        probs = jnp.exp(scores - log_row.reshape(HEADS, local_len, 1)).reshape(
            HEADS * local_len, full_len
        )
        grad_probs = contract_cols(grad_rows, value_rows)
        inner = jnp.sum(probs * grad_probs, axis=-1, keepdims=True)
        grad_scores = (probs * (grad_probs - inner)).astype(jnp.bfloat16)
        grad_query_rows = (
            jnp.dot(grad_scores, key_rows, preferred_element_type=jnp.float32) * score_scale
        )
        grad_key_rows = contract_rows(grad_scores, query_rows) * score_scale
        grad_value_rows = contract_rows(probs.astype(jnp.bfloat16), grad_rows)
        return (grad_query_rows, jnp.concatenate([grad_key_rows, grad_value_rows], axis=-1))

    grad_queries, keyval_terms = lax.map(
        backward_row, (queries, keyval_back, segment_ids, segment_back, log_totals, grad_attended)
    )
    keyval_grad = lax.psum_scatter(
        keyval_terms.astype(jnp.bfloat16), "seq", scatter_dimension=1, tiled=True
    ).astype(jnp.float32) + keyval_cotangent.astype(jnp.float32)
    grad_key_pre = unrotate(keyval_grad[..., :HEAD_DIM], cos_table, sin_table)
    grad_keyval_pre = (
        jnp.concatenate([grad_key_pre, keyval_grad[..., HEAD_DIM:]], axis=-1)
        .reshape(tok_count, 2 * HEAD_DIM)
        .astype(jnp.bfloat16)
    )
    grad_queries = grad_queries.reshape(rows, HEADS, local_len, HEAD_DIM).transpose(0, 2, 1, 3)
    grad_query_pre = (
        unrotate(grad_queries, cos_table[:, None, :], sin_table[:, None, :])
        .reshape(tok_count, width)
        .astype(jnp.bfloat16)
    )
    grad_query_weight = contract_rows(normed, grad_query_pre)
    grad_query_bias = jnp.sum(grad_query_pre.astype(jnp.float32), axis=0)
    grad_keyval_weight = contract_rows(normed, grad_keyval_pre)
    grad_keyval_bias = jnp.sum(grad_keyval_pre.astype(jnp.float32), axis=0)
    grad_normed = contract_cols(grad_query_pre, query_weight) + contract_cols(
        grad_keyval_pre, keyval_weight
    )
    attention_back, grad_attention_gain, grad_attention_shift = attention_pull(grad_normed)
    grad_tokens = (
        (upstream + attention_back + dense_back)
        .astype(jnp.bfloat16)
        .reshape(rows, local_len, width)
    )
    local_grads = (
        grad_query_weight,
        grad_query_bias,
        grad_keyval_weight,
        grad_keyval_bias,
        grad_out_weight,
        branch_sum,
        grad_up_weight,
        grad_up_bias,
        grad_down_weight,
        branch_sum,
        grad_attention_gain,
        grad_attention_shift,
        grad_dense_gain,
        grad_dense_shift,
    )
    shares = (
        lax.psum_scatter(
            local_grads[0].astype(jnp.bfloat16), "seq", scatter_dimension=0, tiled=True
        ).astype(jnp.float32),
        lax.psum_scatter(
            local_grads[1].astype(jnp.bfloat16), "seq", scatter_dimension=0, tiled=True
        ).astype(jnp.float32),
        lax.psum_scatter(
            local_grads[2].astype(jnp.bfloat16), "seq", scatter_dimension=0, tiled=True
        ).astype(jnp.float32),
        lax.psum_scatter(
            local_grads[3].astype(jnp.bfloat16), "seq", scatter_dimension=0, tiled=True
        ).astype(jnp.float32),
        lax.psum_scatter(
            local_grads[4].astype(jnp.bfloat16), "seq", scatter_dimension=0, tiled=True
        ).astype(jnp.float32),
        lax.psum_scatter(
            local_grads[5].astype(jnp.bfloat16), "seq", scatter_dimension=0, tiled=True
        ).astype(jnp.float32),
        lax.psum_scatter(
            local_grads[6].astype(jnp.bfloat16), "seq", scatter_dimension=0, tiled=True
        ).astype(jnp.float32),
        lax.psum_scatter(
            local_grads[7].astype(jnp.bfloat16), "seq", scatter_dimension=0, tiled=True
        ).astype(jnp.float32),
        lax.psum_scatter(
            local_grads[8].astype(jnp.bfloat16), "seq", scatter_dimension=0, tiled=True
        ).astype(jnp.float32),
        lax.psum_scatter(
            local_grads[9].astype(jnp.bfloat16), "seq", scatter_dimension=0, tiled=True
        ).astype(jnp.float32),
        lax.psum_scatter(
            local_grads[10].astype(jnp.bfloat16), "seq", scatter_dimension=0, tiled=True
        ).astype(jnp.float32),
        lax.psum_scatter(
            local_grads[11].astype(jnp.bfloat16), "seq", scatter_dimension=0, tiled=True
        ).astype(jnp.float32),
        lax.psum_scatter(
            local_grads[12].astype(jnp.bfloat16), "seq", scatter_dimension=0, tiled=True
        ).astype(jnp.float32),
        lax.psum_scatter(
            local_grads[13].astype(jnp.bfloat16), "seq", scatter_dimension=0, tiled=True
        ).astype(jnp.float32),
    )
    totals = (
        lax.psum(shares[0].astype(jnp.bfloat16), "batch").astype(jnp.float32),
        lax.psum(shares[1].astype(jnp.bfloat16), "batch").astype(jnp.float32),
        lax.psum(shares[2].astype(jnp.bfloat16), "batch").astype(jnp.float32),
        lax.psum(shares[3].astype(jnp.bfloat16), "batch").astype(jnp.float32),
        lax.psum(shares[4].astype(jnp.bfloat16), "batch").astype(jnp.float32),
        lax.psum(shares[5].astype(jnp.bfloat16), "batch").astype(jnp.float32),
        lax.psum(shares[6].astype(jnp.bfloat16), "batch").astype(jnp.float32),
        lax.psum(shares[7].astype(jnp.bfloat16), "batch").astype(jnp.float32),
        lax.psum(shares[8].astype(jnp.bfloat16), "batch").astype(jnp.float32),
        lax.psum(shares[9].astype(jnp.bfloat16), "batch").astype(jnp.float32),
        lax.psum(shares[10].astype(jnp.bfloat16), "batch").astype(jnp.float32),
        lax.psum(shares[11].astype(jnp.bfloat16), "batch").astype(jnp.float32),
        lax.psum(shares[12].astype(jnp.bfloat16), "batch").astype(jnp.float32),
        lax.psum(shares[13].astype(jnp.bfloat16), "batch").astype(jnp.float32),
    )
    return (
        layer_out,
        keyval_local,
        grad_tokens,
        totals[0],
        totals[1],
        totals[2],
        totals[3],
        totals[4],
        totals[5],
        totals[6],
        totals[7],
        totals[8],
        totals[9],
        totals[10],
        totals[11],
        totals[12],
        totals[13],
    )


ROT_HALF = ROT // 2


def nn(left, right):
    return lax.dot_general(left, right, (((1,), (0,)), ((), ())), preferred_element_type=f32)


def nt(left, right):
    return lax.dot_general(left, right, (((1,), (1,)), ((), ())), preferred_element_type=f32)


def tn(left, right):
    return lax.dot_general(left, right, (((0,), (0,)), ((), ())), preferred_element_type=f32)


def tt(left, right):
    return lax.dot_general(left, right, (((0,), (1,)), ((), ())), preferred_element_type=f32)


def standardize(values):
    centred = values - jnp.mean(values, axis=-1, keepdims=True)
    variance = jnp.mean(centred * centred, axis=-1, keepdims=True)
    spread = lax.rsqrt(variance + epsilon)
    return centred * spread, spread


def turn(columns, cos, sin):
    a, b = columns[0:ROT_HALF], columns[ROT_HALF:ROT]
    return jnp.concatenate([a * cos - b * sin, b * cos + a * sin, columns[ROT:]], axis=0)


def turn_back(columns, cos, sin):
    a, b = columns[0:ROT_HALF], columns[ROT_HALF:ROT]
    return jnp.concatenate([a * cos + b * sin, b * cos - a * sin, columns[ROT:]], axis=0)


def params(megabytes, **rest):
    return pltpu.CompilerParams(vmem_limit_bytes=megabytes * 2**20, **rest)


def cost(flops, moved):
    return pl.CostEstimate(flops=int(flops), bytes_accessed=int(moved), transcendentals=0)


def whole(*shape):
    return pl.BlockSpec(shape, lambda *_: (0,) * len(shape))


AG, AS, DG, DS, QB, OB, DB, KB, UB = range(9)


def vector(pack, at):
    return pack[at : at + 1, :]


def alive(ids):
    count = jnp.sum((ids >= 0).astype(f32), axis=1, keepdims=True)
    return lax.broadcasted_iota(jnp.int32, (ids.shape[1], 1), 0).astype(f32) < count


def norm_kernel(
    x_ref, cot_ref, seg_ref, pack, kw_ref, cos_ref, sin_ref,
    normed_ref, dense_ref, bg_ref, kv_ref, kvo_ref,
):
    count, _, kvw = kv_ref.shape
    blk = kvo_ref.shape[1]
    cos, sin = cos_ref[...], sin_ref[...]
    for n in range(count):
        rows = slice(n * blk, (n + 1) * blk)
        ids = seg_ref[pl.ds(pl.program_id(0) * count + n, 1), :]
        bg_ref[rows] = jnp.where(alive(ids), cot_ref[rows].astype(f32), 0.0).astype(bf16)
        unit, _ = standardize(x_ref[rows].astype(f32))
        normed = (unit * vector(pack, AG) + vector(pack, AS)).astype(bf16)
        normed_ref[rows] = normed
        dense_ref[rows] = (unit * vector(pack, DG) + vector(pack, DS)).astype(bf16)
        keyval = nn(normed, kw_ref[...]) + vector(pack, KB)[:, :kvw]
        keyval = turn(keyval.T, cos, sin).T.astype(bf16)
        kvo_ref[n] = keyval
        kv_ref[n, 0:blk, :] = keyval
        ids = [ids[:, at : at + 128].astype(f32) for at in range(0, blk, 128)]
        kv_ref[n, blk:, :] = jnp.concatenate(
            ids + [jnp.zeros((16 - len(ids), 128), f32)], axis=0
        ).astype(bf16)


def norms(x, cot, seg, pack, kw, cos, sin, count=2):
    tok, width = x.shape
    rows, blk = seg.shape
    kvw = kw.shape[1]
    tile = pl.BlockSpec((count * blk, width), lambda r: (r, 0))
    pair = lambda high: pl.BlockSpec((count, high, kvw), lambda r: (r, 0, 0))
    flat = jax.ShapeDtypeStruct((tok, width), bf16)
    return pl.pallas_call(
        norm_kernel,
        grid=(rows // count,),
        in_specs=[
            tile, tile, whole(rows, blk), whole(*pack.shape), whole(width, kvw),
            whole(ROT_HALF, blk), whole(ROT_HALF, blk),
        ],
        out_specs=[tile, tile, tile, pair(blk + 16), pair(blk)],
        out_shape=[
            flat, flat, flat,
            jax.ShapeDtypeStruct((rows, blk + 16, kvw), bf16),
            jax.ShapeDtypeStruct((rows, blk, kvw), bf16),
        ],
        compiler_params=params(60),
        cost_estimate=cost(2 * tok * width * kvw, 10 * tok * width),
        name="norms",
    )(x, cot, seg, pack, kw, cos, sin)


def gelu_parts(hidden):
    size = jnp.abs(hidden)
    t = pltpu.reciprocal(1.0 + (0.3275911 * 0.5**0.5) * size, approx=True)
    bell = jnp.exp2(hidden * hidden * (-0.5 * LOG2E))
    tail = t * (0.127414796 + t * (-0.142248368 + t * (0.7107068705 + t * (-0.7265760135 + t * 0.5307027145))))
    tail = tail * bell
    share = jnp.where(hidden >= 0.0, 1.0 - tail, tail)
    return share, bell * 0.3989422804014327


def towards(axis, target):
    return dict(device_id={axis: target}, device_id_type=pl.DeviceIdType.MESH)


def send(src, dst, sems, at, axis, target):
    return pltpu.make_async_remote_copy(
        src_ref=src, dst_ref=dst, send_sem=sems.at[0, at], recv_sem=sems.at[1, at],
        **towards(axis, target),
    )


def greet(planes):
    seq, batch = lax.axis_index("seq"), lax.axis_index("batch")
    barrier = pltpu.get_barrier_semaphore()
    column = [lax.rem(seq + 2 * hop, 2 * planes) for hop in range(1, planes)]
    for other in column + [seq + 1 - 2 * lax.rem(seq, 2)]:
        pl.semaphore_signal(barrier, inc=1, **towards("seq", other))
    for other in (batch + 1 - 2 * lax.rem(batch, 2), lax.rem(batch + 2, 4)):
        pl.semaphore_signal(barrier, inc=1, **towards("batch", other))
    pl.semaphore_wait(barrier, planes + 2)


def dense_kernel(
    di_ref, bg_ref, up_ref, down_ref, normed_ref, pack, qw_ref, ow_ref, cos_ref, sin_ref,
    kv_ref, act_ref, gh_ref, red_ref, gub_ref, q_ref, do_ref, kvs_ref,
    hid0, hid1, gac0, gac1, act0, act1, gh0, gh1, acc_up, acc_dn, acc_ub,
    cut_up, cut_dn, core_up, core_dn, half_up, half_dn, x_up, x_dn,
    own_sem, z_sem, y_sem, core_sem, x_sem,
    *, pairs, steps, tile, parts, owners,
):
    i = pl.program_id(0)
    planes = owners // 2
    seq, batch = lax.axis_index("seq"), lax.axis_index("batch")
    plane, side = seq // 2, lax.rem(seq, 2)
    x_at, core_at = batch // 2, lax.rem(batch, 2)
    x_other, core_other = lax.rem(batch + 2, 4), batch + 1 - 2 * core_at
    y_other = seq + 1 - 2 * side

    def own_copy():
        return pltpu.make_async_copy(kv_ref, kvs_ref.at[seq], own_sem)

    def hop_copy(hop):
        block = kv_ref if hop == 0 else kvs_ref.at[seq - 2 * hop]
        return send(block, kvs_ref.at[seq - 2 * hop], z_sem, hop, "seq", seq + 2)

    def across_copy(hop):
        block = kv_ref if hop == 0 else kvs_ref.at[seq - 2 * hop]
        return send(block, kvs_ref.at[seq - 2 * hop], y_sem, hop, "seq", y_other)

    def spread(hop):
        @pl.when(plane >= hop)
        def _():
            if hop > 0:
                arrived(hop)
            across_copy(hop).start()

            @pl.when(plane < planes - 1)
            def _():
                hop_copy(hop).start()

    def arrived(hop):
        block = kvs_ref.at[seq - 2 * hop]
        send(block, block, z_sem, hop - 1, "seq", y_other).wait_recv()

    def settle(hop):
        @pl.when(plane >= hop)
        def _():
            across_copy(hop).wait_send()
            block = kvs_ref.at[y_other - 2 * hop]
            send(block, block, y_sem, hop, "seq", y_other).wait_recv()

            @pl.when(plane < planes - 1)
            def _():
                hop_copy(hop).wait_send()

    def core_copies(c):
        return [
            send(cut_up.at[1 - core_at], core_up.at[c], core_sem, 2 * c, "batch", core_other),
            send(cut_dn.at[1 - core_at], core_dn.at[c], core_sem, 2 * c + 1, "batch", core_other),
        ]

    def x_copies(c):
        return [
            send(half_up.at[c % 2, 1 - x_at], x_up.at[c], x_sem, 2 * c, "batch", x_other),
            send(half_dn.at[c % 2, 1 - x_at], x_dn.at[c], x_sem, 2 * c + 1, "batch", x_other),
        ]

    def plus(first, second):
        return (first.astype(f32) + second.astype(f32)).astype(bf16)

    def cut(c):
        rows, cols = cut_up.shape[3], cut_up.shape[4]
        for core in range(2):
            for x in range(2):
                for o in range(owners):
                    at = (2 * o + core) * rows
                    cut_up[core, x, o] = acc_up[at : at + rows, x * cols : (x + 1) * cols].astype(bf16)
                tall = cut_dn.shape[3]
                for o in range(cut_dn.shape[2]):
                    at = (2 * o + core) * tall
                    cut_dn[core, x, o] = acc_dn[at : at + tall, x * cols : (x + 1) * cols].astype(bf16)
        for copy in core_copies(c):
            copy.start()

    def halve(c):
        for copy in core_copies(c):
            copy.wait()
        for x in range(2):
            half_up[c % 2, x] = plus(cut_up[core_at, x], core_up[c, x])
            half_dn[c % 2, x] = plus(cut_dn[core_at, x], core_dn[c, x])
        for copy in x_copies(c):
            copy.start()

    def fold(c):
        for copy in x_copies(c):
            copy.wait()
        rows = cut_up.shape[3]
        few = cut_dn.shape[2]
        red_ref[:, c * rows : (c + 1) * rows, :] = plus(half_up[c % 2, x_at], x_up[c])
        red_ref[c * few : (c + 1) * few, parts * rows :, :] = plus(half_dn[c % 2, x_at], x_dn[c])

    def rows_of(step, odd):
        return pl.ds(pl.multiple_of((lax.rem(step, pairs) * 2 + odd) * tile, tile), tile)

    def enter(odd, hid, gac):
        rows = rows_of(i, odd)
        hid[...] = nn(di_ref[rows, :], up_ref[...]) + pack[pl.ds(UB + i // pairs, 1), :]
        gac[...] = nt(bg_ref[rows, :], down_ref[...])

    def bend(odd, hid, gac, act_s, gh_s):
        hidden = hid[...]
        share, bell = gelu_parts(hidden)
        act = (hidden * share).astype(bf16)
        grad = (gac[...] * (share + hidden * bell)).astype(bf16)
        act_s[...] = act
        gh_s[...] = grad
        at = (1 - odd) * tile
        act_ref[at : at + tile, :] = act
        gh_ref[at : at + tile, :] = grad

    def gather(odd, act_s, gh_s, fresh=False):
        rows = rows_of(i - 1, odd)
        grad = gh_s[...]
        up, dn = tn(di_ref[rows, :], grad), tn(act_s[...], bg_ref[rows, :])
        ub = jnp.sum(grad.astype(f32), axis=0, keepdims=True)
        if fresh:
            acc_up[...], acc_dn[...], acc_ub[...] = up, dn, ub
        else:
            acc_up[...] += up
            acc_dn[...] += dn
            acc_ub[...] += ub

    def heads(step):
        count, _, wide = q_ref.shape
        blk = wide // HEADS
        cos, sin = cos_ref[...], sin_ref[...]
        for n in range(count):
            rows = pl.ds(pl.multiple_of((step * count + n) * blk, blk), blk)
            queries = (nn(normed_ref[n * blk : (n + 1) * blk, :], qw_ref[...]) + vector(pack, QB)).T
            upstream = nt(ow_ref[...], bg_ref[rows, :])
            for h in range(HEADS):
                part = slice(h * HEAD_DIM, (h + 1) * HEAD_DIM)
                lanes = slice(h * blk, (h + 1) * blk)
                q_ref[n, :, lanes] = (turn(queries[part], cos, sin) * HEAD_DIM**-0.5).astype(bf16)
                do_ref[n, :, lanes] = upstream[part].astype(bf16)

    @pl.when(i == 0)
    def _():
        greet(planes)
        own_copy().start()

    @pl.when(i == 0)
    def _():
        enter(0, hid0, gac0)
        enter(1, hid1, gac1)
        bend(0, hid0, gac0, act0, gh0)

    def body(fresh):
        enter(0, hid0, gac0)
        bend(1, hid1, gac1, act1, gh1)
        gather(0, act0, gh0, fresh)
        enter(1, hid1, gac1)
        bend(0, hid0, gac0, act0, gh0)
        gather(1, act1, gh1)

    @pl.when((i > 0) & (i < steps) & (lax.rem(i - 1, pairs) == 0))
    def _():
        body(True)

    @pl.when((i > 0) & (i < steps) & (lax.rem(i - 1, pairs) > 0))
    def _():
        body(False)

    @pl.when(i == steps)
    def _():
        bend(1, hid1, gac1, act1, gh1)
        gather(0, act0, gh0)
        gather(1, act1, gh1)

    for c in range(parts):
        @pl.when(i == (c + 1) * pairs)
        def _():
            gub_ref[c] = acc_ub[...]
            cut(c)
            if c > 1:
                fold(c - 2)

        if c < parts - 1:
            @pl.when(i == (c + 1) * pairs + 1)
            def _():
                halve(c)

    for hop in range(planes):
        @pl.when(i == hop * pairs)
        def _():
            spread(hop)

    @pl.when(i > steps)
    def _():
        heads(i - steps - 1)

    @pl.when(i == steps + 1)
    def _():
        halve(parts - 1)
        fold(parts - 2)

    @pl.when(i == pl.num_programs(0) - 1)
    def _():
        own_copy().wait()
        for hop in range(planes):
            settle(hop)
        fold(parts - 1)


def dense(di, bg, up, down, normed, pack, qw, ow, cos, sin, kv, parts, owners, tile=512):
    tok, width = di.shape
    ff = up.shape[1]
    chunk = ff // parts
    pairs = tok // tile // 2
    steps = pairs * parts
    high, low, cols = width // owners // 2, chunk // (owners // parts) // 2, chunk // 2
    few = owners // parts
    rows, blk = kv.shape[0], cos.shape[1]
    group = tile // blk
    late = lambda i: jnp.clip(i - steps - 1, 0, rows // group - 1)
    at = lambda i: jnp.clip(i, 0, steps - 1)
    anywhere = pl.BlockSpec(memory_space=pl.ANY)
    once = lambda *shape: pl.BlockSpec(
        shape, lambda *_: (0,) * len(shape), pipeline_mode=pl.Buffered(1)
    )
    dma = pltpu.SemaphoreType.DMA
    return pl.pallas_call(
        partial(
            dense_kernel, pairs=pairs, steps=steps, tile=tile, parts=parts, owners=owners
        ),
        grid=(steps + 1 + rows // group,),
        in_specs=[
            once(tok, width),
            once(tok, width),
            pl.BlockSpec((width, chunk), lambda i: (0, at(i) // pairs)),
            pl.BlockSpec((chunk, width), lambda i: (at(i) // pairs, 0)),
            pl.BlockSpec((tile, width), lambda i: (late(i), 0)),
            once(*pack.shape), once(width, width), once(width, width),
            once(ROT_HALF, blk), once(ROT_HALF, blk),
            anywhere,
        ],
        out_specs=[
            pl.BlockSpec((2 * tile, chunk), lambda i: (jnp.minimum(i, steps), 0)),
            pl.BlockSpec((2 * tile, chunk), lambda i: (jnp.minimum(i, steps), 0)),
            once(owners, parts * high + low, cols),
            once(parts, 1, chunk),
            pl.BlockSpec((group, HEAD_DIM, HEADS * blk), lambda i: (late(i), 0, 0)),
            pl.BlockSpec((group, HEAD_DIM, HEADS * blk), lambda i: (late(i), 0, 0)),
            anywhere,
        ],
        out_shape=[
            jax.ShapeDtypeStruct((2 * tile * (steps + 1), chunk), bf16),
            jax.ShapeDtypeStruct((2 * tile * (steps + 1), chunk), bf16),
            jax.ShapeDtypeStruct((owners, parts * high + low, cols), bf16),
            jax.ShapeDtypeStruct((parts, 1, chunk), f32),
            jax.ShapeDtypeStruct((rows, HEAD_DIM, HEADS * blk), bf16),
            jax.ShapeDtypeStruct((rows, HEAD_DIM, HEADS * blk), bf16),
            jax.ShapeDtypeStruct((owners,) + kv.shape, bf16),
        ],
        scratch_shapes=[pltpu.VMEM((tile, chunk), f32)] * 4
        + [pltpu.VMEM((tile, chunk), bf16)] * 4
        + [
            pltpu.VMEM((width, chunk), f32), pltpu.VMEM((chunk, width), f32),
            pltpu.VMEM((1, chunk), f32),
            pltpu.VMEM((2, 2, owners, high, cols), bf16), pltpu.VMEM((2, 2, few, low, cols), bf16),
            pltpu.VMEM((parts, 2, owners, high, cols), bf16),
            pltpu.VMEM((parts, 2, few, low, cols), bf16),
            pltpu.VMEM((2, 2, owners, high, cols), bf16), pltpu.VMEM((2, 2, few, low, cols), bf16),
            pltpu.VMEM((parts, owners, high, cols), bf16),
            pltpu.VMEM((parts, few, low, cols), bf16),
            dma, dma((2, owners // 2)), dma((2, owners // 2)), dma((2, 2 * parts)),
            dma((2, 2 * parts)),
        ],
        compiler_params=params(63, collective_id=0, has_side_effects=True),
        cost_estimate=cost(8 * tok * width * ff, 8 * tok * width + 4 * tok * ff),
        name="dense",
    )(di, bg, up, down, normed, pack, qw, ow, cos, sin, kv)


DESCEND, PROJECT, CLOSE = (0, 1, 6, 7), (2, 3, 4, 5), (8, 9, 12, 15)
FINISH, BACK = (10, 11, 13, 14), (16, 17, 18, 19)


def stair(*groups):
    jumps = sorted((step, n) for group in groups for n, step in enumerate(group))

    def of(i):
        value = jumps[0][1]
        for (_, before), (step, after) in zip(jumps, jumps[1:]):
            if after != before:
                value = value + jnp.where(i >= step, after - before, 0)
        return value

    return of


def tail_kernel(
    x_ref, cot_ref, seg_ref, att_ref, gq_ref, bg_ref, normed_ref, kcot_ref, first_ref,
    first_across_ref, second_ref, second_across_ref, gub_ref,
    mlp_ref, ow_hbm, down_hbm, up_hbm, qw_hbm, pack, kw_ref, cos_ref, sin_ref, *refs, rows, parts, owners,
):
    acts, ghs, refs = refs[:parts], refs[parts : 2 * parts], refs[2 * parts :]
    (
        out_ref, gt_ref, gow_ref, gqw_ref, guw_ref, gdw_ref, keyval_ref, vector_ref,
        ow_ref, down_ref, up_ref, qw_ref, acc, gd_s, gk_s, vec_s,
        own, across, below, total, stage, mlp_in,
        cut, core_in, x_in, piece, piece_in, part_in,
        small_k, small_v, seq_k, seq_v, mid_k, mid_v, batch_k, batch_v,
        load_sem, stage_sem, own_sem, first_sem, y_sem, z_sem, mlp_sem, core_sem, x_sem, piece_sem, part_sem,
        sk_sem, sv_sem, bk_sem, bv_sem,
    ) = refs
    i = pl.program_id(0)
    planes = owners // 2
    some = rows // 2
    seq, batch = lax.axis_index("seq"), lax.axis_index("batch")
    plane, side = seq // 2, lax.rem(seq, 2)
    x_at, core_at = batch // 2, lax.rem(batch, 2)
    x_other, core_other = lax.rem(batch + 2, 4), batch + 1 - 2 * core_at
    y_other = seq + 1 - 2 * side
    high, cols = cut.shape[3], cut.shape[4]
    seq_at = lambda hop: lax.rem(seq + hop, owners)
    batch_at = lambda hop: lax.rem(batch + hop, parts)

    def enter():
        barrier = pltpu.get_barrier_semaphore()
        for hop in range(1, owners):
            pl.semaphore_signal(barrier, inc=1, **towards("seq", seq_at(hop)))
        for hop in range(1, parts):
            pl.semaphore_signal(barrier, inc=1, **towards("batch", batch_at(hop)))
        pl.semaphore_wait(barrier, owners + parts - 2)

    pairs = ((up_hbm, up_ref), (ow_hbm, ow_ref), (down_hbm, down_ref), (qw_hbm, qw_ref))

    def load(n):
        return pltpu.make_async_copy(pairs[n][0], pairs[n][1], load_sem.at[n])

    def rows_of(part):
        return pl.ds(part * some, some)

    def own_copy(k, part):
        source = second_ref.at[k] if part else first_ref.at[k]
        return pltpu.make_async_copy(source, own.at[k, rows_of(part)], own_sem.at[2 * k + part])

    def first_copy(k):
        return pltpu.make_async_copy(first_across_ref.at[k], across.at[k, rows_of(0)], first_sem.at[k])

    def across_copy(k):
        return send(second_across_ref.at[k], across.at[k, rows_of(1)], y_sem, k, "seq", y_other)

    def below_copy(k, part):
        return send(
            own.at[k, rows_of(part)], below.at[k, rows_of(part)], z_sem, 2 * k + part, "seq",
            lax.rem(seq + owners - 2, owners),
        )

    def start_local(k):
        @pl.when(plane >= k)
        def _():
            own_copy(k, 0).start()
            first_copy(k).start()
            own_copy(k, 1).start()

    def start_across(k):
        @pl.when(plane >= k)
        def _():
            across_copy(k).start()

    def tick(step, part):
        k = step - (planes - 1 - plane)
        rows_at = slice(part * some, (part + 1) * some)

        @pl.when(k >= 0)
        def _():
            own_copy(k, part).wait()
            if part:
                across_copy(k).wait_recv()
            else:
                first_copy(k).wait()
            total[rows_at] = own[k, rows_at].astype(f32) + across[k, rows_at].astype(f32)

            @pl.when(plane < planes - 1)
            def _():
                below_copy(k, part).wait_recv()
                total[rows_at] += below[k, rows_at].astype(f32)

            if step < planes - 1:
                own[k, rows_at] = total[rows_at].astype(bf16)
                below_copy(k, part).start()

    def settle():
        for k in range(planes):
            @pl.when(plane >= k)
            def _():
                across_copy(k).wait_send()

            for part in range(2):
                @pl.when(plane > k)
                def _():
                    below_copy(k, part).wait_send()

    def mlp_copy(hop):
        return send(mlp_ref, mlp_in.at[batch], mlp_sem, hop - 1, "batch", batch_at(hop))

    def write_out(fills):
        copies = []
        for n, (fill, out) in enumerate(fills):
            if n >= 2:
                copies[n - 2].wait()
            fill(stage.at[n % 2])
            copies.append(pltpu.make_async_copy(stage.at[n % 2], out, stage_sem.at[n % 2]))
            copies[n].start()
        for copy in copies[-2:]:
            copy.wait()

    def collect_mlp():
        for hop in range(1, parts):
            mlp_copy(hop).wait()
        tall = mlp_ref.shape[0] - parts * high
        few = tall // (2 * high)

        def fill_up(c):
            def fill(ref):
                for b in range(parts):
                    core, x = b % 2, b // 2
                    ref[core * high : (core + 1) * high, x * cols : (x + 1) * cols] = mlp_in[
                        b, c * high : (c + 1) * high, :
                    ].astype(f32)

            return fill

        def fill_down(core, n):
            def fill(ref):
                at = parts * high + n * 2 * high
                for x in range(2):
                    ref[:, x * cols : (x + 1) * cols] = mlp_in[
                        2 * x + core, at : at + 2 * high, :
                    ].astype(f32)

            return fill

        fills = [
            (fill_up(c), guw_ref.at[:, pl.ds(c * 2 * cols, 2 * cols)]) for c in range(parts)
        ]
        for core in range(2):
            for n in range(few):
                at = core * tall + n * 2 * high
                fills.append((fill_down(core, n), gdw_ref.at[pl.ds(at, 2 * high), :]))
        write_out(fills)

    def core_copy():
        return send(cut, core_in, core_sem, 0, "batch", core_other)

    def x_copy():
        return send(cut.at[1 - x_at], x_in, x_sem, 0, "batch", x_other)

    def piece_copy(hop):
        target = seq_at(hop)
        return send(piece.at[target], piece_in.at[hop - 1], piece_sem, hop - 1, "seq", target)

    def part_copy(hop):
        return send(part_in.at[batch], part_in.at[batch], part_sem, hop - 1, "batch", batch_at(hop))

    def share_of(core, m, x, o):
        rows_at = pl.ds(pl.multiple_of((2 * o + core) * high, high), high)
        return acc[m, rows_at, x * cols : (x + 1) * cols]

    def cut_square():
        for m in range(2):
            for x in range(2):
                for o in range(owners):
                    cut[x, o, m] = share_of(1 - core_at, m, x, o).astype(bf16)
        core_copy().start()

    def halve_square():
        core_copy().wait()
        for m in range(2):
            for x in range(2):
                for o in range(owners):
                    value = share_of(core_at, m, x, o) + core_in[x, o, m].astype(f32)
                    cut[x, o, m] = value.astype(bf16)
        x_copy().start()

    def spread_square():
        x_copy().wait()
        piece[...] = (cut[x_at].astype(f32) + x_in[...].astype(f32)).astype(bf16)
        for hop in range(1, owners):
            piece_copy(hop).start()

    def sum_square():
        value = piece[seq].astype(f32)
        for hop in range(1, owners):
            piece_copy(hop).wait()
            value = value + piece_in[hop - 1].astype(f32)
        part_in[batch] = value.astype(bf16)
        for hop in range(1, parts):
            part_copy(hop).start()

    def collect_square():
        for hop in range(1, parts):
            part_copy(hop).wait()

        def fill_square(m):
            def fill(ref):
                for b in range(parts):
                    core, x = b % 2, b // 2
                    ref[core * high : (core + 1) * high, x * cols : (x + 1) * cols] = part_in[
                        b, m
                    ].astype(f32)

            return fill

        write_out([(fill_square(0), gow_ref), (fill_square(1), gqw_ref)])

    def seq_copies(hop):
        target = seq_at(hop)
        return [
            send(small_k.at[target], seq_k.at[hop - 1], sk_sem, hop - 1, "seq", target),
            send(small_v.at[target], seq_v.at[hop - 1], sv_sem, hop - 1, "seq", target),
        ]

    def batch_copies(hop):
        target = batch_at(hop)
        return [
            send(mid_k, batch_k.at[hop - 1], bk_sem, hop - 1, "batch", target),
            send(mid_v, batch_v.at[hop - 1], bv_sem, hop - 1, "batch", target),
        ]

    def start_small():
        tall = small_k.shape[1]
        keyval = gk_s[...].T
        for o in range(owners):
            small_k[o] = keyval[o * tall : (o + 1) * tall].astype(bf16)
        vectors = vec_s[0:8, :].astype(bf16)
        lane = lax.broadcasted_iota(jnp.int32, (vectors.shape[1], 128), 0)
        column = lax.broadcasted_iota(jnp.int32, (vectors.shape[1], 128), 1)
        for o in range(owners):
            share = nn(vectors, (lane == column + o * tall).astype(bf16))
            long = vec_s[8 + o // 2 : 9 + o // 2, :]
            left = (o % 2) * 4 * tall
            pieces = [long[:, left + n : left + n + 128] for n in range(0, 4 * tall, 128)]
            rows_of_owner = [share, *pieces, vec_s[6:7, 0:128], jnp.zeros((7 - len(pieces), 128), f32)]
            small_v[o] = jnp.concatenate(rows_of_owner, axis=0).astype(bf16)
        for hop in range(1, owners):
            for copy in seq_copies(hop):
                copy.start()

    def turn_small():
        value, vector = small_k[seq].astype(f32), small_v[seq].astype(f32)
        for hop in range(1, owners):
            for copy in seq_copies(hop):
                copy.wait()
            value = value + seq_k[hop - 1].astype(f32)
            vector = vector + seq_v[hop - 1].astype(f32)
        mid_k[...] = value.astype(bf16)
        mid_v[...] = vector.astype(bf16)
        for hop in range(1, parts):
            for copy in batch_copies(hop):
                copy.start()

    def end_small():
        value, vector = mid_k[...].astype(f32), mid_v[...].astype(f32)
        for hop in range(1, parts):
            for copy in batch_copies(hop):
                copy.wait()
            value = value + batch_k[hop - 1].astype(f32)
            vector = vector + batch_v[hop - 1].astype(f32)
        keyval_ref[...] = value
        vector_ref[...] = vector

    count, blk = kcot_ref.shape[0], kcot_ref.shape[1]
    side_by_side = lambda ref: jnp.concatenate([ref[n] for n in range(count)], axis=1)
    ones = jnp.ones((8, count * blk), bf16)

    def project():
        branch, grad = bg_ref[...], side_by_side(gq_ref)
        acc[0] += nn(side_by_side(att_ref), branch)
        acc[1] += tt(normed_ref[...], grad)
        vec_s[0:1] += nt(ones, grad)[0:1]
        vec_s[1:2] += nn(ones, branch)[0:1]

    def close(step):
        act = jnp.concatenate([ref[...] for ref in acts], axis=1)
        branch = tn(side_by_side(att_ref), ow_ref[...]) + vector(pack, OB)
        branch = branch + (nn(act, down_ref[...]) + vector(pack, DB))
        for n in range(count):
            rows_at = slice(n * blk, (n + 1) * blk)
            ids = seg_ref[pl.ds(step * count + n, 1), :]
            part = jnp.where(alive(ids), branch[rows_at], 0.0)
            out_ref[rows_at] = (x_ref[rows_at].astype(f32) + part).astype(bf16)

    def descend(step):
        grad = jnp.concatenate([ref[...] for ref in ghs], axis=1)
        second = nt(grad, up_ref[...])
        unit, _ = standardize(x_ref[...].astype(f32))
        vec_s[4:5] += jnp.sum(second * unit, axis=0, keepdims=True)
        vec_s[5:6] += jnp.sum(second, axis=0, keepdims=True)
        gd_s[step] = second * vector(pack, DG)

    def finish(step):
        unit, _ = standardize(x_ref[...].astype(f32))
        normed = (unit * vector(pack, AG) + vector(pack, AS)).astype(bf16)
        keyval = []
        for n in range(count):
            value = (total[step * count + n] + kcot_ref[n].astype(f32)).T
            keyval.append(turn_back(value, cos_ref[...], sin_ref[...]).astype(bf16))
        keyval = jnp.concatenate(keyval, axis=1)
        gk_s[...] += nn(keyval, normed)
        vec_s[6:7, 0 : keyval.shape[0]] += nt(ones, keyval)[0:1]
        first = tt(side_by_side(gq_ref), qw_ref[...]) + tt(keyval, kw_ref[...])
        vec_s[2:3] += jnp.sum(first * unit, axis=0, keepdims=True)
        vec_s[3:4] += jnp.sum(first, axis=0, keepdims=True)
        gd_s[step] += first * vector(pack, AG)

    def back(step):
        unit, spread = standardize(x_ref[...].astype(f32))
        both = gd_s[step]
        middle = jnp.mean(both, axis=-1, keepdims=True)
        along = jnp.mean(both * unit, axis=-1, keepdims=True)
        gt_ref[...] = (cot_ref[...].astype(f32) + (both - middle - unit * along) * spread).astype(bf16)

    def at(step):
        return pl.when(i == step)

    def when(*steps):
        hit = i == steps[0]
        for step in steps[1:]:
            hit = hit | (i == step)
        return pl.when(hit)

    def ticks(*marks):
        for mark, step, part in marks:
            @at(mark)
            def _():
                tick(step, part)

    @at(0)
    def _():
        load(0).start()
        enter()
        start_across(0)
        for k in range(planes):
            start_local(k)
        for hop in range(1, parts):
            mlp_copy(hop).start()
        mlp_in[batch] = mlp_ref[...]
        acc[...] = jnp.zeros(acc.shape, f32)
        gk_s[...] = jnp.zeros(gk_s.shape, f32)
        vec_s[...] = jnp.zeros(vec_s.shape, f32)
        for c in range(parts):
            vec_s[8 + c : 9 + c] = gub_ref[c]
        load(0).wait()

    @at(2)
    def _():
        for n in range(1, len(pairs)):
            load(n).start()

    for mark, k in ((2, 1), (7, 2), (9, 3)):
        @at(mark)
        def _():
            start_across(k)

    ticks(
        (0, 0, 0), (2, 1, 0), (6, 2, 0), (6, 0, 1), (8, 3, 0), (8, 1, 1), (10, 2, 1), (13, 3, 1),
    )

    @at(7)
    def _():
        halve_square()

    @at(8)
    def _():
        for n in range(1, len(pairs)):
            load(n).wait()

    @at(11)
    def _():
        spread_square()

    @at(12)
    def _():
        collect_mlp()

    @at(15)
    def _():
        start_small()

    @at(16)
    def _():
        turn_small()
        sum_square()

    @when(*DESCEND)
    def _():
        descend(jnp.where(i < 2, i, i - 4))

    @when(*PROJECT)
    def _():
        project()

    @at(PROJECT[-1])
    def _():
        cut_square()

    @when(*CLOSE)
    def _():
        close(jnp.where(i < 10, i - 8, jnp.where(i < 14, 2, 3)))

    @when(*FINISH)
    def _():
        finish(jnp.where(i < 12, i - 10, i - 11))

    @when(*BACK)
    def _():
        back(i - BACK[0])

    @at(BACK[-1])
    def _():
        settle()
        end_small()
        collect_square()


def tail(
    x, cot, seg, att, gq, bg, normed, kcot, first, first_across, second, second_across, gub, mlp, ow,
    down, up, qw, pack, kw, cos, sin, act, gh, parts, owners, count=2,
):
    rows, width, blk = att.shape
    tok, ff, kvw = rows * blk, up.shape[1], kw.shape[1]
    tiles = tok // (count * blk)
    planes = owners // 2
    high, cols, tall = width // owners // 2, width // 2, width // owners
    once = lambda *shape: pl.BlockSpec(
        shape, lambda i: (0,) * len(shape), pipeline_mode=pl.Buffered(1)
    )
    anywhere = pl.BlockSpec(memory_space=pl.ANY)
    s = rows // count
    one, descent, third, last = stair(PROJECT), stair(DESCEND), stair(FINISH), stair(BACK)
    closing, every = stair(CLOSE), stair(DESCEND, CLOSE, FINISH, BACK)
    heads, queries = stair(PROJECT, CLOSE), stair(PROJECT, FINISH)
    flat = lambda of: pl.BlockSpec((count * blk, width), lambda i: (of(i), 0))
    single = pl.BlockSpec(
        (count * blk, width), lambda i: (last(i), 0), pipeline_mode=pl.Buffered(1)
    )
    stack = lambda of, h, w: pl.BlockSpec((count, h, w), lambda i: (of(i), 0, 0))
    wide = lambda of: [
        pl.BlockSpec((count * blk, ff // parts), lambda i, c=c: (c * tiles + of(i) + 1, 0))
        for c in range(parts)
    ]
    dma = pltpu.SemaphoreType.DMA
    vmem = lambda kind, *shape: pltpu.VMEM(shape, kind)
    return pl.pallas_call(
        partial(tail_kernel, rows=rows, parts=parts, owners=owners),
        grid=(BACK[-1] + 1,),
        in_specs=[
            flat(every), single, once(rows, blk), stack(heads, width, blk),
            stack(queries, width, blk), flat(one), flat(one), stack(third, blk, kvw), anywhere,
            anywhere, anywhere, anywhere, once(parts, 1, ff // parts), once(*mlp.shape), anywhere,
            anywhere, anywhere, anywhere, once(*pack.shape), once(width, kvw), once(ROT_HALF, blk),
            once(ROT_HALF, blk),
        ] + wide(closing) + wide(descent),
        out_specs=[
            flat(closing), single, anywhere, anywhere, anywhere, anywhere, once(tall, kvw),
            once(16, 128),
        ],
        out_shape=[
            jax.ShapeDtypeStruct((tok, width), bf16),
            jax.ShapeDtypeStruct((tok, width), bf16),
            jax.ShapeDtypeStruct((tall, width), f32),
            jax.ShapeDtypeStruct((tall, width), f32),
            jax.ShapeDtypeStruct((tall, ff), f32),
            jax.ShapeDtypeStruct((ff // owners, width), f32),
            jax.ShapeDtypeStruct((tall, kvw), f32),
            jax.ShapeDtypeStruct((16, 128), f32),
        ],
        scratch_shapes=[
            vmem(bf16, width, width), vmem(bf16, ff, width), vmem(bf16, width, ff),
            vmem(bf16, width, width),
            vmem(f32, 2, width, width), vmem(f32, s, count * blk, width),
            vmem(f32, kvw, width), vmem(f32, 16, width),
            vmem(bf16, planes, rows, blk, kvw), vmem(bf16, planes, rows, blk, kvw),
            vmem(bf16, planes - 1, rows, blk, kvw), vmem(f32, rows, blk, kvw),
            vmem(f32, 2, tall, width), vmem(bf16, parts, *mlp.shape),
            vmem(bf16, 2, owners, 2, high, cols), vmem(bf16, 2, owners, 2, high, cols),
            vmem(bf16, owners, 2, high, cols),
            vmem(bf16, owners, 2, high, cols), vmem(bf16, owners - 1, 2, high, cols),
            vmem(bf16, parts, 2, high, cols),
            vmem(bf16, owners, tall, kvw), vmem(bf16, owners, 16, 128),
            vmem(bf16, owners - 1, tall, kvw), vmem(bf16, owners - 1, 16, 128),
            vmem(bf16, tall, kvw), vmem(bf16, 16, 128),
            vmem(bf16, parts - 1, tall, kvw), vmem(bf16, parts - 1, 16, 128),
            dma((4,)), dma((2,)), dma((2 * planes,)), dma((planes,)), dma((2, planes)), dma((2, 2 * planes)),
            dma((2, parts - 1)), dma((2, 1)), dma((2, 1)),
            dma((2, owners - 1)), dma((2, parts - 1)), dma((2, owners - 1)), dma((2, owners - 1)),
            dma((2, parts - 1)), dma((2, parts - 1)),
        ],
        compiler_params=params(63, collective_id=1, has_side_effects=True),
        cost_estimate=cost(4 * tok * width * (2 * width + ff), 4 * tok * ff + 20 * tok * width),
        name="tail",
    )(
        x, cot, seg, att, gq, bg, normed, kcot, first, first_across, second, second_across, gub, mlp,
        ow, down, up, qw, pack, kw, cos, sin, *[act] * parts, *[gh] * parts,
    )


def deliver_kernel(*refs):
    half = len(refs) // 2
    for source, target in zip(refs[:half], refs[half:]):
        target[...] = source[...]


def deliver(*arrays, pieces=4):
    def split(array):
        high, wide = array.shape
        return pl.BlockSpec((high // pieces, wide), lambda i: (i, 0))

    return pl.pallas_call(
        deliver_kernel,
        grid=(pieces,),
        in_specs=[split(array) for array in arrays],
        out_specs=[split(array) for array in arrays],
        out_shape=[jax.ShapeDtypeStruct(array.shape, array.dtype) for array in arrays],
        compiler_params=params(60),
        cost_estimate=cost(0, 2e7),
        name="deliver",
    )(*arrays)


def attn_kernel(first_ref, sidx_ref, q_ref, do_ref, kv_ref, start_ref,
                cos_ref, sin_ref, *refs, blk, nblk, begin):
    att_ref, gq_ref, own_ref, other_ref, p_s, m_s, bias_s, o_s, mx, ls, dq_s, dc_s, ic_s, inn_s = refs[-14:]
    r = begin + pl.program_id(0)
    e = sidx_ref[0]
    n = e - first_ref[r] + 1
    start = start_ref[pl.ds(r, 1), :]
    qpos = e*blk + lax.broadcasted_iota(jnp.int32,(1,blk),1)
    krow = lax.broadcasted_iota(jnp.int32,(blk,blk),0)

    def hsl(h):
        return slice(h*blk,(h+1)*blk)

    def put(j, block):
        @pl.when(lax.rem(j + e, 2) == 0)
        def _():
            own_ref[j // 2, 0] = block

        @pl.when(lax.rem(j + e, 2) == 1)
        def _():
            other_ref[j // 2, 0] = block

    @pl.loop(0, nblk)
    def _(j):
        @pl.when((j < first_ref[r]) | (j > e))
        def _():
            put(j, jnp.zeros((blk,2*HEAD_DIM),bf16))

    def forward(jj):
        j = e - jj
        kvj = kv_ref[j, 0, 0:blk, :]
        key = kvj[:, :HEAD_DIM]
        vt = kvj.T[HEAD_DIM:,:]
        kpos = j*blk + krow
        bias_s[...] = jnp.where((kpos>=start)&(kpos<=qpos), 0.0, negative)
        sv = {}; pv = {}; av = {}
        for h in range(HEADS+3):
            if h < HEADS:
                sv[h] = nn(key, q_ref[0,:,hsl(h)])
            g = h-2
            if 0 <= g < HEADS:
                hs = hsl(g)
                s = sv.pop(g)*LOG2E + bias_s[...]
                top = jnp.max(s,axis=0,keepdims=True)
                mo = mx[:,hs]
                mn = jnp.maximum(mo, top)
                p = jnp.exp2(s-mn)
                av[g] = jnp.exp2(mo-mn)
                ls[:,hs] = ls[:,hs]*av[g] + jnp.sum(p,axis=0,keepdims=True)
                pv[g] = p.astype(bf16)
                p_s[jj,:,hs] = pv[g]
                m_s[jj,:,hs] = mn
                mx[:,hs] = mn
            g = h-3
            if 0 <= g < HEADS:
                hs = hsl(g)
                new = nn(vt,pv.pop(g))
                o_s[:,hs] = o_s[:,hs]*av.pop(g) + new

    half = blk//2

    def upper(h):
        return slice(h*blk+half,(h+1)*blk)

    def joined(get, pair):
        return jnp.concatenate([get(upper(2*pair)), get(upper(2*pair+1))],axis=1)

    def own_forward():
        kvj = kv_ref[e, 0, 0:blk, :]
        key = kvj[:, :HEAD_DIM]
        vt = kvj.T[HEAD_DIM:,:]
        bias_s[...] = jnp.where((e*blk+krow>=start)&(e*blk+krow<=qpos), 0.0, negative)
        low, high, pl_, ph = {}, {}, {}, {}
        pairs = HEADS//2
        for n in range(pairs+2):
            if n < pairs:
                for h in (2*n, 2*n+1):
                    low[h] = nn(key[:half], q_ref[0,:,hsl(h)])
                high[n] = nn(key[half:], joined(lambda at: q_ref[0,:,at], n))
            m = n-1
            if 0 <= m < pairs:
                two = high.pop(m)
                top_part = []
                for k in (0, 1):
                    h = 2*m+k
                    hs = hsl(h)
                    s = low.pop(h)*LOG2E + bias_s[0:half,:]
                    u = two[:,k*half:(k+1)*half]*LOG2E + bias_s[half:,half:]
                    top = jnp.max(s,axis=0,keepdims=True)
                    rest = jnp.maximum(top[:,half:], jnp.max(u,axis=0,keepdims=True))
                    mn = jnp.concatenate([top[:,:half], rest],axis=1)
                    p = jnp.exp2(s-mn)
                    v = jnp.exp2(u-rest)
                    total = jnp.sum(p,axis=0,keepdims=True)
                    more = total[:,half:] + jnp.sum(v,axis=0,keepdims=True)
                    ls[:,hs] = jnp.concatenate([total[:,:half], more],axis=1)
                    pl_[h] = p.astype(bf16)
                    p_s[0,0:half,hs] = pl_[h]
                    v = v.astype(bf16)
                    p_s[0,half:,upper(h)] = v
                    top_part.append(v)
                    m_s[0,:,hs] = mn
                    mx[:,hs] = mn
                ph[m] = jnp.concatenate(top_part,axis=1)
            m = n-2
            if 0 <= m < pairs:
                two = nn(vt[:,half:], ph.pop(m))
                for k in (0, 1):
                    h = 2*m+k
                    first = nn(vt[:,:half], pl_.pop(h))
                    o_s[:,hsl(h)] = jnp.concatenate(
                        [first[:,:half], first[:,half:]+two[:,k*half:(k+1)*half]],axis=1)

    own_forward()

    @pl.loop(1, n)
    def _(jj):
        forward(jj)

    for h in range(HEADS):
        hs = hsl(h)
        inv = 1.0/ls[:,hs]
        ls[:,hs] = inv
        o = o_s[:,hs]*inv
        att_ref[0, h*HEAD_DIM:(h+1)*HEAD_DIM, :] = o.astype(bf16)
        inn_s[:,hs] = jnp.sum(o*do_ref[0,:,hs].astype(f32),axis=0,keepdims=True)

    def backward(jj):
        j = e - jj
        kvj = kv_ref[j, 0, 0:blk, :]
        value = kvj[:, HEAD_DIM:]
        kt = kvj.T[:HEAD_DIM,:]
        for h in range(HEADS):
            hs = hsl(h)
            c = jnp.exp2(m_s[jj,:,hs]-mx[:,hs])*ls[:,hs]
            dc_s[:,hs] = (do_ref[0,:,hs].astype(f32)*c).astype(bf16)
            ic_s[:,hs] = inn_s[:,hs]*c
        dpv = {}; dsv = {}; pbv = {}
        dk = dv = None
        for h in range(HEADS+4):
            if h < HEADS:
                dpv[h] = nn(value, dc_s[:,hsl(h)])
            g = h-2
            if 0 <= g < HEADS:
                hs = hsl(g)
                pb = p_s[jj,:,hs]
                dsv[g] = (pb.astype(f32)*(dpv.pop(g)-ic_s[:,hs])).astype(bf16)
                new = nt(pb, dc_s[:,hs])
                dv = new if dv is None else dv + new
            g = h-4
            if 0 <= g < HEADS:
                hs = hsl(g)
                ds = dsv.pop(g)
                new = nn(kt, ds)
                dq_s[:,hs] = dq_s[:,hs] + new
                new = nt(ds, q_ref[0,:,hs])
                dk = new if dk is None else dk + new
        put(j, jnp.concatenate([dk,dv],axis=1).astype(bf16))

    def own_backward():
        kvj = kv_ref[e, 0, 0:blk, :]
        value = kvj[:, HEAD_DIM:]
        kt = kvj.T[:HEAD_DIM,:]
        for h in range(HEADS):
            hs = hsl(h)
            c = jnp.exp2(m_s[0,:,hs]-mx[:,hs])*ls[:,hs]
            dc_s[:,hs] = (do_ref[0,:,hs].astype(f32)*c).astype(bf16)
            ic_s[:,hs] = inn_s[:,hs]*c
        low, high, dl, dh = {}, {}, {}, {}
        dk = [None, None]
        dv = [None, None]

        def add(sums, at, new):
            sums[at] = new if sums[at] is None else sums[at] + new

        pairs = HEADS//2
        for n in range(pairs+2):
            if n < pairs:
                for h in (2*n, 2*n+1):
                    low[h] = nn(value[:half], dc_s[:,hsl(h)])
                high[n] = nn(value[half:], joined(lambda at: dc_s[:,at], n))
            m = n-1
            if 0 <= m < pairs:
                for h in (2*m, 2*m+1):
                    hs = hsl(h)
                    pb = p_s[0,0:half,hs]
                    dl[h] = (pb.astype(f32)*(low.pop(h)-ic_s[:,hs])).astype(bf16)
                    add(dv, 0, nt(pb, dc_s[:,hs]))
                pb = joined(lambda at: p_s[0,half:,at], m)
                dh[m] = (pb.astype(f32)*(high.pop(m)-joined(lambda at: ic_s[:,at], m))).astype(bf16)
                add(dv, 1, nt(pb, joined(lambda at: dc_s[:,at], m)))
            m = n-2
            if 0 <= m < pairs:
                ds = dh.pop(m)
                two = nn(kt[:,half:], ds)
                add(dk, 1, nt(ds, joined(lambda at: q_ref[0,:,at], m)))
                for k in (0, 1):
                    h = 2*m+k
                    ds = dl.pop(h)
                    first = nn(kt[:,:half], ds)
                    dq_s[:,hsl(h)] = jnp.concatenate(
                        [first[:,:half], first[:,half:]+two[:,k*half:(k+1)*half]],axis=1)
                    add(dk, 0, nt(ds, q_ref[0,:,hsl(h)]))
        put(e, jnp.concatenate(
            [jnp.concatenate(dk,axis=0), jnp.concatenate(dv,axis=0)],axis=1).astype(bf16))

    own_backward()

    @pl.loop(1, n)
    def _(jj):
        backward(jj)

    cos = cos_ref[...]; sin = sin_ref[...]
    for h in range(HEADS):
        g = dq_s[:, hsl(h)]*(HEAD_DIM**-0.5)
        a, b = g[0:8], g[8:16]
        gq_ref[0, h*HEAD_DIM:(h+1)*HEAD_DIM, :] = jnp.concatenate([a*cos+b*sin, b*cos-a*sin, g[16:]],axis=0).astype(bf16)


def attention(first, sidx, queries, upstream, kv, start, cos, sin, begin, count, before=()):
    rows, _, wide = queries.shape
    nblk, blk = kv.shape[0], wide // HEADS
    stack = lambda high, across: pl.BlockSpec((1, high, across), lambda r, *_: (begin + r, 0, 0))
    held = jax.ShapeDtypeStruct((rows, HEADS * HEAD_DIM, blk), bf16)
    specs = pltpu.PrefetchScalarGridSpec(
        num_scalar_prefetch=2,
        grid=(count,),
        in_specs=[
            stack(HEAD_DIM, wide), stack(HEAD_DIM, wide),
            pl.BlockSpec((nblk, 1, blk + 16, 2 * HEAD_DIM), lambda r, *_: (0, begin + r, 0, 0)),
            whole(rows, blk), whole(ROT_HALF, blk), whole(ROT_HALF, blk),
        ] + [pl.BlockSpec(memory_space=pl.ANY)] * len(before),
        out_specs=[
            stack(HEADS * HEAD_DIM, blk), stack(HEADS * HEAD_DIM, blk),
        ] + [pl.BlockSpec((nblk // 2, 1, blk, 2 * HEAD_DIM), lambda r, *_: (0, r, 0, 0))] * 2,
        scratch_shapes=[
            pltpu.VMEM((nblk, blk, wide), bf16), pltpu.VMEM((nblk, 1, wide), f32),
            pltpu.VMEM((blk, blk), f32), pltpu.VMEM((HEAD_DIM, wide), f32),
            pltpu.VMEM((1, wide), f32), pltpu.VMEM((1, wide), f32),
            pltpu.VMEM((HEAD_DIM, wide), f32), pltpu.VMEM((HEAD_DIM, wide), bf16),
            pltpu.VMEM((1, wide), f32), pltpu.VMEM((1, wide), f32),
        ],
    )
    return pl.pallas_call(
        partial(attn_kernel, blk=blk, nblk=nblk, begin=begin),
        out_shape=[held, held]
        + [jax.ShapeDtypeStruct((nblk // 2, count, blk, 2 * HEAD_DIM), bf16)] * 2,
        grid_spec=specs,
        input_output_aliases={8 + n: n for n in range(len(before))},
        compiler_params=params(60),
        cost_estimate=cost(6e9 * count, 5e6 * count),
        name="attention",
    )(first, sidx, queries, upstream, kv, start, cos, sin, *before)


def local(
    tokens,
    segment_ids,
    query_weight,
    query_bias,
    keyval_weight,
    keyval_bias,
    out_weight,
    out_bias,
    up_weight,
    up_bias,
    down_weight,
    down_bias,
    attention_gain,
    attention_shift,
    dense_gain,
    dense_shift,
    out_cotangent,
    keyval_cotangent,
):
    rows, blk, width = tokens.shape
    ff = up_weight.shape[1]
    kvw = 2 * HEAD_DIM
    tok = rows * blk
    owners, parts = lax.axis_size("seq"), lax.axis_size("batch")
    place = lax.axis_index("seq")
    cos, sin = rotary_tables(place * blk + jnp.arange(blk, dtype=jnp.int32))
    cos, sin = cos.T, sin.T
    x = tokens.reshape(tok, width)
    cot = out_cotangent.reshape(tok, width)
    lines = [
        attention_gain, attention_shift, dense_gain, dense_shift, query_bias, out_bias, down_bias,
        jnp.pad(keyval_bias, (0, width - kvw)),
    ] + [up_bias[at : at + width] for at in range(0, ff, width)]
    line = lax.broadcasted_iota(jnp.int32, (16, width), 0)
    pack = jnp.zeros((16, width), f32)
    for n, values in enumerate(lines):
        pack = jnp.where(line == n, values[None, :], pack)

    normed, dense_in, branch_grad, keyval, keyval_out = norms(
        x, cot, segment_ids, pack, keyval_weight, cos, sin
    )
    act, grad_hidden, mlp, gub, queries, grad_attended, keyval_all = dense(
        dense_in, branch_grad, up_weight, down_weight, normed, pack, query_weight, out_weight, cos,
        sin, keyval, parts, owners,
    )
    mlp = lax.psum_scatter(mlp, "seq", scatter_dimension=0)

    ids = keyval_all[:, :, blk : blk + blk // 128, :].reshape(owners, rows, blk).astype(f32)
    before = (jnp.arange(owners) <= place)[:, None, None]
    order = lambda values: jnp.where(values < 0, 1024.0, values)
    ids = jnp.where(before, order(ids), 2048.0)
    start = jnp.sum(
        (ids[:, :, None, :] < order(segment_ids.astype(f32))[None, :, :, None]).astype(jnp.int32),
        axis=(0, 3),
    ).astype(jnp.int32)
    first_block = start[:, 0] // blk
    index = place.astype(jnp.int32)[None]
    run = partial(
        attention, first_block, index, queries, grad_attended, keyval_all, start, cos, sin,
        count=rows // 2,
    )
    attended, grad_query, first, first_other = run(begin=0)
    across = lax.ppermute(first_other, "seq", [(i, i ^ 1) for i in range(owners)])
    attended, grad_query, own, other = run(begin=rows // 2, before=(attended, grad_query))
    (
        layer_out, grad_tokens, grad_out_weight, grad_query_weight, grad_up_weight,
        grad_down_weight, grad_keyval_weight, vectors,
    ) = tail(
        x, cot, segment_ids, attended, grad_query, branch_grad, normed, keyval_cotangent,
        first, across, own, other, gub, mlp, out_weight, down_weight, up_weight, query_weight,
        pack, keyval_weight, cos, sin, act, grad_hidden, parts, owners,
    )
    (
        layer_out, grad_tokens, grad_out_weight, grad_query_weight, grad_up_weight,
        grad_down_weight, grad_keyval_weight,
    ) = deliver(
        layer_out, grad_tokens, grad_out_weight, grad_query_weight, grad_up_weight,
        grad_down_weight, grad_keyval_weight,
    )
    share = width // owners
    query_bias_grad, branch_sum, ag, ash, dg, dsh = [vectors[n, :share] for n in range(6)]
    return (
        layer_out.reshape(rows, blk, width),
        keyval_out,
        grad_tokens.reshape(rows, blk, width),
        grad_query_weight,
        query_bias_grad,
        grad_keyval_weight,
        lax.dynamic_slice(vectors[11], (place * (kvw // owners),), (kvw // owners,)),
        grad_out_weight,
        branch_sum,
        grad_up_weight,
        vectors[8:11].reshape(ff // owners),
        grad_down_weight,
        branch_sum,
        ag,
        ash,
        dg,
        dsh,
    )


def choose(tokens, *rest):
    rows, blk, width = tokens.shape
    fits = blk == 256 and rows == 8 and rest[7].shape == (width, 4 * width) and width % 256 == 0
    fits = fits and lax.axis_size("batch") == 4 and lax.axis_size("seq") == 8
    return (local if fits else local_plain)(tokens, *rest)


def solution(mesh):
    placed = (
        P("batch", "seq", None),
        P("batch", "seq"),
        P(),
        P(),
        P(),
        P(),
        P(),
        P(),
        P(),
        P(),
        P(),
        P(),
        P(),
        P(),
        P(),
        P(),
        P("batch", "seq", None),
        P("batch", "seq", None),
    )
    return jax.shard_map(
        choose,
        mesh=mesh,
        in_specs=placed,
        out_specs=(
            P("batch", "seq", None),
            P("batch", "seq", None),
            P("batch", "seq", None),
            P("seq", None),
            P("seq"),
            P("seq", None),
            P("seq"),
            P("seq", None),
            P("seq"),
            P("seq", None),
            P("seq"),
            P("seq", None),
            P("seq"),
            P("seq"),
            P("seq"),
            P("seq"),
            P("seq"),
        ),
        check_vma=False,
    )
```

```python
from functools import partial

import jax
import jax.numpy as jnp
from jax import lax
from jax.experimental import pallas as pl
from jax.experimental.pallas import tpu as pltpu
from jax.sharding import PartitionSpec as P

HEADS = 12
HEAD_DIM = 64
ROT = 16
LOG2E = 1.4426950408889634
f32 = jnp.float32
bf16 = jnp.bfloat16


epsilon = 1e-05
rope_base = 10000.0
negative = -1e30


def layer_norm(values, gain_vector, shift_vector):
    average = jnp.mean(values, axis=-1, keepdims=True)
    centred = values - average
    variance = jnp.mean(centred * centred, axis=-1, keepdims=True)
    return centred * lax.rsqrt(variance + epsilon) * gain_vector + shift_vector


def rotary_tables(positions):
    half_rot = ROT // 2
    frequency = rope_base ** (-(2.0 * jnp.arange(half_rot, dtype=jnp.float32)) / ROT)
    angles = positions.astype(jnp.float32)[:, None] * frequency[None, :]
    return (jnp.cos(angles), jnp.sin(angles))


def rotate(values, cos_table, sin_table):
    half_rot = ROT // 2
    first_half = values[..., :half_rot]
    second_half = values[..., half_rot:ROT]
    return jnp.concatenate(
        [
            first_half * cos_table - second_half * sin_table,
            second_half * cos_table + first_half * sin_table,
            values[..., ROT:],
        ],
        axis=-1,
    )


def unrotate(values, cos_table, sin_table):
    half_rot = ROT // 2
    first_half = values[..., :half_rot]
    second_half = values[..., half_rot:ROT]
    return jnp.concatenate(
        [
            first_half * cos_table + second_half * sin_table,
            second_half * cos_table - first_half * sin_table,
            values[..., ROT:],
        ],
        axis=-1,
    )


def contract_rows(left_side, right_side):
    return lax.dot_general(
        left_side, right_side, (((0,), (0,)), ((), ())), preferred_element_type=jnp.float32
    )


def contract_cols(left_side, right_side):
    return lax.dot_general(
        left_side, right_side, (((1,), (1,)), ((), ())), preferred_element_type=jnp.float32
    )


def local_plain(
    tokens,
    segment_ids,
    query_weight,
    query_bias,
    keyval_weight,
    keyval_bias,
    out_weight,
    out_bias,
    up_weight,
    up_bias,
    down_weight,
    down_bias,
    attention_gain,
    attention_shift,
    dense_gain,
    dense_shift,
    out_cotangent,
    keyval_cotangent,
):
    rows, local_len, width = tokens.shape
    full_len = local_len * lax.axis_size("seq")
    tok_count = rows * local_len
    offset = lax.axis_index("seq") * local_len
    positions = offset + jnp.arange(local_len, dtype=jnp.int32)
    key_positions = jnp.arange(full_len, dtype=jnp.int32)
    score_scale = HEAD_DIM ** (-0.5)
    inputs = tokens.astype(jnp.float32).reshape(tok_count, width)
    valid_rows = (segment_ids >= 0).astype(jnp.float32).reshape(tok_count, 1)
    normed_full, attention_pull = jax.vjp(layer_norm, inputs, attention_gain, attention_shift)
    normed = normed_full.astype(jnp.bfloat16)
    query_pre = jnp.dot(normed, query_weight, preferred_element_type=jnp.float32) + query_bias
    keyval_pre = jnp.dot(normed, keyval_weight, preferred_element_type=jnp.float32) + keyval_bias
    cos_table, sin_table = rotary_tables(positions)
    queries = rotate(
        query_pre.reshape(rows, local_len, HEADS, HEAD_DIM),
        cos_table[:, None, :],
        sin_table[:, None, :],
    ).astype(jnp.bfloat16)
    queries = queries.transpose(0, 2, 1, 3).reshape(rows, HEADS * local_len, HEAD_DIM)
    key_part = keyval_pre[:, :HEAD_DIM].reshape(rows, local_len, HEAD_DIM)
    value_part = keyval_pre[:, HEAD_DIM:].reshape(rows, local_len, HEAD_DIM)
    keyval_local = jnp.concatenate(
        [rotate(key_part, cos_table, sin_table), value_part], axis=-1
    ).astype(jnp.bfloat16)
    keyval_all, segment_all = (
        lax.all_gather(keyval_local, "seq", axis=1, tiled=True),
        lax.all_gather(segment_ids, "seq", axis=1, tiled=True),
    )

    def scores_of(query_rows, key_rows, segment_row, segment_keys):
        scores = contract_cols(query_rows, key_rows) * score_scale
        allowed = (positions[:, None] >= key_positions[None, :]) & (
            segment_row[:, None] == segment_keys[None, :]
        )
        scores = scores.reshape(HEADS, local_len, full_len)
        return jnp.where(allowed[None], scores, negative)

    def forward_row(pieces):
        query_rows, keyval_row, segment_row, segment_keys = pieces
        scores = scores_of(query_rows, keyval_row[:, :HEAD_DIM], segment_row, segment_keys)
        top_score = jnp.max(scores, axis=-1, keepdims=True)
        expanded = jnp.exp(scores - top_score)
        row_total = jnp.sum(expanded, axis=-1, keepdims=True)
        weights = (expanded / row_total).reshape(HEADS * local_len, full_len).astype(jnp.bfloat16)
        attended_row = jnp.dot(
            weights, keyval_row[:, HEAD_DIM:], preferred_element_type=jnp.float32
        ).astype(jnp.bfloat16)
        log_total = (top_score + jnp.log(row_total)).reshape(HEADS * local_len)
        return (attended_row, log_total)

    attended, log_totals = lax.map(forward_row, (queries, keyval_all, segment_ids, segment_all))
    attended_flat = (
        attended.reshape(rows, HEADS, local_len, HEAD_DIM)
        .transpose(0, 2, 1, 3)
        .reshape(tok_count, width)
    )
    attn_out = jnp.dot(attended_flat, out_weight, preferred_element_type=jnp.float32) + out_bias
    dense_full, dense_pull = jax.vjp(layer_norm, inputs, dense_gain, dense_shift)
    dense_in = dense_full.astype(jnp.bfloat16)
    hidden = jnp.dot(dense_in, up_weight, preferred_element_type=jnp.float32) + up_bias
    activated_full, gelu_pull = jax.vjp(partial(jax.nn.gelu, approximate=False), hidden)
    activated = activated_full.astype(jnp.bfloat16)
    dense_out = jnp.dot(activated, down_weight, preferred_element_type=jnp.float32) + down_bias
    layer_out = (
        (inputs + valid_rows * (attn_out + dense_out))
        .astype(jnp.bfloat16)
        .reshape(rows, local_len, width)
    )
    upstream = out_cotangent.astype(jnp.float32).reshape(tok_count, width)
    branch_full = valid_rows * upstream
    branch_grad = branch_full.astype(jnp.bfloat16)
    branch_sum = jnp.sum(branch_full, axis=0)
    grad_out_weight = contract_rows(attended_flat, branch_grad)
    grad_down_weight = contract_rows(activated, branch_grad)
    (grad_hidden_full,) = gelu_pull(contract_cols(branch_grad, down_weight))
    grad_hidden = grad_hidden_full.astype(jnp.bfloat16)
    grad_up_weight = contract_rows(dense_in, grad_hidden)
    grad_up_bias = jnp.sum(grad_hidden.astype(jnp.float32), axis=0)
    grad_dense_in = contract_cols(grad_hidden, up_weight)
    dense_back, grad_dense_gain, grad_dense_shift = dense_pull(grad_dense_in)
    grad_attended = contract_cols(branch_grad, out_weight).astype(jnp.bfloat16)
    grad_attended = (
        grad_attended.reshape(rows, local_len, HEADS, HEAD_DIM)
        .transpose(0, 2, 1, 3)
        .reshape(rows, HEADS * local_len, HEAD_DIM)
    )
    keyval_back, segment_back = (
        lax.all_gather(keyval_local, "seq", axis=1, tiled=True),
        lax.all_gather(segment_ids, "seq", axis=1, tiled=True),
    )

    def backward_row(pieces):
        query_rows, keyval_row, segment_row, segment_keys, log_row, grad_rows = pieces
        key_rows = keyval_row[:, :HEAD_DIM]
        value_rows = keyval_row[:, HEAD_DIM:]
        scores = scores_of(query_rows, key_rows, segment_row, segment_keys)
        probs = jnp.exp(scores - log_row.reshape(HEADS, local_len, 1)).reshape(
            HEADS * local_len, full_len
        )
        grad_probs = contract_cols(grad_rows, value_rows)
        inner = jnp.sum(probs * grad_probs, axis=-1, keepdims=True)
        grad_scores = (probs * (grad_probs - inner)).astype(jnp.bfloat16)
        grad_query_rows = (
            jnp.dot(grad_scores, key_rows, preferred_element_type=jnp.float32) * score_scale
        )
        grad_key_rows = contract_rows(grad_scores, query_rows) * score_scale
        grad_value_rows = contract_rows(probs.astype(jnp.bfloat16), grad_rows)
        return (grad_query_rows, jnp.concatenate([grad_key_rows, grad_value_rows], axis=-1))

    grad_queries, keyval_terms = lax.map(
        backward_row, (queries, keyval_back, segment_ids, segment_back, log_totals, grad_attended)
    )
    keyval_grad = lax.psum_scatter(
        keyval_terms.astype(jnp.bfloat16), "seq", scatter_dimension=1, tiled=True
    ).astype(jnp.float32) + keyval_cotangent.astype(jnp.float32)
    grad_key_pre = unrotate(keyval_grad[..., :HEAD_DIM], cos_table, sin_table)
    grad_keyval_pre = (
        jnp.concatenate([grad_key_pre, keyval_grad[..., HEAD_DIM:]], axis=-1)
        .reshape(tok_count, 2 * HEAD_DIM)
        .astype(jnp.bfloat16)
    )
    grad_queries = grad_queries.reshape(rows, HEADS, local_len, HEAD_DIM).transpose(0, 2, 1, 3)
    grad_query_pre = (
        unrotate(grad_queries, cos_table[:, None, :], sin_table[:, None, :])
        .reshape(tok_count, width)
        .astype(jnp.bfloat16)
    )
    grad_query_weight = contract_rows(normed, grad_query_pre)
    grad_query_bias = jnp.sum(grad_query_pre.astype(jnp.float32), axis=0)
    grad_keyval_weight = contract_rows(normed, grad_keyval_pre)
    grad_keyval_bias = jnp.sum(grad_keyval_pre.astype(jnp.float32), axis=0)
    grad_normed = contract_cols(grad_query_pre, query_weight) + contract_cols(
        grad_keyval_pre, keyval_weight
    )
    attention_back, grad_attention_gain, grad_attention_shift = attention_pull(grad_normed)
    grad_tokens = (
        (upstream + attention_back + dense_back)
        .astype(jnp.bfloat16)
        .reshape(rows, local_len, width)
    )
    local_grads = (
        grad_query_weight,
        grad_query_bias,
        grad_keyval_weight,
        grad_keyval_bias,
        grad_out_weight,
        branch_sum,
        grad_up_weight,
        grad_up_bias,
        grad_down_weight,
        branch_sum,
        grad_attention_gain,
        grad_attention_shift,
        grad_dense_gain,
        grad_dense_shift,
    )
    shares = (
        lax.psum_scatter(
            local_grads[0].astype(jnp.bfloat16), "seq", scatter_dimension=0, tiled=True
        ).astype(jnp.float32),
        lax.psum_scatter(
            local_grads[1].astype(jnp.bfloat16), "seq", scatter_dimension=0, tiled=True
        ).astype(jnp.float32),
        lax.psum_scatter(
            local_grads[2].astype(jnp.bfloat16), "seq", scatter_dimension=0, tiled=True
        ).astype(jnp.float32),
        lax.psum_scatter(
            local_grads[3].astype(jnp.bfloat16), "seq", scatter_dimension=0, tiled=True
        ).astype(jnp.float32),
        lax.psum_scatter(
            local_grads[4].astype(jnp.bfloat16), "seq", scatter_dimension=0, tiled=True
        ).astype(jnp.float32),
        lax.psum_scatter(
            local_grads[5].astype(jnp.bfloat16), "seq", scatter_dimension=0, tiled=True
        ).astype(jnp.float32),
        lax.psum_scatter(
            local_grads[6].astype(jnp.bfloat16), "seq", scatter_dimension=0, tiled=True
        ).astype(jnp.float32),
        lax.psum_scatter(
            local_grads[7].astype(jnp.bfloat16), "seq", scatter_dimension=0, tiled=True
        ).astype(jnp.float32),
        lax.psum_scatter(
            local_grads[8].astype(jnp.bfloat16), "seq", scatter_dimension=0, tiled=True
        ).astype(jnp.float32),
        lax.psum_scatter(
            local_grads[9].astype(jnp.bfloat16), "seq", scatter_dimension=0, tiled=True
        ).astype(jnp.float32),
        lax.psum_scatter(
            local_grads[10].astype(jnp.bfloat16), "seq", scatter_dimension=0, tiled=True
        ).astype(jnp.float32),
        lax.psum_scatter(
            local_grads[11].astype(jnp.bfloat16), "seq", scatter_dimension=0, tiled=True
        ).astype(jnp.float32),
        lax.psum_scatter(
            local_grads[12].astype(jnp.bfloat16), "seq", scatter_dimension=0, tiled=True
        ).astype(jnp.float32),
        lax.psum_scatter(
            local_grads[13].astype(jnp.bfloat16), "seq", scatter_dimension=0, tiled=True
        ).astype(jnp.float32),
    )
    totals = (
        lax.psum(shares[0].astype(jnp.bfloat16), "batch").astype(jnp.float32),
        lax.psum(shares[1].astype(jnp.bfloat16), "batch").astype(jnp.float32),
        lax.psum(shares[2].astype(jnp.bfloat16), "batch").astype(jnp.float32),
        lax.psum(shares[3].astype(jnp.bfloat16), "batch").astype(jnp.float32),
        lax.psum(shares[4].astype(jnp.bfloat16), "batch").astype(jnp.float32),
        lax.psum(shares[5].astype(jnp.bfloat16), "batch").astype(jnp.float32),
        lax.psum(shares[6].astype(jnp.bfloat16), "batch").astype(jnp.float32),
        lax.psum(shares[7].astype(jnp.bfloat16), "batch").astype(jnp.float32),
        lax.psum(shares[8].astype(jnp.bfloat16), "batch").astype(jnp.float32),
        lax.psum(shares[9].astype(jnp.bfloat16), "batch").astype(jnp.float32),
        lax.psum(shares[10].astype(jnp.bfloat16), "batch").astype(jnp.float32),
        lax.psum(shares[11].astype(jnp.bfloat16), "batch").astype(jnp.float32),
        lax.psum(shares[12].astype(jnp.bfloat16), "batch").astype(jnp.float32),
        lax.psum(shares[13].astype(jnp.bfloat16), "batch").astype(jnp.float32),
    )
    return (
        layer_out,
        keyval_local,
        grad_tokens,
        totals[0],
        totals[1],
        totals[2],
        totals[3],
        totals[4],
        totals[5],
        totals[6],
        totals[7],
        totals[8],
        totals[9],
        totals[10],
        totals[11],
        totals[12],
        totals[13],
    )


ROT_HALF = ROT // 2


def nn(left, right):
    return lax.dot_general(left, right, (((1,), (0,)), ((), ())), preferred_element_type=f32)


def nt(left, right):
    return lax.dot_general(left, right, (((1,), (1,)), ((), ())), preferred_element_type=f32)


def tn(left, right):
    return lax.dot_general(left, right, (((0,), (0,)), ((), ())), preferred_element_type=f32)


def tt(left, right):
    return lax.dot_general(left, right, (((0,), (1,)), ((), ())), preferred_element_type=f32)


def standardize(values):
    centred = values - jnp.mean(values, axis=-1, keepdims=True)
    variance = jnp.mean(centred * centred, axis=-1, keepdims=True)
    spread = lax.rsqrt(variance + epsilon)
    return centred * spread, spread


def turn(columns, cos, sin):
    a, b = columns[0:ROT_HALF], columns[ROT_HALF:ROT]
    return jnp.concatenate([a * cos - b * sin, b * cos + a * sin, columns[ROT:]], axis=0)


def turn_back(columns, cos, sin):
    a, b = columns[0:ROT_HALF], columns[ROT_HALF:ROT]
    return jnp.concatenate([a * cos + b * sin, b * cos - a * sin, columns[ROT:]], axis=0)


def params(megabytes, **rest):
    return pltpu.CompilerParams(vmem_limit_bytes=megabytes * 2**20, **rest)


def cost(flops, moved):
    return pl.CostEstimate(flops=int(flops), bytes_accessed=int(moved), transcendentals=0)


def whole(*shape):
    return pl.BlockSpec(shape, lambda *_: (0,) * len(shape))


AG, AS, DG, DS, QB, OB, DB, KB, UB = range(9)


def vector(pack, at):
    return pack[at : at + 1, :]


def alive(ids):
    count = jnp.sum((ids >= 0).astype(f32), axis=1, keepdims=True)
    return lax.broadcasted_iota(jnp.int32, (ids.shape[1], 1), 0).astype(f32) < count


def norm_kernel(
    x_ref, cot_ref, seg_ref, pack, kw_ref, cos_ref, sin_ref,
    normed_ref, dense_ref, bg_ref, kv_ref, kvo_ref,
):
    count, _, kvw = kv_ref.shape
    blk = kvo_ref.shape[1]
    cos, sin = cos_ref[...], sin_ref[...]
    for n in range(count):
        rows = slice(n * blk, (n + 1) * blk)
        ids = seg_ref[pl.ds(pl.program_id(0) * count + n, 1), :]
        bg_ref[rows] = jnp.where(alive(ids), cot_ref[rows].astype(f32), 0.0).astype(bf16)
        unit, _ = standardize(x_ref[rows].astype(f32))
        normed = (unit * vector(pack, AG) + vector(pack, AS)).astype(bf16)
        normed_ref[rows] = normed
        dense_ref[rows] = (unit * vector(pack, DG) + vector(pack, DS)).astype(bf16)
        keyval = nn(normed, kw_ref[...]) + vector(pack, KB)[:, :kvw]
        keyval = turn(keyval.T, cos, sin).T.astype(bf16)
        kvo_ref[n] = keyval
        kv_ref[n, 0:blk, :] = keyval
        ids = [ids[:, at : at + 128].astype(f32) for at in range(0, blk, 128)]
        kv_ref[n, blk:, :] = jnp.concatenate(
            ids + [jnp.zeros((16 - len(ids), 128), f32)], axis=0
        ).astype(bf16)


def norms(x, cot, seg, pack, kw, cos, sin, count=2):
    tok, width = x.shape
    rows, blk = seg.shape
    kvw = kw.shape[1]
    tile = pl.BlockSpec((count * blk, width), lambda r: (r, 0))
    pair = lambda high: pl.BlockSpec((count, high, kvw), lambda r: (r, 0, 0))
    flat = jax.ShapeDtypeStruct((tok, width), bf16)
    return pl.pallas_call(
        norm_kernel,
        grid=(rows // count,),
        in_specs=[
            tile, tile, whole(rows, blk), whole(*pack.shape), whole(width, kvw),
            whole(ROT_HALF, blk), whole(ROT_HALF, blk),
        ],
        out_specs=[tile, tile, tile, pair(blk + 16), pair(blk)],
        out_shape=[
            flat, flat, flat,
            jax.ShapeDtypeStruct((rows, blk + 16, kvw), bf16),
            jax.ShapeDtypeStruct((rows, blk, kvw), bf16),
        ],
        compiler_params=params(60),
        cost_estimate=cost(2 * tok * width * kvw, 10 * tok * width),
        name="norms",
    )(x, cot, seg, pack, kw, cos, sin)


def gelu_parts(hidden):
    size = jnp.abs(hidden)
    t = pltpu.reciprocal(1.0 + (0.3275911 * 0.5**0.5) * size, approx=True)
    bell = jnp.exp2(hidden * hidden * (-0.5 * LOG2E))
    tail = t * (0.127414796 + t * (-0.142248368 + t * (0.7107068705 + t * (-0.7265760135 + t * 0.5307027145))))
    tail = tail * bell
    share = jnp.where(hidden >= 0.0, 1.0 - tail, tail)
    return share, bell * 0.3989422804014327


def towards(axis, target):
    return dict(device_id={axis: target}, device_id_type=pl.DeviceIdType.MESH)


def send(src, dst, sems, at, axis, target):
    return pltpu.make_async_remote_copy(
        src_ref=src, dst_ref=dst, send_sem=sems.at[0, at], recv_sem=sems.at[1, at],
        **towards(axis, target),
    )


def greet(planes):
    seq, batch = lax.axis_index("seq"), lax.axis_index("batch")
    barrier = pltpu.get_barrier_semaphore()
    column = [lax.rem(seq + 2 * hop, 2 * planes) for hop in range(1, planes)]
    for other in column + [seq + 1 - 2 * lax.rem(seq, 2)]:
        pl.semaphore_signal(barrier, inc=1, **towards("seq", other))
    for other in (batch + 1 - 2 * lax.rem(batch, 2), lax.rem(batch + 2, 4)):
        pl.semaphore_signal(barrier, inc=1, **towards("batch", other))
    pl.semaphore_wait(barrier, planes + 2)


def dense_kernel(
    di_ref, bg_ref, up_ref, down_ref, normed_ref, pack, qw_ref, ow_ref, cos_ref, sin_ref,
    kv_ref, act_ref, gh_ref, red_ref, gub_ref, q_ref, do_ref, kvs_ref,
    hid0, hid1, gac0, gac1, act0, act1, gh0, gh1, acc_up, acc_dn, acc_ub,
    cut_up, cut_dn, core_up, core_dn, half_up, half_dn, x_up, x_dn,
    own_sem, z_sem, y_sem, core_sem, x_sem,
    *, pairs, steps, tile, parts, owners,
):
    i = pl.program_id(0)
    planes = owners // 2
    seq, batch = lax.axis_index("seq"), lax.axis_index("batch")
    plane, side = seq // 2, lax.rem(seq, 2)
    x_at, core_at = batch // 2, lax.rem(batch, 2)
    x_other, core_other = lax.rem(batch + 2, 4), batch + 1 - 2 * core_at
    y_other = seq + 1 - 2 * side

    def own_copy():
        return pltpu.make_async_copy(kv_ref, kvs_ref.at[seq], own_sem)

    def hop_copy(hop):
        block = kv_ref if hop == 0 else kvs_ref.at[seq - 2 * hop]
        return send(block, kvs_ref.at[seq - 2 * hop], z_sem, hop, "seq", seq + 2)

    def across_copy(hop):
        block = kv_ref if hop == 0 else kvs_ref.at[seq - 2 * hop]
        return send(block, kvs_ref.at[seq - 2 * hop], y_sem, hop, "seq", y_other)

    def spread(hop):
        @pl.when(plane >= hop)
        def _():
            if hop > 0:
                arrived(hop)
            across_copy(hop).start()

            @pl.when(plane < planes - 1)
            def _():
                hop_copy(hop).start()

    def arrived(hop):
        block = kvs_ref.at[seq - 2 * hop]
        send(block, block, z_sem, hop - 1, "seq", y_other).wait_recv()

    def settle(hop):
        @pl.when(plane >= hop)
        def _():
            across_copy(hop).wait_send()
            block = kvs_ref.at[y_other - 2 * hop]
            send(block, block, y_sem, hop, "seq", y_other).wait_recv()

            @pl.when(plane < planes - 1)
            def _():
                hop_copy(hop).wait_send()

    def core_copies(c):
        return [
            send(cut_up.at[1 - core_at], core_up.at[c], core_sem, 2 * c, "batch", core_other),
            send(cut_dn.at[1 - core_at], core_dn.at[c], core_sem, 2 * c + 1, "batch", core_other),
        ]

    def x_copies(c):
        return [
            send(half_up.at[c % 2, 1 - x_at], x_up.at[c], x_sem, 2 * c, "batch", x_other),
            send(half_dn.at[c % 2, 1 - x_at], x_dn.at[c], x_sem, 2 * c + 1, "batch", x_other),
        ]

    def plus(first, second):
        return (first.astype(f32) + second.astype(f32)).astype(bf16)

    def cut(c):
        rows, cols = cut_up.shape[3], cut_up.shape[4]
        for core in range(2):
            for x in range(2):
                for o in range(owners):
                    at = (2 * o + core) * rows
                    cut_up[core, x, o] = acc_up[at : at + rows, x * cols : (x + 1) * cols].astype(bf16)
                tall = cut_dn.shape[3]
                for o in range(cut_dn.shape[2]):
                    at = (2 * o + core) * tall
                    cut_dn[core, x, o] = acc_dn[at : at + tall, x * cols : (x + 1) * cols].astype(bf16)
        for copy in core_copies(c):
            copy.start()

    def halve(c):
        for copy in core_copies(c):
            copy.wait()
        for x in range(2):
            half_up[c % 2, x] = plus(cut_up[core_at, x], core_up[c, x])
            half_dn[c % 2, x] = plus(cut_dn[core_at, x], core_dn[c, x])
        for copy in x_copies(c):
            copy.start()

    def fold(c):
        for copy in x_copies(c):
            copy.wait()
        rows = cut_up.shape[3]
        few = cut_dn.shape[2]
        red_ref[:, c * rows : (c + 1) * rows, :] = plus(half_up[c % 2, x_at], x_up[c])
        red_ref[c * few : (c + 1) * few, parts * rows :, :] = plus(half_dn[c % 2, x_at], x_dn[c])

    def rows_of(step, odd):
        return pl.ds(pl.multiple_of((lax.rem(step, pairs) * 2 + odd) * tile, tile), tile)

    def enter(odd, hid, gac):
        rows = rows_of(i, odd)
        hid[...] = nn(di_ref[rows, :], up_ref[...]) + pack[pl.ds(UB + i // pairs, 1), :]
        gac[...] = nt(bg_ref[rows, :], down_ref[...])

    def bend(odd, hid, gac, act_s, gh_s):
        hidden = hid[...]
        share, bell = gelu_parts(hidden)
        act = (hidden * share).astype(bf16)
        grad = (gac[...] * (share + hidden * bell)).astype(bf16)
        act_s[...] = act
        gh_s[...] = grad
        at = (1 - odd) * tile
        act_ref[at : at + tile, :] = act
        gh_ref[at : at + tile, :] = grad

    def gather(odd, act_s, gh_s, fresh=False):
        rows = rows_of(i - 1, odd)
        grad = gh_s[...]
        up, dn = tn(di_ref[rows, :], grad), tn(act_s[...], bg_ref[rows, :])
        ub = jnp.sum(grad.astype(f32), axis=0, keepdims=True)
        if fresh:
            acc_up[...], acc_dn[...], acc_ub[...] = up, dn, ub
        else:
            acc_up[...] += up
            acc_dn[...] += dn
            acc_ub[...] += ub

    def heads(step):
        count, _, wide = q_ref.shape
        blk = wide // HEADS
        cos, sin = cos_ref[...], sin_ref[...]
        for n in range(count):
            rows = pl.ds(pl.multiple_of((step * count + n) * blk, blk), blk)
            queries = (nn(normed_ref[n * blk : (n + 1) * blk, :], qw_ref[...]) + vector(pack, QB)).T
            upstream = nt(ow_ref[...], bg_ref[rows, :])
            for h in range(HEADS):
                part = slice(h * HEAD_DIM, (h + 1) * HEAD_DIM)
                lanes = slice(h * blk, (h + 1) * blk)
                q_ref[n, :, lanes] = (turn(queries[part], cos, sin) * HEAD_DIM**-0.5).astype(bf16)
                do_ref[n, :, lanes] = upstream[part].astype(bf16)

    @pl.when(i == 0)
    def _():
        greet(planes)
        own_copy().start()

    @pl.when(i == 0)
    def _():
        enter(0, hid0, gac0)
        enter(1, hid1, gac1)
        bend(0, hid0, gac0, act0, gh0)

    def body(fresh):
        enter(0, hid0, gac0)
        bend(1, hid1, gac1, act1, gh1)
        gather(0, act0, gh0, fresh)
        enter(1, hid1, gac1)
        bend(0, hid0, gac0, act0, gh0)
        gather(1, act1, gh1)

    @pl.when((i > 0) & (i < steps) & (lax.rem(i - 1, pairs) == 0))
    def _():
        body(True)

    @pl.when((i > 0) & (i < steps) & (lax.rem(i - 1, pairs) > 0))
    def _():
        body(False)

    @pl.when(i == steps)
    def _():
        bend(1, hid1, gac1, act1, gh1)
        gather(0, act0, gh0)
        gather(1, act1, gh1)

    for c in range(parts):
        @pl.when(i == (c + 1) * pairs)
        def _():
            gub_ref[c] = acc_ub[...]
            cut(c)
            if c > 1:
                fold(c - 2)

        if c < parts - 1:
            @pl.when(i == (c + 1) * pairs + 1)
            def _():
                halve(c)

    for hop in range(planes):
        @pl.when(i == hop * pairs)
        def _():
            spread(hop)

    @pl.when(i > steps)
    def _():
        heads(i - steps - 1)

    @pl.when(i == steps + 1)
    def _():
        halve(parts - 1)
        fold(parts - 2)

    @pl.when(i == pl.num_programs(0) - 1)
    def _():
        own_copy().wait()
        for hop in range(planes):
            settle(hop)
        fold(parts - 1)


def dense(di, bg, up, down, normed, pack, qw, ow, cos, sin, kv, parts, owners, tile=512):
    tok, width = di.shape
    ff = up.shape[1]
    chunk = ff // parts
    pairs = tok // tile // 2
    steps = pairs * parts
    high, low, cols = width // owners // 2, chunk // (owners // parts) // 2, chunk // 2
    few = owners // parts
    rows, blk = kv.shape[0], cos.shape[1]
    group = tile // blk
    late = lambda i: jnp.clip(i - steps - 1, 0, rows // group - 1)
    at = lambda i: jnp.clip(i, 0, steps - 1)
    anywhere = pl.BlockSpec(memory_space=pl.ANY)
    once = lambda *shape: pl.BlockSpec(
        shape, lambda *_: (0,) * len(shape), pipeline_mode=pl.Buffered(1)
    )
    dma = pltpu.SemaphoreType.DMA
    return pl.pallas_call(
        partial(
            dense_kernel, pairs=pairs, steps=steps, tile=tile, parts=parts, owners=owners
        ),
        grid=(steps + 1 + rows // group,),
        in_specs=[
            once(tok, width),
            once(tok, width),
            pl.BlockSpec((width, chunk), lambda i: (0, at(i) // pairs)),
            pl.BlockSpec((chunk, width), lambda i: (at(i) // pairs, 0)),
            pl.BlockSpec((tile, width), lambda i: (late(i), 0)),
            once(*pack.shape), once(width, width), once(width, width),
            once(ROT_HALF, blk), once(ROT_HALF, blk),
            anywhere,
        ],
        out_specs=[
            pl.BlockSpec((2 * tile, chunk), lambda i: (jnp.minimum(i, steps), 0)),
            pl.BlockSpec((2 * tile, chunk), lambda i: (jnp.minimum(i, steps), 0)),
            once(owners, parts * high + low, cols),
            once(parts, 1, chunk),
            pl.BlockSpec((group, HEAD_DIM, HEADS * blk), lambda i: (late(i), 0, 0)),
            pl.BlockSpec((group, HEAD_DIM, HEADS * blk), lambda i: (late(i), 0, 0)),
            anywhere,
        ],
        out_shape=[
            jax.ShapeDtypeStruct((2 * tile * (steps + 1), chunk), bf16),
            jax.ShapeDtypeStruct((2 * tile * (steps + 1), chunk), bf16),
            jax.ShapeDtypeStruct((owners, parts * high + low, cols), bf16),
            jax.ShapeDtypeStruct((parts, 1, chunk), f32),
            jax.ShapeDtypeStruct((rows, HEAD_DIM, HEADS * blk), bf16),
            jax.ShapeDtypeStruct((rows, HEAD_DIM, HEADS * blk), bf16),
            jax.ShapeDtypeStruct((owners,) + kv.shape, bf16),
        ],
        scratch_shapes=[pltpu.VMEM((tile, chunk), f32)] * 4
        + [pltpu.VMEM((tile, chunk), bf16)] * 4
        + [
            pltpu.VMEM((width, chunk), f32), pltpu.VMEM((chunk, width), f32),
            pltpu.VMEM((1, chunk), f32),
            pltpu.VMEM((2, 2, owners, high, cols), bf16), pltpu.VMEM((2, 2, few, low, cols), bf16),
            pltpu.VMEM((parts, 2, owners, high, cols), bf16),
            pltpu.VMEM((parts, 2, few, low, cols), bf16),
            pltpu.VMEM((2, 2, owners, high, cols), bf16), pltpu.VMEM((2, 2, few, low, cols), bf16),
            pltpu.VMEM((parts, owners, high, cols), bf16),
            pltpu.VMEM((parts, few, low, cols), bf16),
            dma, dma((2, owners // 2)), dma((2, owners // 2)), dma((2, 2 * parts)),
            dma((2, 2 * parts)),
        ],
        compiler_params=params(63, collective_id=0, has_side_effects=True),
        cost_estimate=cost(8 * tok * width * ff, 8 * tok * width + 4 * tok * ff),
        name="dense",
    )(di, bg, up, down, normed, pack, qw, ow, cos, sin, kv)


DESCEND, PROJECT, CLOSE = (0, 1, 6, 7), (2, 3, 4, 5), (8, 9, 12, 15)
FINISH, BACK = (10, 11, 13, 14), (16, 17, 18, 19)


def stair(*groups):
    jumps = sorted((step, n) for group in groups for n, step in enumerate(group))

    def of(i):
        value = jumps[0][1]
        for (_, before), (step, after) in zip(jumps, jumps[1:]):
            if after != before:
                value = value + jnp.where(i >= step, after - before, 0)
        return value

    return of


def tail_kernel(
    x_ref, cot_ref, seg_ref, att_ref, gq_ref, bg_ref, normed_ref, kcot_ref, first_ref,
    first_across_ref, second_ref, second_across_ref, gub_ref,
    mlp_ref, ow_hbm, down_hbm, up_hbm, qw_hbm, pack, kw_ref, cos_ref, sin_ref, *refs, rows, parts, owners,
):
    acts, ghs, refs = refs[:parts], refs[parts : 2 * parts], refs[2 * parts :]
    (
        out_ref, gt_ref, gow_ref, gqw_ref, guw_ref, gdw_ref, keyval_ref, vector_ref,
        ow_ref, down_ref, up_ref, qw_ref, acc, gd_s, gk_s, vec_s,
        own, across, below, total, stage, mlp_in,
        cut, core_in, x_in, piece, piece_in, part_in,
        small_k, small_v, seq_k, seq_v, mid_k, mid_v, batch_k, batch_v,
        load_sem, stage_sem, own_sem, first_sem, y_sem, z_sem, mlp_sem, core_sem, x_sem, piece_sem, part_sem,
        sk_sem, sv_sem, bk_sem, bv_sem,
    ) = refs
    i = pl.program_id(0)
    planes = owners // 2
    some = rows // 2
    seq, batch = lax.axis_index("seq"), lax.axis_index("batch")
    plane, side = seq // 2, lax.rem(seq, 2)
    x_at, core_at = batch // 2, lax.rem(batch, 2)
    x_other, core_other = lax.rem(batch + 2, 4), batch + 1 - 2 * core_at
    y_other = seq + 1 - 2 * side
    high, cols = cut.shape[3], cut.shape[4]
    seq_at = lambda hop: lax.rem(seq + hop, owners)
    batch_at = lambda hop: lax.rem(batch + hop, parts)

    def enter():
        barrier = pltpu.get_barrier_semaphore()
        for hop in range(1, owners):
            pl.semaphore_signal(barrier, inc=1, **towards("seq", seq_at(hop)))
        for hop in range(1, parts):
            pl.semaphore_signal(barrier, inc=1, **towards("batch", batch_at(hop)))
        pl.semaphore_wait(barrier, owners + parts - 2)

    pairs = ((up_hbm, up_ref), (ow_hbm, ow_ref), (down_hbm, down_ref), (qw_hbm, qw_ref))

    def load(n):
        return pltpu.make_async_copy(pairs[n][0], pairs[n][1], load_sem.at[n])

    def rows_of(part):
        return pl.ds(part * some, some)

    def own_copy(k, part):
        source = second_ref.at[k] if part else first_ref.at[k]
        return pltpu.make_async_copy(source, own.at[k, rows_of(part)], own_sem.at[2 * k + part])

    def first_copy(k):
        return pltpu.make_async_copy(first_across_ref.at[k], across.at[k, rows_of(0)], first_sem.at[k])

    def across_copy(k):
        return send(second_across_ref.at[k], across.at[k, rows_of(1)], y_sem, k, "seq", y_other)

    def below_copy(k, part):
        return send(
            own.at[k, rows_of(part)], below.at[k, rows_of(part)], z_sem, 2 * k + part, "seq",
            lax.rem(seq + owners - 2, owners),
        )

    def start_local(k):
        @pl.when(plane >= k)
        def _():
            own_copy(k, 0).start()
            first_copy(k).start()
            own_copy(k, 1).start()

    def start_across(k):
        @pl.when(plane >= k)
        def _():
            across_copy(k).start()

    def tick(step, part):
        k = step - (planes - 1 - plane)
        rows_at = slice(part * some, (part + 1) * some)

        @pl.when(k >= 0)
        def _():
            own_copy(k, part).wait()
            if part:
                across_copy(k).wait_recv()
            else:
                first_copy(k).wait()
            total[rows_at] = own[k, rows_at].astype(f32) + across[k, rows_at].astype(f32)

            @pl.when(plane < planes - 1)
            def _():
                below_copy(k, part).wait_recv()
                total[rows_at] += below[k, rows_at].astype(f32)

            if step < planes - 1:
                own[k, rows_at] = total[rows_at].astype(bf16)
                below_copy(k, part).start()

    def settle():
        for k in range(planes):
            @pl.when(plane >= k)
            def _():
                across_copy(k).wait_send()

            for part in range(2):
                @pl.when(plane > k)
                def _():
                    below_copy(k, part).wait_send()

    def mlp_copy(hop):
        return send(mlp_ref, mlp_in.at[batch], mlp_sem, hop - 1, "batch", batch_at(hop))

    def write_out(fills):
        copies = []
        for n, (fill, out) in enumerate(fills):
            if n >= 2:
                copies[n - 2].wait()
            fill(stage.at[n % 2])
            copies.append(pltpu.make_async_copy(stage.at[n % 2], out, stage_sem.at[n % 2]))
            copies[n].start()
        for copy in copies[-2:]:
            copy.wait()

    def collect_mlp():
        for hop in range(1, parts):
            mlp_copy(hop).wait()
        tall = mlp_ref.shape[0] - parts * high
        few = tall // (2 * high)

        def fill_up(c):
            def fill(ref):
                for b in range(parts):
                    core, x = b % 2, b // 2
                    ref[core * high : (core + 1) * high, x * cols : (x + 1) * cols] = mlp_in[
                        b, c * high : (c + 1) * high, :
                    ].astype(f32)

            return fill

        def fill_down(core, n):
            def fill(ref):
                at = parts * high + n * 2 * high
                for x in range(2):
                    ref[:, x * cols : (x + 1) * cols] = mlp_in[
                        2 * x + core, at : at + 2 * high, :
                    ].astype(f32)

            return fill

        fills = [
            (fill_up(c), guw_ref.at[:, pl.ds(c * 2 * cols, 2 * cols)]) for c in range(parts)
        ]
        for core in range(2):
            for n in range(few):
                at = core * tall + n * 2 * high
                fills.append((fill_down(core, n), gdw_ref.at[pl.ds(at, 2 * high), :]))
        write_out(fills)

    def core_copy():
        return send(cut, core_in, core_sem, 0, "batch", core_other)

    def x_copy():
        return send(cut.at[1 - x_at], x_in, x_sem, 0, "batch", x_other)

    def piece_copy(hop):
        target = seq_at(hop)
        return send(piece.at[target], piece_in.at[hop - 1], piece_sem, hop - 1, "seq", target)

    def part_copy(hop):
        return send(part_in.at[batch], part_in.at[batch], part_sem, hop - 1, "batch", batch_at(hop))

    def share_of(core, m, x, o):
        rows_at = pl.ds(pl.multiple_of((2 * o + core) * high, high), high)
        return acc[m, rows_at, x * cols : (x + 1) * cols]

    def cut_square():
        for m in range(2):
            for x in range(2):
                for o in range(owners):
                    cut[x, o, m] = share_of(1 - core_at, m, x, o).astype(bf16)
        core_copy().start()

    def halve_square():
        core_copy().wait()
        for m in range(2):
            for x in range(2):
                for o in range(owners):
                    value = share_of(core_at, m, x, o) + core_in[x, o, m].astype(f32)
                    cut[x, o, m] = value.astype(bf16)
        x_copy().start()

    def spread_square():
        x_copy().wait()
        piece[...] = (cut[x_at].astype(f32) + x_in[...].astype(f32)).astype(bf16)
        for hop in range(1, owners):
            piece_copy(hop).start()

    def sum_square():
        value = piece[seq].astype(f32)
        for hop in range(1, owners):
            piece_copy(hop).wait()
            value = value + piece_in[hop - 1].astype(f32)
        part_in[batch] = value.astype(bf16)
        for hop in range(1, parts):
            part_copy(hop).start()

    def collect_square():
        for hop in range(1, parts):
            part_copy(hop).wait()

        def fill_square(m):
            def fill(ref):
                for b in range(parts):
                    core, x = b % 2, b // 2
                    ref[core * high : (core + 1) * high, x * cols : (x + 1) * cols] = part_in[
                        b, m
                    ].astype(f32)

            return fill

        write_out([(fill_square(0), gow_ref), (fill_square(1), gqw_ref)])

    def seq_copies(hop):
        target = seq_at(hop)
        return [
            send(small_k.at[target], seq_k.at[hop - 1], sk_sem, hop - 1, "seq", target),
            send(small_v.at[target], seq_v.at[hop - 1], sv_sem, hop - 1, "seq", target),
        ]

    def batch_copies(hop):
        target = batch_at(hop)
        return [
            send(mid_k, batch_k.at[hop - 1], bk_sem, hop - 1, "batch", target),
            send(mid_v, batch_v.at[hop - 1], bv_sem, hop - 1, "batch", target),
        ]

    def start_small():
        tall = small_k.shape[1]
        keyval = gk_s[...].T
        for o in range(owners):
            small_k[o] = keyval[o * tall : (o + 1) * tall].astype(bf16)
        vectors = vec_s[0:8, :].astype(bf16)
        lane = lax.broadcasted_iota(jnp.int32, (vectors.shape[1], 128), 0)
        column = lax.broadcasted_iota(jnp.int32, (vectors.shape[1], 128), 1)
        for o in range(owners):
            share = nn(vectors, (lane == column + o * tall).astype(bf16))
            long = vec_s[8 + o // 2 : 9 + o // 2, :]
            left = (o % 2) * 4 * tall
            pieces = [long[:, left + n : left + n + 128] for n in range(0, 4 * tall, 128)]
            rows_of_owner = [share, *pieces, vec_s[6:7, 0:128], jnp.zeros((7 - len(pieces), 128), f32)]
            small_v[o] = jnp.concatenate(rows_of_owner, axis=0).astype(bf16)
        for hop in range(1, owners):
            for copy in seq_copies(hop):
                copy.start()

    def turn_small():
        value, vector = small_k[seq].astype(f32), small_v[seq].astype(f32)
        for hop in range(1, owners):
            for copy in seq_copies(hop):
                copy.wait()
            value = value + seq_k[hop - 1].astype(f32)
            vector = vector + seq_v[hop - 1].astype(f32)
        mid_k[...] = value.astype(bf16)
        mid_v[...] = vector.astype(bf16)
        for hop in range(1, parts):
            for copy in batch_copies(hop):
                copy.start()

    def end_small():
        value, vector = mid_k[...].astype(f32), mid_v[...].astype(f32)
        for hop in range(1, parts):
            for copy in batch_copies(hop):
                copy.wait()
            value = value + batch_k[hop - 1].astype(f32)
            vector = vector + batch_v[hop - 1].astype(f32)
        keyval_ref[...] = value
        vector_ref[...] = vector

    count, blk = kcot_ref.shape[0], kcot_ref.shape[1]
    side_by_side = lambda ref: jnp.concatenate([ref[n] for n in range(count)], axis=1)
    ones = jnp.ones((8, count * blk), bf16)

    def project():
        branch, grad = bg_ref[...], side_by_side(gq_ref)
        acc[0] += nn(side_by_side(att_ref), branch)
        acc[1] += tt(normed_ref[...], grad)
        vec_s[0:1] += nt(ones, grad)[0:1]
        vec_s[1:2] += nn(ones, branch)[0:1]

    def close(step):
        act = jnp.concatenate([ref[...] for ref in acts], axis=1)
        branch = tn(side_by_side(att_ref), ow_ref[...]) + vector(pack, OB)
        branch = branch + (nn(act, down_ref[...]) + vector(pack, DB))
        for n in range(count):
            rows_at = slice(n * blk, (n + 1) * blk)
            ids = seg_ref[pl.ds(step * count + n, 1), :]
            part = jnp.where(alive(ids), branch[rows_at], 0.0)
            out_ref[rows_at] = (x_ref[rows_at].astype(f32) + part).astype(bf16)

    def descend(step):
        grad = jnp.concatenate([ref[...] for ref in ghs], axis=1)
        second = nt(grad, up_ref[...])
        unit, _ = standardize(x_ref[...].astype(f32))
        vec_s[4:5] += jnp.sum(second * unit, axis=0, keepdims=True)
        vec_s[5:6] += jnp.sum(second, axis=0, keepdims=True)
        gd_s[step] = second * vector(pack, DG)

    def finish(step):
        unit, _ = standardize(x_ref[...].astype(f32))
        normed = (unit * vector(pack, AG) + vector(pack, AS)).astype(bf16)
        keyval = []
        for n in range(count):
            value = (total[step * count + n] + kcot_ref[n].astype(f32)).T
            keyval.append(turn_back(value, cos_ref[...], sin_ref[...]).astype(bf16))
        keyval = jnp.concatenate(keyval, axis=1)
        gk_s[...] += nn(keyval, normed)
        vec_s[6:7, 0 : keyval.shape[0]] += nt(ones, keyval)[0:1]
        first = tt(side_by_side(gq_ref), qw_ref[...]) + tt(keyval, kw_ref[...])
        vec_s[2:3] += jnp.sum(first * unit, axis=0, keepdims=True)
        vec_s[3:4] += jnp.sum(first, axis=0, keepdims=True)
        gd_s[step] += first * vector(pack, AG)

    def back(step):
        unit, spread = standardize(x_ref[...].astype(f32))
        both = gd_s[step]
        middle = jnp.mean(both, axis=-1, keepdims=True)
        along = jnp.mean(both * unit, axis=-1, keepdims=True)
        gt_ref[...] = (cot_ref[...].astype(f32) + (both - middle - unit * along) * spread).astype(bf16)

    def at(step):
        return pl.when(i == step)

    def when(*steps):
        hit = i == steps[0]
        for step in steps[1:]:
            hit = hit | (i == step)
        return pl.when(hit)

    def ticks(*marks):
        for mark, step, part in marks:
            @at(mark)
            def _():
                tick(step, part)

    @at(0)
    def _():
        load(0).start()
        enter()
        start_across(0)
        for k in range(planes):
            start_local(k)
        for hop in range(1, parts):
            mlp_copy(hop).start()
        mlp_in[batch] = mlp_ref[...]
        acc[...] = jnp.zeros(acc.shape, f32)
        gk_s[...] = jnp.zeros(gk_s.shape, f32)
        vec_s[...] = jnp.zeros(vec_s.shape, f32)
        for c in range(parts):
            vec_s[8 + c : 9 + c] = gub_ref[c]
        load(0).wait()

    @at(2)
    def _():
        for n in range(1, len(pairs)):
            load(n).start()

    for mark, k in ((1, 1), (6, 2), (8, 3)):
        @at(mark)
        def _():
            start_across(k)

    ticks(
        (0, 0, 0), (2, 1, 0), (6, 0, 1), (7, 2, 0), (8, 1, 1), (9, 3, 0), (10, 2, 1), (13, 3, 1),
    )

    @at(7)
    def _():
        halve_square()

    @at(8)
    def _():
        for n in range(1, len(pairs)):
            load(n).wait()

    @at(11)
    def _():
        spread_square()

    @at(12)
    def _():
        collect_mlp()

    @at(15)
    def _():
        start_small()

    @at(16)
    def _():
        turn_small()
        sum_square()

    @when(*DESCEND)
    def _():
        descend(jnp.where(i < 2, i, i - 4))

    @when(*PROJECT)
    def _():
        project()

    @at(PROJECT[-1])
    def _():
        cut_square()

    @when(*CLOSE)
    def _():
        close(jnp.where(i < 10, i - 8, jnp.where(i < 14, 2, 3)))

    @when(*FINISH)
    def _():
        finish(jnp.where(i < 12, i - 10, i - 11))

    @when(*BACK)
    def _():
        back(i - BACK[0])

    @at(BACK[-1])
    def _():
        settle()
        end_small()
        collect_square()


def tail(
    x, cot, seg, att, gq, bg, normed, kcot, first, first_across, second, second_across, gub, mlp, ow,
    down, up, qw, pack, kw, cos, sin, act, gh, parts, owners, count=2,
):
    rows, width, blk = att.shape
    tok, ff, kvw = rows * blk, up.shape[1], kw.shape[1]
    tiles = tok // (count * blk)
    planes = owners // 2
    high, cols, tall = width // owners // 2, width // 2, width // owners
    once = lambda *shape: pl.BlockSpec(
        shape, lambda i: (0,) * len(shape), pipeline_mode=pl.Buffered(1)
    )
    anywhere = pl.BlockSpec(memory_space=pl.ANY)
    s = rows // count
    one, descent, third, last = stair(PROJECT), stair(DESCEND), stair(FINISH), stair(BACK)
    closing, every = stair(CLOSE), stair(DESCEND, CLOSE, FINISH, BACK)
    heads, queries = stair(PROJECT, CLOSE), stair(PROJECT, FINISH)
    flat = lambda of: pl.BlockSpec((count * blk, width), lambda i: (of(i), 0))
    single = pl.BlockSpec(
        (count * blk, width), lambda i: (last(i), 0), pipeline_mode=pl.Buffered(1)
    )
    stack = lambda of, h, w: pl.BlockSpec((count, h, w), lambda i: (of(i), 0, 0))
    wide = lambda of: [
        pl.BlockSpec((count * blk, ff // parts), lambda i, c=c: (c * tiles + of(i) + 1, 0))
        for c in range(parts)
    ]
    dma = pltpu.SemaphoreType.DMA
    vmem = lambda kind, *shape: pltpu.VMEM(shape, kind)
    return pl.pallas_call(
        partial(tail_kernel, rows=rows, parts=parts, owners=owners),
        grid=(BACK[-1] + 1,),
        in_specs=[
            flat(every), single, once(rows, blk), stack(heads, width, blk),
            stack(queries, width, blk), flat(one), flat(one), stack(third, blk, kvw), anywhere,
            anywhere, anywhere, anywhere, once(parts, 1, ff // parts), once(*mlp.shape), anywhere,
            anywhere, anywhere, anywhere, once(*pack.shape), once(width, kvw), once(ROT_HALF, blk),
            once(ROT_HALF, blk),
        ] + wide(closing) + wide(descent),
        out_specs=[
            flat(closing), single, anywhere, anywhere, anywhere, anywhere, once(tall, kvw),
            once(16, 128),
        ],
        out_shape=[
            jax.ShapeDtypeStruct((tok, width), bf16),
            jax.ShapeDtypeStruct((tok, width), bf16),
            jax.ShapeDtypeStruct((tall, width), f32),
            jax.ShapeDtypeStruct((tall, width), f32),
            jax.ShapeDtypeStruct((tall, ff), f32),
            jax.ShapeDtypeStruct((ff // owners, width), f32),
            jax.ShapeDtypeStruct((tall, kvw), f32),
            jax.ShapeDtypeStruct((16, 128), f32),
        ],
        scratch_shapes=[
            vmem(bf16, width, width), vmem(bf16, ff, width), vmem(bf16, width, ff),
            vmem(bf16, width, width),
            vmem(f32, 2, width, width), vmem(f32, s, count * blk, width),
            vmem(f32, kvw, width), vmem(f32, 16, width),
            vmem(bf16, planes, rows, blk, kvw), vmem(bf16, planes, rows, blk, kvw),
            vmem(bf16, planes - 1, rows, blk, kvw), vmem(f32, rows, blk, kvw),
            vmem(f32, 2, tall, width), vmem(bf16, parts, *mlp.shape),
            vmem(bf16, 2, owners, 2, high, cols), vmem(bf16, 2, owners, 2, high, cols),
            vmem(bf16, owners, 2, high, cols),
            vmem(bf16, owners, 2, high, cols), vmem(bf16, owners - 1, 2, high, cols),
            vmem(bf16, parts, 2, high, cols),
            vmem(bf16, owners, tall, kvw), vmem(bf16, owners, 16, 128),
            vmem(bf16, owners - 1, tall, kvw), vmem(bf16, owners - 1, 16, 128),
            vmem(bf16, tall, kvw), vmem(bf16, 16, 128),
            vmem(bf16, parts - 1, tall, kvw), vmem(bf16, parts - 1, 16, 128),
            dma((4,)), dma((2,)), dma((2 * planes,)), dma((planes,)), dma((2, planes)), dma((2, 2 * planes)),
            dma((2, parts - 1)), dma((2, 1)), dma((2, 1)),
            dma((2, owners - 1)), dma((2, parts - 1)), dma((2, owners - 1)), dma((2, owners - 1)),
            dma((2, parts - 1)), dma((2, parts - 1)),
        ],
        compiler_params=params(63, collective_id=1, has_side_effects=True),
        cost_estimate=cost(4 * tok * width * (2 * width + ff), 4 * tok * ff + 20 * tok * width),
        name="tail",
    )(
        x, cot, seg, att, gq, bg, normed, kcot, first, first_across, second, second_across, gub, mlp,
        ow, down, up, qw, pack, kw, cos, sin, *[act] * parts, *[gh] * parts,
    )


def deliver_kernel(*refs):
    half = len(refs) // 2
    for source, target in zip(refs[:half], refs[half:]):
        target[...] = source[...]


def deliver(*arrays, pieces=4):
    def split(array):
        high, wide = array.shape
        return pl.BlockSpec((high // pieces, wide), lambda i: (i, 0))

    return pl.pallas_call(
        deliver_kernel,
        grid=(pieces,),
        in_specs=[split(array) for array in arrays],
        out_specs=[split(array) for array in arrays],
        out_shape=[jax.ShapeDtypeStruct(array.shape, array.dtype) for array in arrays],
        compiler_params=params(60),
        cost_estimate=cost(0, 2e7),
        name="deliver",
    )(*arrays)


def attn_kernel(first_ref, sidx_ref, q_ref, do_ref, kv_ref, start_ref,
                cos_ref, sin_ref, *refs, blk, nblk, begin):
    att_ref, gq_ref, own_ref, other_ref, p_s, m_s, bias_s, o_s, mx, ls, dq_s, dc_s, ic_s, inn_s = refs[-14:]
    r = begin + pl.program_id(0)
    e = sidx_ref[0]
    n = e - first_ref[r] + 1
    start = start_ref[pl.ds(r, 1), :]
    qpos = e*blk + lax.broadcasted_iota(jnp.int32,(1,blk),1)
    krow = lax.broadcasted_iota(jnp.int32,(blk,blk),0)

    def hsl(h):
        return slice(h*blk,(h+1)*blk)

    def put(j, block):
        @pl.when(lax.rem(j + e, 2) == 0)
        def _():
            own_ref[j // 2, 0] = block

        @pl.when(lax.rem(j + e, 2) == 1)
        def _():
            other_ref[j // 2, 0] = block

    @pl.loop(0, nblk)
    def _(j):
        @pl.when((j < first_ref[r]) | (j > e))
        def _():
            put(j, jnp.zeros((blk,2*HEAD_DIM),bf16))

    def forward(jj):
        j = e - jj
        kvj = kv_ref[j, 0, 0:blk, :]
        key = kvj[:, :HEAD_DIM]
        vt = kvj.T[HEAD_DIM:,:]
        kpos = j*blk + krow
        bias_s[...] = jnp.where((kpos>=start)&(kpos<=qpos), 0.0, negative)
        sv = {}; pv = {}; av = {}
        for h in range(HEADS+3):
            if h < HEADS:
                sv[h] = nn(key, q_ref[0,:,hsl(h)])
            g = h-2
            if 0 <= g < HEADS:
                hs = hsl(g)
                s = sv.pop(g)*LOG2E + bias_s[...]
                top = jnp.max(s,axis=0,keepdims=True)
                mo = mx[:,hs]
                mn = jnp.maximum(mo, top)
                p = jnp.exp2(s-mn)
                av[g] = jnp.exp2(mo-mn)
                ls[:,hs] = ls[:,hs]*av[g] + jnp.sum(p,axis=0,keepdims=True)
                pv[g] = p.astype(bf16)
                p_s[jj,:,hs] = pv[g]
                m_s[jj,:,hs] = mn
                mx[:,hs] = mn
            g = h-3
            if 0 <= g < HEADS:
                hs = hsl(g)
                new = nn(vt,pv.pop(g))
                o_s[:,hs] = o_s[:,hs]*av.pop(g) + new

    half = blk//2

    def upper(h):
        return slice(h*blk+half,(h+1)*blk)

    def joined(get, pair):
        return jnp.concatenate([get(upper(2*pair)), get(upper(2*pair+1))],axis=1)

    def own_forward():
        kvj = kv_ref[e, 0, 0:blk, :]
        key = kvj[:, :HEAD_DIM]
        vt = kvj.T[HEAD_DIM:,:]
        bias_s[...] = jnp.where((e*blk+krow>=start)&(e*blk+krow<=qpos), 0.0, negative)
        low, high, pl_, ph = {}, {}, {}, {}
        pairs = HEADS//2
        for n in range(pairs+2):
            if n < pairs:
                for h in (2*n, 2*n+1):
                    low[h] = nn(key[:half], q_ref[0,:,hsl(h)])
                high[n] = nn(key[half:], joined(lambda at: q_ref[0,:,at], n))
            m = n-1
            if 0 <= m < pairs:
                two = high.pop(m)
                top_part = []
                for k in (0, 1):
                    h = 2*m+k
                    hs = hsl(h)
                    s = low.pop(h)*LOG2E + bias_s[0:half,:]
                    u = two[:,k*half:(k+1)*half]*LOG2E + bias_s[half:,half:]
                    top = jnp.max(s,axis=0,keepdims=True)
                    rest = jnp.maximum(top[:,half:], jnp.max(u,axis=0,keepdims=True))
                    mn = jnp.concatenate([top[:,:half], rest],axis=1)
                    p = jnp.exp2(s-mn)
                    v = jnp.exp2(u-rest)
                    total = jnp.sum(p,axis=0,keepdims=True)
                    more = total[:,half:] + jnp.sum(v,axis=0,keepdims=True)
                    ls[:,hs] = jnp.concatenate([total[:,:half], more],axis=1)
                    pl_[h] = p.astype(bf16)
                    p_s[0,0:half,hs] = pl_[h]
                    v = v.astype(bf16)
                    p_s[0,half:,upper(h)] = v
                    top_part.append(v)
                    m_s[0,:,hs] = mn
                    mx[:,hs] = mn
                ph[m] = jnp.concatenate(top_part,axis=1)
            m = n-2
            if 0 <= m < pairs:
                two = nn(vt[:,half:], ph.pop(m))
                for k in (0, 1):
                    h = 2*m+k
                    first = nn(vt[:,:half], pl_.pop(h))
                    o_s[:,hsl(h)] = jnp.concatenate(
                        [first[:,:half], first[:,half:]+two[:,k*half:(k+1)*half]],axis=1)

    own_forward()

    @pl.loop(1, n)
    def _(jj):
        forward(jj)

    for h in range(HEADS):
        hs = hsl(h)
        inv = 1.0/ls[:,hs]
        ls[:,hs] = inv
        o = o_s[:,hs]*inv
        att_ref[0, h*HEAD_DIM:(h+1)*HEAD_DIM, :] = o.astype(bf16)
        inn_s[:,hs] = jnp.sum(o*do_ref[0,:,hs].astype(f32),axis=0,keepdims=True)

    def backward(jj):
        j = e - jj
        kvj = kv_ref[j, 0, 0:blk, :]
        value = kvj[:, HEAD_DIM:]
        kt = kvj.T[:HEAD_DIM,:]
        for h in range(HEADS):
            hs = hsl(h)
            c = jnp.exp2(m_s[jj,:,hs]-mx[:,hs])*ls[:,hs]
            dc_s[:,hs] = (do_ref[0,:,hs].astype(f32)*c).astype(bf16)
            ic_s[:,hs] = inn_s[:,hs]*c
        dpv = {}; dsv = {}; pbv = {}
        dk = dv = None
        for h in range(HEADS+4):
            if h < HEADS:
                dpv[h] = nn(value, dc_s[:,hsl(h)])
            g = h-2
            if 0 <= g < HEADS:
                hs = hsl(g)
                pb = p_s[jj,:,hs]
                dsv[g] = (pb.astype(f32)*(dpv.pop(g)-ic_s[:,hs])).astype(bf16)
                new = nt(pb, dc_s[:,hs])
                dv = new if dv is None else dv + new
            g = h-4
            if 0 <= g < HEADS:
                hs = hsl(g)
                ds = dsv.pop(g)
                new = nn(kt, ds)
                dq_s[:,hs] = dq_s[:,hs] + new
                new = nt(ds, q_ref[0,:,hs])
                dk = new if dk is None else dk + new
        put(j, jnp.concatenate([dk,dv],axis=1).astype(bf16))

    def own_backward():
        kvj = kv_ref[e, 0, 0:blk, :]
        value = kvj[:, HEAD_DIM:]
        kt = kvj.T[:HEAD_DIM,:]
        for h in range(HEADS):
            hs = hsl(h)
            c = jnp.exp2(m_s[0,:,hs]-mx[:,hs])*ls[:,hs]
            dc_s[:,hs] = (do_ref[0,:,hs].astype(f32)*c).astype(bf16)
            ic_s[:,hs] = inn_s[:,hs]*c
        low, high, dl, dh = {}, {}, {}, {}
        dk = [None, None]
        dv = [None, None]

        def add(sums, at, new):
            sums[at] = new if sums[at] is None else sums[at] + new

        pairs = HEADS//2
        for n in range(pairs+2):
            if n < pairs:
                for h in (2*n, 2*n+1):
                    low[h] = nn(value[:half], dc_s[:,hsl(h)])
                high[n] = nn(value[half:], joined(lambda at: dc_s[:,at], n))
            m = n-1
            if 0 <= m < pairs:
                for h in (2*m, 2*m+1):
                    hs = hsl(h)
                    pb = p_s[0,0:half,hs]
                    dl[h] = (pb.astype(f32)*(low.pop(h)-ic_s[:,hs])).astype(bf16)
                    add(dv, 0, nt(pb, dc_s[:,hs]))
                pb = joined(lambda at: p_s[0,half:,at], m)
                dh[m] = (pb.astype(f32)*(high.pop(m)-joined(lambda at: ic_s[:,at], m))).astype(bf16)
                add(dv, 1, nt(pb, joined(lambda at: dc_s[:,at], m)))
            m = n-2
            if 0 <= m < pairs:
                ds = dh.pop(m)
                two = nn(kt[:,half:], ds)
                add(dk, 1, nt(ds, joined(lambda at: q_ref[0,:,at], m)))
                for k in (0, 1):
                    h = 2*m+k
                    ds = dl.pop(h)
                    first = nn(kt[:,:half], ds)
                    dq_s[:,hsl(h)] = jnp.concatenate(
                        [first[:,:half], first[:,half:]+two[:,k*half:(k+1)*half]],axis=1)
                    add(dk, 0, nt(ds, q_ref[0,:,hsl(h)]))
        put(e, jnp.concatenate(
            [jnp.concatenate(dk,axis=0), jnp.concatenate(dv,axis=0)],axis=1).astype(bf16))

    own_backward()

    @pl.loop(1, n)
    def _(jj):
        backward(jj)

    cos = cos_ref[...]; sin = sin_ref[...]
    for h in range(HEADS):
        g = dq_s[:, hsl(h)]*(HEAD_DIM**-0.5)
        a, b = g[0:8], g[8:16]
        gq_ref[0, h*HEAD_DIM:(h+1)*HEAD_DIM, :] = jnp.concatenate([a*cos+b*sin, b*cos-a*sin, g[16:]],axis=0).astype(bf16)


def attention(first, sidx, queries, upstream, kv, start, cos, sin, begin, count, before=()):
    rows, _, wide = queries.shape
    nblk, blk = kv.shape[0], wide // HEADS
    stack = lambda high, across: pl.BlockSpec((1, high, across), lambda r, *_: (begin + r, 0, 0))
    held = jax.ShapeDtypeStruct((rows, HEADS * HEAD_DIM, blk), bf16)
    specs = pltpu.PrefetchScalarGridSpec(
        num_scalar_prefetch=2,
        grid=(count,),
        in_specs=[
            stack(HEAD_DIM, wide), stack(HEAD_DIM, wide),
            pl.BlockSpec((nblk, 1, blk + 16, 2 * HEAD_DIM), lambda r, *_: (0, begin + r, 0, 0)),
            whole(rows, blk), whole(ROT_HALF, blk), whole(ROT_HALF, blk),
        ] + [pl.BlockSpec(memory_space=pl.ANY)] * len(before),
        out_specs=[
            stack(HEADS * HEAD_DIM, blk), stack(HEADS * HEAD_DIM, blk),
        ] + [pl.BlockSpec((nblk // 2, 1, blk, 2 * HEAD_DIM), lambda r, *_: (0, r, 0, 0))] * 2,
        scratch_shapes=[
            pltpu.VMEM((nblk, blk, wide), bf16), pltpu.VMEM((nblk, 1, wide), f32),
            pltpu.VMEM((blk, blk), f32), pltpu.VMEM((HEAD_DIM, wide), f32),
            pltpu.VMEM((1, wide), f32), pltpu.VMEM((1, wide), f32),
            pltpu.VMEM((HEAD_DIM, wide), f32), pltpu.VMEM((HEAD_DIM, wide), bf16),
            pltpu.VMEM((1, wide), f32), pltpu.VMEM((1, wide), f32),
        ],
    )
    return pl.pallas_call(
        partial(attn_kernel, blk=blk, nblk=nblk, begin=begin),
        out_shape=[held, held]
        + [jax.ShapeDtypeStruct((nblk // 2, count, blk, 2 * HEAD_DIM), bf16)] * 2,
        grid_spec=specs,
        input_output_aliases={8 + n: n for n in range(len(before))},
        compiler_params=params(60),
        cost_estimate=cost(6e9 * count, 5e6 * count),
        name="attention",
    )(first, sidx, queries, upstream, kv, start, cos, sin, *before)


def local(
    tokens,
    segment_ids,
    query_weight,
    query_bias,
    keyval_weight,
    keyval_bias,
    out_weight,
    out_bias,
    up_weight,
    up_bias,
    down_weight,
    down_bias,
    attention_gain,
    attention_shift,
    dense_gain,
    dense_shift,
    out_cotangent,
    keyval_cotangent,
):
    rows, blk, width = tokens.shape
    ff = up_weight.shape[1]
    kvw = 2 * HEAD_DIM
    tok = rows * blk
    owners, parts = lax.axis_size("seq"), lax.axis_size("batch")
    place = lax.axis_index("seq")
    cos, sin = rotary_tables(place * blk + jnp.arange(blk, dtype=jnp.int32))
    cos, sin = cos.T, sin.T
    x = tokens.reshape(tok, width)
    cot = out_cotangent.reshape(tok, width)
    lines = [
        attention_gain, attention_shift, dense_gain, dense_shift, query_bias, out_bias, down_bias,
        jnp.pad(keyval_bias, (0, width - kvw)),
    ] + [up_bias[at : at + width] for at in range(0, ff, width)]
    line = lax.broadcasted_iota(jnp.int32, (16, width), 0)
    pack = jnp.zeros((16, width), f32)
    for n, values in enumerate(lines):
        pack = jnp.where(line == n, values[None, :], pack)

    normed, dense_in, branch_grad, keyval, keyval_out = norms(
        x, cot, segment_ids, pack, keyval_weight, cos, sin
    )
    act, grad_hidden, mlp, gub, queries, grad_attended, keyval_all = dense(
        dense_in, branch_grad, up_weight, down_weight, normed, pack, query_weight, out_weight, cos,
        sin, keyval, parts, owners,
    )
    mlp = lax.psum_scatter(mlp, "seq", scatter_dimension=0)

    ids = keyval_all[:, :, blk : blk + blk // 128, :].reshape(owners, rows, blk).astype(f32)
    before = (jnp.arange(owners) <= place)[:, None, None]
    order = lambda values: jnp.where(values < 0, 1024.0, values)
    ids = jnp.where(before, order(ids), 2048.0)
    start = jnp.sum(
        (ids[:, :, None, :] < order(segment_ids.astype(f32))[None, :, :, None]).astype(jnp.int32),
        axis=(0, 3),
    ).astype(jnp.int32)
    first_block = start[:, 0] // blk
    index = place.astype(jnp.int32)[None]
    run = partial(
        attention, first_block, index, queries, grad_attended, keyval_all, start, cos, sin,
        count=rows // 2,
    )
    attended, grad_query, first, first_other = run(begin=0)
    across = lax.ppermute(first_other, "seq", [(i, i ^ 1) for i in range(owners)])
    attended, grad_query, own, other = run(begin=rows // 2, before=(attended, grad_query))
    (
        layer_out, grad_tokens, grad_out_weight, grad_query_weight, grad_up_weight,
        grad_down_weight, grad_keyval_weight, vectors,
    ) = tail(
        x, cot, segment_ids, attended, grad_query, branch_grad, normed, keyval_cotangent,
        first, across, own, other, gub, mlp, out_weight, down_weight, up_weight, query_weight,
        pack, keyval_weight, cos, sin, act, grad_hidden, parts, owners,
    )
    (
        layer_out, grad_tokens, grad_out_weight, grad_query_weight, grad_up_weight,
        grad_down_weight, grad_keyval_weight,
    ) = deliver(
        layer_out, grad_tokens, grad_out_weight, grad_query_weight, grad_up_weight,
        grad_down_weight, grad_keyval_weight,
    )
    share = width // owners
    query_bias_grad, branch_sum, ag, ash, dg, dsh = [vectors[n, :share] for n in range(6)]
    return (
        layer_out.reshape(rows, blk, width),
        keyval_out,
        grad_tokens.reshape(rows, blk, width),
        grad_query_weight,
        query_bias_grad,
        grad_keyval_weight,
        lax.dynamic_slice(vectors[11], (place * (kvw // owners),), (kvw // owners,)),
        grad_out_weight,
        branch_sum,
        grad_up_weight,
        vectors[8:11].reshape(ff // owners),
        grad_down_weight,
        branch_sum,
        ag,
        ash,
        dg,
        dsh,
    )


def choose(tokens, *rest):
    rows, blk, width = tokens.shape
    fits = blk == 256 and rows == 8 and rest[7].shape == (width, 4 * width) and width % 256 == 0
    fits = fits and lax.axis_size("batch") == 4 and lax.axis_size("seq") == 8
    return (local if fits else local_plain)(tokens, *rest)


def solution(mesh):
    placed = (
        P("batch", "seq", None),
        P("batch", "seq"),
        P(),
        P(),
        P(),
        P(),
        P(),
        P(),
        P(),
        P(),
        P(),
        P(),
        P(),
        P(),
        P(),
        P(),
        P("batch", "seq", None),
        P("batch", "seq", None),
    )
    return jax.shard_map(
        choose,
        mesh=mesh,
        in_specs=placed,
        out_specs=(
            P("batch", "seq", None),
            P("batch", "seq", None),
            P("batch", "seq", None),
            P("seq", None),
            P("seq"),
            P("seq", None),
            P("seq"),
            P("seq", None),
            P("seq"),
            P("seq", None),
            P("seq"),
            P("seq", None),
            P("seq"),
            P("seq"),
            P("seq"),
            P("seq"),
            P("seq"),
        ),
        check_vma=False,
    )
```
